32 devices in a mesh: fsdp: 2 (over core), ctx: 16 (over z, y, x).
Axes of the slice: x: 2, y: 2, z: 4, core: 2. Of those that a mesh axis runs over, the one named last changes fastest.
Arguments:
- token_ids: int32 [2, 2048], P('fsdp', 'ctx'), may hold values from 0 to 511
- embedding: bfloat16 [512, 4096], P(None, 'fsdp'), may hold values from -5 to 5
- conv_taps: float32 [3, 3, 4096], replicated, may hold values from -2.5 to 2.5
- residues: float32 [4096, 16], replicated, may hold values from -1.2 to 1.2
- decays: float32 [4096, 16], replicated, may hold values from 9.765625e-06 to 0.05
- filter_seed: int32 [4096, 16], replicated, may hold values from 0 to 4095
- skip_gain: float32 [4096], replicated, may hold values from 0.5 to 1.5
- cotangent: float32 [2, 4096, 2048], P('fsdp', None, 'ctx'), may hold values from -6 to 6
Outputs:
- mixer_out: float32 [2, 4096, 2048], P('fsdp', None, 'ctx')
- embed_grad: float32 [512, 4096], P(None, 'fsdp')
The draws below stay inside these ranges and needn't reach their ends.
All inputs are finite; a program needn't handle non-finite values.
Results may differ from the reference program's by a relative error of at most 0.0006.
Values may be sent and summed in bfloat16 or wider, within the bound.
No kernel may reach another device: no remote copies, remote signals or barrier semaphores. Data moves between devices by JAX's collectives and lax.ppermute only.
A program may use at most 320 MiB of HBM per device.

```python
import math
import jax
import jax.numpy as jnp

D = 4096
VOCAB = 512
MODES = 16
PERIOD = 4096
SEQ = 2048
BATCH = 2


def touch_ends(drawn, stream_key, least, high):
    longest = drawn.shape.index(max(drawn.shape))
    spots = []
    for shift in (0, 1):
        where = [jax.random.randint(jax.random.fold_in(stream_key, axis), (), 0, length) for axis, length in enumerate(drawn.shape)]
        where[longest] = (where[longest] + shift) % drawn.shape[longest]
        spots.append(tuple(where))
    return drawn.at[spots[0]].set(least).at[spots[1]].set(high)


def shard_levels(stream_key, dims, split, least, high):
    gain = 1.0
    for axis_at, shards_of in split:
        heights = jax.random.uniform(jax.random.fold_in(jax.random.fold_in(stream_key, 6), axis_at), (shards_of,), jnp.float32, least / len(split), high / len(split))
        gain = gain * jnp.repeat(jnp.exp(heights), dims[axis_at] // shards_of).reshape((-1,) + (1,) * (len(dims) - 1 - axis_at))
    return gain


def scatter_about(rng, dims, deviation, bound, pieces=(), kind=jnp.bfloat16):
    factor_of = shard_levels(rng, dims, pieces, -0.22, 0.18) if pieces else 1.0
    entries = jax.random.normal(rng, dims, jnp.float32) * deviation * factor_of
    return jnp.minimum(jnp.maximum(entries, -bound), bound).astype(kind)


def setup_inputs(seed: int = 0) -> dict:
    streams_of = jax.random.split(jax.random.key(seed), 9)
    token_ids = touch_ends(jax.random.randint(streams_of[0], (BATCH, SEQ), 0, VOCAB), jax.random.fold_in(streams_of[0], 1), 0, VOCAB - 1).astype(jnp.int32)
    embedding = scatter_about(streams_of[1], (VOCAB, D), 1.0, 5.0, ((1, 2),))
    conv_taps = scatter_about(streams_of[2], (3, 3, D), 0.6, 2.5, (), jnp.float32)
    residues = scatter_about(streams_of[3], (D, MODES), 0.3, 1.2, (), jnp.float32)
    decays = jnp.clip(jnp.exp(jax.random.uniform(streams_of[4], (D, MODES), jnp.float32, math.log(9.765624781721272e-06), math.log(0.05))), 9.765624781721272e-06, 0.05)
    filter_seed = touch_ends(jax.random.randint(streams_of[5], (D, MODES), 0, PERIOD), jax.random.fold_in(streams_of[5], 1), 0, PERIOD - 1).astype(jnp.int32)
    skip_gain = jnp.clip(jax.random.uniform(streams_of[6], (D,), jnp.float32, 0.5, 1.5), 0.5, 1.5)
    cotangent = scatter_about(streams_of[7], (BATCH, D, SEQ), 1.0, 6.0, ((0, 2), (2, 16)), jnp.float32)
    return {"token_ids": token_ids, "embedding": embedding, "conv_taps": conv_taps, "residues": residues, "decays": decays, "filter_seed": filter_seed, "skip_gain": skip_gain, "cotangent": cotangent}


TWO_PI = 2.0 * math.pi

def filter_kernel(residues, decays, filter_seed):
    positions = jnp.arange(SEQ, dtype=jnp.int32)
    time_float = positions.astype(jnp.float32)
    kernel = jnp.zeros((D, SEQ), jnp.float32)
    for mode_index in range(MODES):
        decay_rate = decays[:, mode_index][:, None]
        phase_int = filter_seed[:, mode_index][:, None] * positions[None, :] % PERIOD
        phase_angle = TWO_PI / PERIOD * phase_int.astype(jnp.float32)
        weight = residues[:, mode_index][:, None] * jnp.sqrt(decay_rate + 1.0 / SEQ)
        kernel = kernel + weight * jnp.exp(-decay_rate * time_float[None, :]) * jnp.cos(phase_angle)
    return kernel

def causal_mix(signal, tap_set):
    padded = jnp.pad(signal, ((0, 0), (2, 0)))
    return tap_set[0][:, None] * signal + tap_set[1][:, None] * padded[:, 1:SEQ + 1] + tap_set[2][:, None] * padded[:, :SEQ]

def reverse_mix(gradient, tap_set):
    padded = jnp.pad(gradient, ((0, 0), (0, 2)))
    return tap_set[0][:, None] * gradient + tap_set[1][:, None] * padded[:, 1:SEQ + 1] + tap_set[2][:, None] * padded[:, 2:SEQ + 2]

def reference(token_ids, embedding, conv_taps, residues, decays, filter_seed, skip_gain, cotangent):
    kernel = filter_kernel(residues, decays, filter_seed)
    length = 2 * SEQ
    spectrum = jnp.fft.rfft(kernel, n=length, axis=-1)
    skip_column = skip_gain[:, None]
    outputs = []
    grad_table = jnp.zeros((VOCAB, D), jnp.float32)
    for seq_index in range(BATCH):
        signal = jnp.take(embedding, token_ids[seq_index], axis=0).astype(jnp.float32).T
        query_stream = causal_mix(signal, conv_taps[0])
        key_stream = causal_mix(signal, conv_taps[1])
        value_stream = causal_mix(signal, conv_taps[2])
        mixed_in = key_stream * value_stream
        conv_full = jnp.fft.irfft(jnp.fft.rfft(mixed_in, n=length, axis=-1) * spectrum, n=length, axis=-1)[:, :SEQ]
        long_out = conv_full + skip_column * mixed_in
        outputs.append(query_stream * long_out)
        grad_long = cotangent[seq_index] * query_stream
        grad_query = cotangent[seq_index] * long_out
        correlated = jnp.fft.irfft(jnp.conj(spectrum) * jnp.fft.rfft(grad_long, n=length, axis=-1), n=length, axis=-1)[:, :SEQ]
        grad_mixed = correlated + skip_column * grad_long
        grad_signal = reverse_mix(grad_query, conv_taps[0]) + reverse_mix(grad_mixed * value_stream, conv_taps[1]) + reverse_mix(grad_mixed * key_stream, conv_taps[2])
        grad_table = grad_table + jax.ops.segment_sum(grad_signal.T, token_ids[seq_index], num_segments=VOCAB)
    return (jnp.stack(outputs), grad_table)
```

```python
import math

import jax
import jax.numpy as jnp
import ml_dtypes
import numpy as np
from jax import lax
from jax.experimental import pallas as pl
from jax.experimental.pallas import tpu as pltpu
from jax.sharding import PartitionSpec as P

PERIOD = 4096
LANES = 128
SUBLANES = 8
FULL = 32000.0
TINY = 2.0**-110
CODE = 1024.0
VMEM_BYTES = 56 * 1024 * 1024
F32 = jnp.float32
BF16 = jnp.bfloat16


def pack_pair(upper, lower):
    top = jnp.max(jnp.maximum(jnp.abs(upper), jnp.abs(lower)), axis=0, keepdims=True)
    code = jnp.ceil(jnp.log2(jnp.maximum(top, TINY)) * CODE)
    gain = FULL * jnp.exp2(code * (-1.0 / CODE))
    high = jnp.round(upper * gain).astype(jnp.int32)
    low = jnp.round(lower * gain).astype(jnp.int32)
    words = (high << 16) | (low & 0xFFFF)
    return words, jnp.broadcast_to(code.astype(jnp.int32), (SUBLANES, upper.shape[1]))


def unpack_pair(words, code):
    step = jnp.exp2(code.astype(F32) * (1.0 / CODE)) * (1.0 / FULL)
    return (
        (words >> 16).astype(F32) * step,
        ((words << 16) >> 16).astype(F32) * step,
    )


def plus(a, b):
    return b if a is None else a if b is None else a + b


def minus(a, b):
    return a if b is None else -b if a is None else a - b


def turn(re, im, top, bottom):
    top %= bottom
    if 8 * top % bottom == 0:
        eighth = 8 * top // bottom
        if eighth == 0:
            return re, im
        if eighth == 4:
            return -re, -im
        if eighth == 2:
            return im, -re
        if eighth == 6:
            return -im, re
        half = math.sqrt(0.5)
        if eighth == 1:
            return (re + im) * half, (im - re) * half
        if eighth == 5:
            return (re + im) * -half, (re - im) * half
        if eighth == 3:
            return (im - re) * half, (re + im) * -half
        return (re - im) * half, (re + im) * half
    angle = 2.0 * math.pi * top / bottom
    c, s = math.cos(angle), math.sin(angle)
    return re * c + im * s, im * c - re * s


def complex_dft(points):
    n = len(points)
    if n == 1:
        return points
    even, odd = complex_dft(points[::2]), complex_dft(points[1::2])
    out = [None] * n
    for k in range(n // 2):
        re, im = turn(*odd[k], k, n)
        out[k] = (even[k][0] + re, even[k][1] + im)
        out[k + n // 2] = (even[k][0] - re, even[k][1] - im)
    return out


def odd_part(diff, n):
    quarter = n // 4
    return complex_dft([turn(diff[s], -diff[s + quarter], s, n) for s in range(quarter)])


def place_odd(out, odd, n):
    for index, (re, im) in enumerate(odd):
        k = 4 * index + 1
        if k <= n // 2:
            out[k] = (re, im)
        else:
            out[n - k] = (re, -im)


def real_dft(x):
    n = len(x)
    if n == 1:
        return [(x[0], None)]
    if n == 2:
        return [(x[0] + x[1], None), (x[0] - x[1], None)]
    half = n // 2
    out = [None] * (half + 1)
    out[::2] = real_dft([x[s] + x[s + half] for s in range(half)])
    place_odd(out, odd_part([x[s] - x[s + half] for s in range(half)], n), n)
    return out


def padded_real_dft(x):
    n = 2 * len(x)
    out = [None] * (len(x) + 1)
    out[::2] = real_dft(x)
    place_odd(out, odd_part(x, n), n)
    return out


def odd_back(spectrum, n):
    quarter = n // 4
    points = []
    for index in range(quarter):
        k = 4 * index + 1
        re, im = spectrum[k] if k <= n // 2 else spectrum[n - k]
        points.append((im if k <= n // 2 else -im, re))
    waves = [(re, im) for im, re in complex_dft(points)]
    first, second = [], []
    for s, (re, im) in enumerate(waves):
        im, re = turn(im, re, s, n)
        first.append(re)
        second.append(-im)
    return first + second


def real_back(spectrum):
    n = 2 * (len(spectrum) - 1)
    if n == 2:
        a, b = spectrum[0][0], spectrum[1][0]
        return [a + b, a - b]
    even = real_back(spectrum[::2])
    odd = odd_back(spectrum, n)
    return [a + b for a, b in zip(even, odd)] + [a - b for a, b in zip(even, odd)]


def padded_real_back(spectrum):
    n = 2 * (len(spectrum) - 1)
    even = real_back(spectrum[::2])
    return [a + b for a, b in zip(even, odd_back(spectrum, n))]


def stacked(matrix):
    high = matrix.astype(ml_dtypes.bfloat16)
    low = (matrix - high.astype(np.float64)).astype(ml_dtypes.bfloat16)
    return np.concatenate([high, high, low], axis=0)


def transform_tables(blocks):
    total = 2 * blocks * LANES
    inner = np.arange(LANES)[:, None] * np.arange(LANES)[None, :] % LANES
    angle = 2.0 * np.pi / LANES * inner
    c, s = np.cos(angle), np.sin(angle)
    ahead = np.block([[c, -s], [s, c]])
    back = np.block([[c, s], [-s, c]]) * (2.0 / total)
    turns = np.arange(blocks + 1)[:, None] * np.arange(LANES)[None, :] % total
    angle = 2.0 * np.pi / total * turns
    weight = np.ones((blocks + 1, 1))
    weight[0] = weight[-1] = 0.5
    twist = np.stack([np.cos(angle), np.sin(angle), np.cos(angle) * weight, np.sin(angle) * weight], axis=1)
    return (
        jnp.asarray(stacked(ahead)),
        jnp.asarray(stacked(back)),
        jnp.asarray(np.pad(twist, ((0, 0), (0, 4), (0, 0))), F32),
    )


def split_dot(value, table):
    high = value.astype(BF16)
    low = (value - high.astype(F32)).astype(BF16)
    return jnp.dot(jnp.concatenate([high, low, high], axis=1), table, preferred_element_type=F32)


def inner_ahead(value, twist, table):
    re, im = value[:, :LANES], value[:, LANES:]
    c, s = twist[0:1], twist[1:2]
    turned = jnp.concatenate([re * c + im * s, im * c - re * s], axis=1)
    return split_dot(turned, table)


def inner_back(value, twist, table):
    out = split_dot(value, table)
    re, im = out[:, :LANES], out[:, LANES:]
    c, s = twist[2:3], twist[3:4]
    return jnp.concatenate([re * c - im * s, im * c + re * s], axis=1)


def store_spectrum(ref, rows, spectrum):
    for k, (re, im) in enumerate(spectrum):
        ref[k, rows, :LANES] = re
        ref[k, rows, LANES:] = jnp.zeros_like(re) if im is None else im


def load_spectrum(ref, rows, count):
    return [(ref[k, rows, :LANES], ref[k, rows, LANES:]) for k in range(count)]


def later(previous, current, steps, lane):
    moved = pltpu.roll(current, steps, 1)
    if previous is None:
        return jnp.where(lane < steps, 0.0, moved), moved
    return jnp.where(lane < steps, previous, moved), moved


def earlier(following, current, steps, lane):
    moved = pltpu.roll(current, LANES - steps, 1)
    kept = lane < LANES - steps
    if following is None:
        return jnp.where(kept, moved, 0.0), moved
    return jnp.where(kept, moved, following), moved


def shifted_blocks(x_ref, rows, blocks, lane):
    one = two = None
    for block in range(blocks):
        x = x_ref[block, rows, :]
        back_one, one = later(one, x, 1, lane)
        back_two, two = later(two, x, 2, lane)
        yield block, (x, back_one, back_two)


def column(values, index):
    return values[:, index : index + 1]


def mix(taps, stream, terms):
    return sum(taps[3 * stream + j] * terms[j] for j in range(3))


def wide_taps(tap_ref, rows):
    taps = tap_ref[rows, :]
    return [jnp.broadcast_to(column(taps, i), (SUBLANES, LANES)) for i in range(9)]


def for_tiles(channels, step):
    def run(tile, carry):
        step(pl.ds(pl.multiple_of(tile * SUBLANES, SUBLANES), SUBLANES))
        return carry

    lax.fori_loop(0, channels // SUBLANES, run, 0)


def unit_turn(phase):
    phase = phase & (PERIOD - 1)
    quadrant = (phase + PERIOD // 8) >> 10
    angle = (phase - (quadrant << 10)).astype(F32) * (2.0 * math.pi / PERIOD)
    square = angle * angle
    sin = angle * (1.0 + square * (-1.0 / 6 + square * (1.0 / 120 + square * (-1.0 / 5040 + square * (1.0 / 362880)))))
    cos = 1.0 + square * (-0.5 + square * (1.0 / 24 + square * (-1.0 / 720 + square * (1.0 / 40320))))
    swap = (quadrant & 1) == 1
    c = jnp.where(swap, sin, cos)
    s = jnp.where(swap, cos, sin)
    c = jnp.where(((quadrant + 1) & 2) == 2, -c, c)
    s = jnp.where((quadrant & 2) == 2, -s, s)
    return c, s


RESTART = 16


def filter_blocks(weights, decays, seeds, blocks, modes):
    position = lax.broadcasted_iota(jnp.int32, (SUBLANES, LANES), 1)
    time = position.astype(F32)
    leap_decay = jnp.exp(decays * (-1.0 * LANES))
    leap_cos, leap_sin = unit_turn(seeds * LANES)
    leap_re, leap_im = leap_decay * leap_cos, leap_decay * leap_sin
    twice, size = 2.0 * leap_re, leap_decay * leap_decay
    starts = []
    for start in range(0, blocks, RESTART):
        if start == 0:
            starts.append((weights, None))
        else:
            fall = weights * jnp.exp(decays * (-1.0 * LANES * start))
            c, s = unit_turn(seeds * (LANES * start))
            starts.append((fall * c, fall * s))
    total = [None] * blocks
    for mode in range(modes):
        c, s = unit_turn(column(seeds, mode) * position)
        fall = jnp.exp(-column(decays, mode) * time)
        base_re, base_im = fall * c, fall * s
        wide = lambda v: jnp.broadcast_to(column(v, mode), (SUBLANES, LANES))
        jump_re, jump_im, ahead, behind = wide(leap_re), wide(leap_im), wide(twice), wide(size)
        for index, (start_re, start_im) in enumerate(starts):
            first = index * RESTART
            re, im = base_re, base_im
            if start_im is None:
                w = wide(start_re)
                re, im = w * re, w * im
            else:
                a, b = wide(start_re), wide(start_im)
                re, im = a * re - b * im, a * im + b * re
            old, new = re, jump_re * re - jump_im * im
            total[first] = plus(total[first], old)
            for block in range(first + 1, min(first + RESTART, blocks)):
                total[block] = plus(total[block], new)
                old, new = new, ahead * new - behind * old
    return total


def encode_kernel(value_ref, out_ref):
    height = value_ref.shape[2]
    words, code = pack_pair(value_ref[0, 0], value_ref[1, 0])
    out_ref[0, :height, :] = words
    out_ref[0, height:, :] = code


def decode_kernel(words_ref, out_ref):
    height = out_ref.shape[2]
    out_ref[0, 0], out_ref[1, 0] = unpack_pair(words_ref[0, :height, :], words_ref[0, height : height + 1, :])


def encode(value, blocks):
    half = value.shape[0] // 2 // blocks
    return pl.pallas_call(
        encode_kernel,
        grid=(blocks,),
        in_specs=[pl.BlockSpec((2, 1, half, LANES), lambda i: (0, i, 0, 0))],
        out_specs=pl.BlockSpec((1, half + SUBLANES, LANES), lambda i: (i, 0, 0)),
        out_shape=jax.ShapeDtypeStruct((blocks, half + SUBLANES, LANES), jnp.int32),
        name="encode_cotangent",
    )(value.reshape(2, blocks, half, LANES))


def decode(words, blocks):
    half = words.shape[1] - SUBLANES
    out = pl.pallas_call(
        decode_kernel,
        grid=(blocks,),
        in_specs=[pl.BlockSpec((1, half + SUBLANES, LANES), lambda i: (i, 0, 0))],
        out_specs=pl.BlockSpec((2, 1, half, LANES), lambda i: (0, i, 0, 0)),
        out_shape=jax.ShapeDtypeStruct((2, blocks, half, LANES), F32),
        name="decode_mixer",
    )(words)
    return out.reshape(2 * blocks * half, LANES)


def pack_table_kernel(mine_ref, other_ref, out_ref):
    total = mine_ref[...] + other_ref[...]
    half = total.shape[0] // 2
    words, code = pack_pair(total[:half], total[half:])
    out_ref[:half, :] = words
    out_ref[half:, :] = code


def unpack_table_kernel(words_ref, out_ref):
    half = out_ref.shape[0] // 2
    upper, lower = unpack_pair(words_ref[0, :half, :], words_ref[0, half : half + 1, :])
    out_ref[:half, :] = upper
    out_ref[half:, :] = lower


def one_hot_block(token_ref, block, vocab):
    wanted = token_ref[pl.ds(block, 1), :]
    entry = lax.broadcasted_iota(jnp.int32, (vocab, LANES), 0)
    return (entry == wanted).astype(F32).astype(BF16)


def forward_kernel(
    table_ref, token_ref, tap_ref, residue_ref, decay_ref, seed_ref, gain_ref, ahead_ref, back_ref, twist_ref,
    words_ref, response_ref, long_ref, x_ref,
    work_ref, mixed_ref, query_ref,
):
    blocks, channels, _ = x_ref.shape
    half = channels // 2
    vocab = table_ref.shape[1]
    modes = residue_ref.shape[1]
    tall = jnp.concatenate([table_ref[0].astype(F32).T, table_ref[1].astype(F32).T], axis=0).astype(BF16)

    @pl.loop(0, blocks // 2)
    def _(pair):
        hot = jnp.concatenate([one_hot_block(token_ref, 2 * pair + i, vocab) for i in range(2)], axis=1)
        found = jnp.dot(tall, hot, preferred_element_type=F32)
        x_ref[2 * pair] = found[:, :LANES]
        x_ref[2 * pair + 1] = found[:, LANES:]

    def filters(rows):
        decays = decay_ref[rows, :]
        weights = residue_ref[rows, :] * jnp.sqrt(decays + 1.0 / (blocks * LANES))
        taken = filter_blocks(weights, decays, seed_ref[rows, :], blocks, modes)
        store_spectrum(response_ref, rows, padded_real_dft(taken))

    def streams(rows):
        lane = lax.broadcasted_iota(jnp.int32, (SUBLANES, LANES), 1)
        taps = wide_taps(tap_ref, rows)
        mixed = []
        for block, terms in shifted_blocks(x_ref, rows, blocks, lane):
            query_ref[block, rows, :] = mix(taps, 0, terms)
            mixed.append(mix(taps, 1, terms) * mix(taps, 2, terms))
            mixed_ref[block, rows, :] = mixed[-1]
        store_spectrum(work_ref, rows, padded_real_dft(mixed))

    for_tiles(channels, filters)
    for_tiles(channels, streams)

    @pl.loop(0, blocks + 1)
    def _(k):
        twist = twist_ref[k]
        response = inner_ahead(response_ref[k], twist, ahead_ref[...])
        response_ref[k] = response
        spectrum = inner_ahead(work_ref[k], twist, ahead_ref[...])
        a, b = response[:, :LANES], response[:, LANES:]
        c, d = spectrum[:, :LANES], spectrum[:, LANES:]
        product = jnp.concatenate([a * c - b * d, a * d + b * c], axis=1)
        work_ref[k] = inner_back(product, twist, back_ref[...])

    def results(rows):
        conv = padded_real_back(load_spectrum(work_ref, rows, blocks + 1))
        gain = jnp.broadcast_to(gain_ref[rows, :], (SUBLANES, LANES))
        for block in range(blocks):
            long_out = conv[block] + gain * mixed_ref[block, rows, :]
            long_ref[block, rows, :] = long_out
            query_ref[block, rows, :] = query_ref[block, rows, :] * long_out

    for_tiles(channels, results)

    @pl.loop(0, blocks)
    def _(block):
        words, code = pack_pair(query_ref[block, :half, :], query_ref[block, half:, :])
        words_ref[block, :half, :] = words
        words_ref[block, half:, :] = code


def backward_kernel(
    words_ref, x_ref, long_ref, response_ref, token_ref, tap_ref, gain_ref, ahead_ref, back_ref, twist_ref,
    grad_ref,
    work_ref, cot_ref, late_ref,
):
    blocks, channels, _ = x_ref.shape
    half = channels // 2
    vocab = grad_ref.shape[1]

    @pl.loop(0, blocks)
    def _(block):
        upper, lower = unpack_pair(words_ref[block, :half, :], words_ref[block, half : half + 1, :])
        cot_ref[block, :half, :] = upper
        cot_ref[block, half:, :] = lower

    def streams(rows):
        lane = lax.broadcasted_iota(jnp.int32, (SUBLANES, LANES), 1)
        taps = wide_taps(tap_ref, rows)
        long_grad = []
        for block, terms in shifted_blocks(x_ref, rows, blocks, lane):
            long_grad.append(cot_ref[block, rows, :] * mix(taps, 0, terms))
            late_ref[block, rows, :] = long_grad[-1]
        store_spectrum(work_ref, rows, padded_real_dft(long_grad))

    for_tiles(channels, streams)

    @pl.loop(0, blocks + 1)
    def _(k):
        twist = twist_ref[k]
        spectrum = inner_ahead(work_ref[k], twist, ahead_ref[...])
        a, b = response_ref[k, :, :LANES], response_ref[k, :, LANES:]
        c, d = spectrum[:, :LANES], spectrum[:, LANES:]
        product = jnp.concatenate([a * c + b * d, a * d - b * c], axis=1)
        work_ref[k] = inner_back(product, twist, back_ref[...])

    def results(rows):
        lane = lax.broadcasted_iota(jnp.int32, (SUBLANES, LANES), 1)
        taps = wide_taps(tap_ref, rows)
        gain = jnp.broadcast_to(gain_ref[rows, :], (SUBLANES, LANES))
        correlated = padded_real_back(load_spectrum(work_ref, rows, blocks + 1))
        for block in range(blocks):
            late_ref[block, rows, :] = correlated[block] + gain * late_ref[block, rows, :]
        held = None
        for block, terms in shifted_blocks(x_ref, rows, blocks, lane):
            mixed_grad = late_ref[block, rows, :]
            grads = (
                cot_ref[block, rows, :] * long_ref[block, rows, :],
                mixed_grad * mix(taps, 2, terms),
                mixed_grad * mix(taps, 1, terms),
            )
            now, next_one, next_two = (sum(taps[3 * s + j] * grads[s] for s in range(3)) for j in range(3))
            next_one = pltpu.roll(next_one, LANES - 1, 1)
            next_two = pltpu.roll(next_two, LANES - 2, 1)
            if held is not None:
                base, one, two = held
                late_ref[block - 1, rows, :] = (
                    base + jnp.where(lane < LANES - 1, one, next_one) + jnp.where(lane < LANES - 2, two, next_two)
                )
            held = (now, next_one, next_two)
        base, one, two = held
        late_ref[blocks - 1, rows, :] = (
            base + jnp.where(lane < LANES - 1, one, 0.0) + jnp.where(lane < LANES - 2, two, 0.0)
        )

    for_tiles(channels, results)

    def gather(block, total):
        hot = one_hot_block(token_ref, block, vocab)
        value = late_ref[block]
        high = value.astype(BF16)
        low = (value - high.astype(F32)).astype(BF16)
        return total + lax.dot_general(
            jnp.concatenate([hot, hot], axis=1),
            jnp.concatenate([high, low], axis=1),
            (((1,), (1,)), ((), ())),
            preferred_element_type=F32,
        )

    total = lax.fori_loop(0, blocks, gather, jnp.zeros((vocab, channels), F32))
    grad_ref[0] = total[:, :half]
    grad_ref[1] = total[:, half:]


def in_vmem(count):
    return [pl.BlockSpec(memory_space=pltpu.VMEM)] * count


def body(token_ids, embedding, conv_taps, residues, decays, filter_seed, skip_gain, cotangent):
    blocks = lax.axis_size("ctx")
    rank = lax.axis_index("ctx")
    side = lax.axis_index("fsdp")
    width = conv_taps.shape[2]
    vocab = embedding.shape[0]
    half = width // 2 // blocks
    channels = 2 * half
    modes = residues.shape[1]

    cot_words = lax.all_to_all(encode(cotangent[0], blocks), "ctx", split_axis=0, concat_axis=0, tiled=True)

    tokens = lax.all_gather(token_ids, "ctx", axis=0, tiled=True)
    own_columns = lax.dynamic_slice_in_dim(embedding, rank * half, half, 1)
    other_columns = lax.ppermute(own_columns, "fsdp", [(0, 1), (1, 0)])
    table = jnp.where(
        side == 0, jnp.stack([own_columns, other_columns]), jnp.stack([other_columns, own_columns])
    )

    def slab(value):
        parts = value.reshape(2, blocks, half, value.shape[1])
        return lax.dynamic_index_in_dim(parts, rank, 1, keepdims=False).reshape(channels, value.shape[1])

    taps = lax.dynamic_index_in_dim(conv_taps.reshape(9, 2, blocks, half), rank, 2, keepdims=False)
    taps = jnp.pad(taps.reshape(9, channels).T, ((0, 0), (0, 7)))
    gain = slab(skip_gain[:, None])
    ahead, back, twist = transform_tables(blocks)
    slots = blocks + 1
    stack = jax.ShapeDtypeStruct((blocks, channels, LANES), F32)
    params = pltpu.CompilerParams(vmem_limit_bytes=VMEM_BYTES)
    work = pltpu.VMEM((slots, channels, 2 * LANES), F32)
    buffer = pltpu.VMEM((blocks, channels, LANES), F32)

    mixer_words, response, long_out, x = pl.pallas_call(
        forward_kernel,
        in_specs=in_vmem(10),
        out_specs=tuple(in_vmem(4)),
        out_shape=(
            jax.ShapeDtypeStruct((blocks, half + SUBLANES, LANES), jnp.int32),
            jax.ShapeDtypeStruct((slots, channels, 2 * LANES), F32),
            stack,
            stack,
        ),
        scratch_shapes=[work, buffer, buffer],
        compiler_params=params,
        name="forward",
    )(table, tokens, taps, slab(residues), slab(decays), slab(filter_seed), gain, ahead, back, twist)

    mixer_words = lax.all_to_all(mixer_words, "ctx", split_axis=0, concat_axis=0, tiled=True)

    grads = pl.pallas_call(
        backward_kernel,
        in_specs=in_vmem(10),
        out_specs=in_vmem(1)[0],
        out_shape=jax.ShapeDtypeStruct((2, vocab, half), F32),
        scratch_shapes=[work, buffer, buffer],
        compiler_params=params,
        name="backward",
    )(cot_words, x, long_out, response, tokens, taps, gain, ahead, back, twist)

    mine = lax.dynamic_index_in_dim(grads, side, 0, keepdims=False)
    theirs = lax.dynamic_index_in_dim(grads, 1 - side, 0, keepdims=False)
    theirs = lax.ppermute(theirs, "fsdp", [(0, 1), (1, 0)])
    tall = vocab // 2 + SUBLANES
    grad_words = pl.pallas_call(
        pack_table_kernel,
        out_shape=jax.ShapeDtypeStruct((tall, half), jnp.int32),
        name="pack_table",
    )(mine, theirs)
    grad_words = lax.all_gather(grad_words, "ctx", axis=0, tiled=False)
    group = max(1, LANES // half)
    if group > 1:
        grad_words = grad_words.reshape(blocks // group, group, tall, half)
        grad_words = jnp.swapaxes(grad_words, 1, 2).reshape(blocks // group, tall, group * half)
    embed_grad = pl.pallas_call(
        unpack_table_kernel,
        grid=(blocks // group,),
        in_specs=[pl.BlockSpec((1, tall, group * half), lambda i: (i, 0, 0))],
        out_specs=pl.BlockSpec((vocab, group * half), lambda i: (0, i)),
        out_shape=jax.ShapeDtypeStruct((vocab, blocks * half), F32),
        name="unpack_table",
    )(grad_words)
    mixer_out = decode(mixer_words, blocks)
    return mixer_out[None], embed_grad


def solution(mesh):
    placed = (P("fsdp", "ctx"), P(None, "fsdp"), P(), P(), P(), P(), P(), P("fsdp", None, "ctx"))
    return jax.shard_map(
        body,
        mesh=mesh,
        in_specs=placed,
        out_specs=(P("fsdp", None, "ctx"), P(None, "fsdp")),
        check_vma=False,
    )
```

```python
import math

import jax
import jax.numpy as jnp
import ml_dtypes
import numpy as np
from jax import lax
from jax.experimental import pallas as pl
from jax.experimental.pallas import tpu as pltpu
from jax.sharding import PartitionSpec as P

PERIOD = 4096
LANES = 128
SUBLANES = 8
FULL = 32000.0
TINY = 2.0**-110
CODE = 1024.0
VMEM_BYTES = 60 * 1024 * 1024
F32 = jnp.float32
BF16 = jnp.bfloat16


def pack_pair(upper, lower):
    top = jnp.max(jnp.maximum(jnp.abs(upper), jnp.abs(lower)), axis=0, keepdims=True)
    code = jnp.ceil(jnp.log2(jnp.maximum(top, TINY)) * CODE)
    gain = FULL * jnp.exp2(code * (-1.0 / CODE))
    high = jnp.round(upper * gain).astype(jnp.int32)
    low = jnp.round(lower * gain).astype(jnp.int32)
    words = (high << 16) | (low & 0xFFFF)
    return words, jnp.broadcast_to(code.astype(jnp.int32), (SUBLANES, upper.shape[1]))


def unpack_pair(words, code):
    step = jnp.exp2(code.astype(F32) * (1.0 / CODE)) * (1.0 / FULL)
    return (
        (words >> 16).astype(F32) * step,
        ((words << 16) >> 16).astype(F32) * step,
    )


def plus(a, b):
    return b if a is None else a if b is None else a + b


def minus(a, b):
    return a if b is None else -b if a is None else a - b


def turn(re, im, top, bottom):
    top %= bottom
    if 8 * top % bottom == 0:
        eighth = 8 * top // bottom
        if eighth == 0:
            return re, im
        if eighth == 4:
            return -re, -im
        if eighth == 2:
            return im, -re
        if eighth == 6:
            return -im, re
        half = math.sqrt(0.5)
        if eighth == 1:
            return (re + im) * half, (im - re) * half
        if eighth == 5:
            return (re + im) * -half, (re - im) * half
        if eighth == 3:
            return (im - re) * half, (re + im) * -half
        return (re - im) * half, (re + im) * half
    angle = 2.0 * math.pi * top / bottom
    c, s = math.cos(angle), math.sin(angle)
    return re * c + im * s, im * c - re * s


def complex_dft(points):
    n = len(points)
    if n == 1:
        return points
    even, odd = complex_dft(points[::2]), complex_dft(points[1::2])
    out = [None] * n
    for k in range(n // 2):
        re, im = turn(*odd[k], k, n)
        out[k] = (even[k][0] + re, even[k][1] + im)
        out[k + n // 2] = (even[k][0] - re, even[k][1] - im)
    return out


def odd_part(diff, n):
    quarter = n // 4
    return complex_dft([turn(diff[s], -diff[s + quarter], s, n) for s in range(quarter)])


def place_odd(out, odd, n):
    for index, (re, im) in enumerate(odd):
        k = 4 * index + 1
        if k <= n // 2:
            out[k] = (re, im)
        else:
            out[n - k] = (re, -im)


def real_dft(x):
    n = len(x)
    if n == 1:
        return [(x[0], None)]
    if n == 2:
        return [(x[0] + x[1], None), (x[0] - x[1], None)]
    half = n // 2
    out = [None] * (half + 1)
    out[::2] = real_dft([x[s] + x[s + half] for s in range(half)])
    place_odd(out, odd_part([x[s] - x[s + half] for s in range(half)], n), n)
    return out


def padded_real_dft(x):
    n = 2 * len(x)
    out = [None] * (len(x) + 1)
    out[::2] = real_dft(x)
    place_odd(out, odd_part(x, n), n)
    return out


def odd_back(spectrum, n):
    quarter = n // 4
    points = []
    for index in range(quarter):
        k = 4 * index + 1
        re, im = spectrum[k] if k <= n // 2 else spectrum[n - k]
        points.append((im if k <= n // 2 else -im, re))
    waves = [(re, im) for im, re in complex_dft(points)]
    first, second = [], []
    for s, (re, im) in enumerate(waves):
        im, re = turn(im, re, s, n)
        first.append(re)
        second.append(-im)
    return first + second


def real_back(spectrum):
    n = 2 * (len(spectrum) - 1)
    if n == 2:
        a, b = spectrum[0][0], spectrum[1][0]
        return [a + b, a - b]
    even = real_back(spectrum[::2])
    odd = odd_back(spectrum, n)
    return [a + b for a, b in zip(even, odd)] + [a - b for a, b in zip(even, odd)]


def padded_real_back(spectrum):
    n = 2 * (len(spectrum) - 1)
    even = real_back(spectrum[::2])
    return [a + b for a, b in zip(even, odd_back(spectrum, n))]


def stacked(matrix):
    high = matrix.astype(ml_dtypes.bfloat16)
    low = (matrix - high.astype(np.float64)).astype(ml_dtypes.bfloat16)
    return np.concatenate([high, high, low], axis=0)


def transform_tables(blocks):
    total = 2 * blocks * LANES
    inner = np.arange(LANES)[:, None] * np.arange(LANES)[None, :] % LANES
    angle = 2.0 * np.pi / LANES * inner
    c, s = np.cos(angle), np.sin(angle)
    ahead = np.block([[c, -s], [s, c]])
    back = np.block([[c, s], [-s, c]]) * (2.0 / total)
    turns = np.arange(blocks + 1)[:, None] * np.arange(LANES)[None, :] % total
    angle = 2.0 * np.pi / total * turns
    weight = np.ones((blocks + 1, 1))
    weight[0] = weight[-1] = 0.5
    twist = np.stack([np.cos(angle), np.sin(angle), np.cos(angle) * weight, np.sin(angle) * weight], axis=1)
    return (
        jnp.asarray(stacked(ahead)),
        jnp.asarray(stacked(back)),
        jnp.asarray(np.pad(twist, ((0, 0), (0, 4), (0, 0))), F32),
    )


def split_dot(value, table):
    high = value.astype(BF16)
    low = (value - high.astype(F32)).astype(BF16)
    return jnp.dot(jnp.concatenate([high, low, high], axis=1), table, preferred_element_type=F32)


def inner_ahead(value, twist, table):
    re, im = value[:, :LANES], value[:, LANES:]
    c, s = twist[0:1], twist[1:2]
    turned = jnp.concatenate([re * c + im * s, im * c - re * s], axis=1)
    return split_dot(turned, table)


def inner_back(value, twist, table):
    out = split_dot(value, table)
    re, im = out[:, :LANES], out[:, LANES:]
    c, s = twist[2:3], twist[3:4]
    return jnp.concatenate([re * c - im * s, im * c + re * s], axis=1)


def store_spectrum(ref, rows, spectrum):
    for k, (re, im) in enumerate(spectrum):
        ref[k, rows, :LANES] = re
        ref[k, rows, LANES:] = jnp.zeros_like(re) if im is None else im


def load_spectrum(ref, rows, count):
    return [(ref[k, rows, :LANES], ref[k, rows, LANES:]) for k in range(count)]


def later(previous, current, steps, lane):
    moved = pltpu.roll(current, steps, 1)
    if previous is None:
        return jnp.where(lane < steps, 0.0, moved), moved
    return jnp.where(lane < steps, previous, moved), moved


def earlier(following, current, steps, lane):
    moved = pltpu.roll(current, LANES - steps, 1)
    kept = lane < LANES - steps
    if following is None:
        return jnp.where(kept, moved, 0.0), moved
    return jnp.where(kept, moved, following), moved


def shifted_blocks(x_ref, rows, blocks, lane):
    one = two = None
    for block in range(blocks):
        x = x_ref[block, rows, :]
        back_one, one = later(one, x, 1, lane)
        back_two, two = later(two, x, 2, lane)
        yield block, (x, back_one, back_two)


def column(values, index):
    return values[:, index : index + 1]


def mix(taps, stream, terms):
    return sum(taps[3 * stream + j] * terms[j] for j in range(3))


def wide_column(ref, rows, index):
    return jnp.broadcast_to(ref[rows, index : index + 1], (SUBLANES, LANES))


def wide_taps(ref, rows):
    return [wide_column(ref, rows, i) for i in range(9)]


def for_tiles(channels, step):
    def run(tile, carry):
        step(pl.ds(pl.multiple_of(tile * SUBLANES, SUBLANES), SUBLANES))
        return carry

    lax.fori_loop(0, channels // SUBLANES, run, 0)


def unit_turn(phase):
    phase = phase & (PERIOD - 1)
    quadrant = (phase + PERIOD // 8) >> 10
    angle = (phase - (quadrant << 10)).astype(F32) * (2.0 * math.pi / PERIOD)
    square = angle * angle
    sin = angle * (1.0 + square * (-1.0 / 6 + square * (1.0 / 120 + square * (-1.0 / 5040 + square * (1.0 / 362880)))))
    cos = 1.0 + square * (-0.5 + square * (1.0 / 24 + square * (-1.0 / 720 + square * (1.0 / 40320))))
    swap = (quadrant & 1) == 1
    c = jnp.where(swap, sin, cos)
    s = jnp.where(swap, cos, sin)
    c = jnp.where(((quadrant + 1) & 2) == 2, -c, c)
    s = jnp.where((quadrant & 2) == 2, -s, s)
    return c, s


RESTART = 16


def filter_blocks(weights, decays, seeds, blocks, modes):
    position = lax.broadcasted_iota(jnp.int32, (SUBLANES, LANES), 1)
    time = position.astype(F32)
    leap_decay = jnp.exp(decays * (-1.0 * LANES))
    leap_cos, leap_sin = unit_turn(seeds * LANES)
    leap_re, leap_im = leap_decay * leap_cos, leap_decay * leap_sin
    twice, size = 2.0 * leap_re, leap_decay * leap_decay
    starts = []
    for start in range(0, blocks, RESTART):
        if start == 0:
            starts.append((weights, None))
        else:
            fall = weights * jnp.exp(decays * (-1.0 * LANES * start))
            c, s = unit_turn(seeds * (LANES * start))
            starts.append((fall * c, fall * s))
    total = [None] * blocks
    for mode in range(modes):
        c, s = unit_turn(column(seeds, mode) * position)
        fall = jnp.exp(-column(decays, mode) * time)
        base_re, base_im = fall * c, fall * s
        wide = lambda v: jnp.broadcast_to(column(v, mode), (SUBLANES, LANES))
        jump_re, jump_im, ahead, behind = wide(leap_re), wide(leap_im), wide(twice), wide(size)
        for index, (start_re, start_im) in enumerate(starts):
            first = index * RESTART
            re, im = base_re, base_im
            if start_im is None:
                w = wide(start_re)
                re, im = w * re, w * im
            else:
                a, b = wide(start_re), wide(start_im)
                re, im = a * re - b * im, a * im + b * re
            old, new = re, jump_re * re - jump_im * im
            total[first] = plus(total[first], old)
            for block in range(first + 1, min(first + RESTART, blocks)):
                total[block] = plus(total[block], new)
                old, new = new, ahead * new - behind * old
    return total


GAIN_COLUMN = 9
UNROLLED = 32


def over_slots(count, step):
    if count <= UNROLLED:
        for k in range(count):
            step(k)
    else:
        pl.loop(0, count)(step)


def encode_kernel(value_ref, out_ref):
    height = value_ref.shape[2]
    for i in range(value_ref.shape[1]):
        words, code = pack_pair(value_ref[0, i], value_ref[1, i])
        out_ref[i, :height, :] = words
        out_ref[i, height:, :] = code


def decode_kernel(words_ref, out_ref):
    height = out_ref.shape[2]
    for i in range(out_ref.shape[1]):
        upper, lower = unpack_pair(words_ref[i, :height, :], words_ref[i, height : height + 1, :])
        out_ref[0, i] = upper
        out_ref[1, i] = lower


def encode(value, blocks):
    half = value.shape[0] // 2 // blocks
    some = blocks // 4
    return pl.pallas_call(
        encode_kernel,
        grid=(blocks // some,),
        in_specs=[pl.BlockSpec((2, some, half, LANES), lambda i: (0, i, 0, 0))],
        out_specs=pl.BlockSpec((some, half + SUBLANES, LANES), lambda i: (i, 0, 0)),
        out_shape=jax.ShapeDtypeStruct((blocks, half + SUBLANES, LANES), jnp.int32),
        cost_estimate=takes(2),
        name="encode_cotangent",
    )(value.reshape(2, blocks, half, LANES))


def decode(words, blocks):
    half = words.shape[1] - SUBLANES
    some = blocks // 4
    out = pl.pallas_call(
        decode_kernel,
        grid=(blocks // some,),
        in_specs=[pl.BlockSpec((some, half + SUBLANES, LANES), lambda i: (i, 0, 0))],
        out_specs=pl.BlockSpec((2, some, half, LANES), lambda i: (0, i, 0, 0)),
        out_shape=jax.ShapeDtypeStruct((2, blocks, half, LANES), F32),
        cost_estimate=takes(2),
        name="decode_mixer",
    )(words)
    return out.reshape(2 * blocks * half, LANES)


def takes(microseconds):
    return pl.CostEstimate(flops=int(microseconds * 1e9), bytes_accessed=int(microseconds * 3e6), transcendentals=0)


def pack_table_kernel(mine_ref, other_ref, out_ref):
    total = mine_ref[...] + other_ref[...]
    half = total.shape[0] // 2
    words, code = pack_pair(total[:half], total[half:])
    out_ref[:half, :] = words
    out_ref[half:, :] = code


def unpack_table_kernel(words_ref, out_ref):
    half = out_ref.shape[0] // 2
    upper, lower = unpack_pair(words_ref[0, :half, :], words_ref[0, half : half + 1, :])
    out_ref[:half, :] = upper
    out_ref[half:, :] = lower


def unpack_square_kernel(rank_ref, *refs):
    *word_refs, out_ref = refs
    half = out_ref.shape[0] // 2
    for away, ref in enumerate(word_refs):
        upper, lower = unpack_pair(ref[0, :half, :], ref[0, half : half + 1, :])
        place = pl.ds(pl.multiple_of(((rank_ref[0] & 3) ^ away) * LANES, LANES), LANES)
        out_ref[:half, place] = upper
        out_ref[half:, place] = lower


def one_hot_block(token_ref, block, vocab):
    wanted = token_ref[block, 0:1, :]
    entry = lax.broadcasted_iota(jnp.int32, (vocab, LANES), 0)
    return (entry == wanted).astype(F32).astype(BF16)


def filter_kernel(
    _,
    tap_ref, tap_next_ref, gain_ref, gain_next_ref, residue_ref, residue_next_ref, decay_ref, decay_next_ref, seed_ref, seed_next_ref,
    ahead_ref, twist_ref,
    response_out, side_ref,
    work_ref, response_ref, mode_ref, sems,
):
    slots, channels, _ = response_ref.shape
    blocks = slots - 1
    half = channels // 2
    modes = residue_ref.shape[0]
    for rows, parts in (
        (slice(0, half), (tap_ref, gain_ref, residue_ref, decay_ref, seed_ref)),
        (slice(half, channels), (tap_next_ref, gain_next_ref, residue_next_ref, decay_next_ref, seed_next_ref)),
    ):
        taps, gain, residues, decays, seeds = (part[...] for part in parts)
        weights = residues * jnp.sqrt(decays + 1.0 / (blocks * LANES))
        listed = jnp.concatenate([taps[0], taps[1], taps[2], gain], axis=0)
        side_ref[rows, :] = jnp.pad(listed, ((0, LANES - listed.shape[0]), (0, 0))).T
        listed = jnp.concatenate([weights, decays, seeds.astype(F32)], axis=0)
        mode_ref[rows, :] = jnp.pad(listed, ((0, LANES - listed.shape[0]), (0, 0))).T

    def filters(rows):
        weights, decays, seeds = (mode_ref[rows, i * modes : (i + 1) * modes] for i in range(3))
        store_spectrum(work_ref, rows, padded_real_dft(filter_blocks(weights, decays, seeds.astype(jnp.int32), blocks, modes)))

    for_tiles(channels, filters)

    def step(k):
        response_ref[k] = inner_ahead(work_ref[k], twist_ref[k], ahead_ref[...])
        pltpu.make_async_copy(response_ref.at[k], response_out.at[k], sems.at[k]).start()

    over_slots(slots, step)

    @pl.loop(0, slots)
    def _(k):
        pltpu.make_async_copy(response_ref.at[k], response_out.at[k], sems.at[k]).wait()


def filtered(work_ref, response_ref, ahead_ref, back_ref, twist_ref, sign):
    def step(k):
        twist = twist_ref[k]
        spectrum = inner_ahead(work_ref[k], twist, ahead_ref[...])
        a, b = response_ref[k, :, :LANES], response_ref[k, :, LANES:] * sign
        c, d = spectrum[:, :LANES], spectrum[:, LANES:]
        product = jnp.concatenate([a * c - b * d, a * d + b * c], axis=1)
        work_ref[k] = inner_back(product, twist, back_ref[...])

    over_slots(work_ref.shape[0], step)


def forward_kernel(
    place_ref, own_ref, other_ref, token_ref, side_ref, *refs
):
    held, (words_ref, long_out_ref, x_out_ref), refs = refs[:4], refs[4:7], refs[7:]
    (response_ref, ahead_ref, back_ref, twist_ref), (long_ref, x_ref, work_ref, mixed_ref, query_ref, sems) = refs[:4], refs[4:]
    tables = [pltpu.make_async_copy(held[i], refs[i], sems.at[i]) for i in range(4)]
    x_copy = pltpu.make_async_copy(x_ref, x_out_ref, sems.at[4])
    long_copy = pltpu.make_async_copy(long_ref, long_out_ref, sems.at[5])
    for copy in tables:
        copy.start()
    blocks, channels, _ = x_ref.shape
    half = channels // 2
    vocab = own_ref.shape[0]
    own, other = own_ref[...].astype(F32).T, other_ref[...].astype(F32).T
    first = place_ref[1] == 0
    tall = jnp.concatenate([jnp.where(first, own, other), jnp.where(first, other, own)], axis=0).astype(BF16)

    def lookup(pair):
        hot = jnp.concatenate([one_hot_block(token_ref, 2 * pair + i, vocab) for i in range(2)], axis=1)
        found = jnp.dot(tall, hot, preferred_element_type=F32)
        x_ref[2 * pair] = found[:, :LANES]
        x_ref[2 * pair + 1] = found[:, LANES:]

    over_slots(blocks // 2, lookup)
    x_copy.start()

    def streams(rows):
        lane = lax.broadcasted_iota(jnp.int32, (SUBLANES, LANES), 1)
        taps = wide_taps(side_ref, rows)
        mixed = []
        for block, terms in shifted_blocks(x_ref, rows, blocks, lane):
            query_ref[block, rows, :] = mix(taps, 0, terms)
            mixed.append(mix(taps, 1, terms) * mix(taps, 2, terms))
            mixed_ref[block, rows, :] = mixed[-1]
        store_spectrum(work_ref, rows, padded_real_dft(mixed))

    for_tiles(channels, streams)
    for copy in tables:
        copy.wait()
    filtered(work_ref, response_ref, ahead_ref, back_ref, twist_ref, 1.0)

    def results(rows):
        conv = padded_real_back(load_spectrum(work_ref, rows, blocks + 1))
        gain = wide_column(side_ref, rows, GAIN_COLUMN)
        for block in range(blocks):
            long_out = conv[block] + gain * mixed_ref[block, rows, :]
            long_ref[block, rows, :] = long_out
            query_ref[block, rows, :] = query_ref[block, rows, :] * long_out

    for_tiles(channels, results)
    long_copy.start()

    @pl.loop(0, blocks)
    def _(block):
        words, code = pack_pair(query_ref[block, :half, :], query_ref[block, half:, :])
        words_ref[block, :half, :] = words
        words_ref[block, half:, :] = code

    x_copy.wait()
    long_copy.wait()


def backward_kernel(
    words_ref, token_ref, side_ref, *refs
):
    held, grad_ref, refs = refs[:6], refs[6], refs[7:]
    x_ref, response_ref, ahead_ref, back_ref, twist_ref, long_ref, work_ref, cot_ref, late_ref, sems = refs
    copies = [pltpu.make_async_copy(held[i], refs[i], sems.at[i]) for i in range(6)]
    for copy in copies:
        copy.start()
    blocks, channels, _ = x_ref.shape
    half = channels // 2
    vocab = grad_ref.shape[1]

    @pl.loop(0, blocks)
    def _(block):
        upper, lower = unpack_pair(words_ref[block, :half, :], words_ref[block, half : half + 1, :])
        cot_ref[block, :half, :] = upper
        cot_ref[block, half:, :] = lower

    copies[0].wait()

    def streams(rows):
        lane = lax.broadcasted_iota(jnp.int32, (SUBLANES, LANES), 1)
        taps = wide_taps(side_ref, rows)
        long_grad = []
        for block, terms in shifted_blocks(x_ref, rows, blocks, lane):
            long_grad.append(cot_ref[block, rows, :] * mix(taps, 0, terms))
            late_ref[block, rows, :] = long_grad[-1]
        store_spectrum(work_ref, rows, padded_real_dft(long_grad))

    for_tiles(channels, streams)

    for copy in copies[1:]:
        copy.wait()
    filtered(work_ref, response_ref, ahead_ref, back_ref, twist_ref, -1.0)

    def results(rows):
        lane = lax.broadcasted_iota(jnp.int32, (SUBLANES, LANES), 1)
        taps = wide_taps(side_ref, rows)
        gain = wide_column(side_ref, rows, GAIN_COLUMN)
        correlated = padded_real_back(load_spectrum(work_ref, rows, blocks + 1))
        for block in range(blocks):
            late_ref[block, rows, :] = correlated[block] + gain * late_ref[block, rows, :]
        held = None
        for block, terms in shifted_blocks(x_ref, rows, blocks, lane):
            mixed_grad = late_ref[block, rows, :]
            grads = (
                cot_ref[block, rows, :] * long_ref[block, rows, :],
                mixed_grad * mix(taps, 2, terms),
                mixed_grad * mix(taps, 1, terms),
            )
            now, next_one, next_two = (sum(taps[3 * s + j] * grads[s] for s in range(3)) for j in range(3))
            next_one = pltpu.roll(next_one, LANES - 1, 1)
            next_two = pltpu.roll(next_two, LANES - 2, 1)
            if held is not None:
                base, one, two = held
                late_ref[block - 1, rows, :] = (
                    base + jnp.where(lane < LANES - 1, one, next_one) + jnp.where(lane < LANES - 2, two, next_two)
                )
            held = (now, next_one, next_two)
        base, one, two = held
        late_ref[blocks - 1, rows, :] = (
            base + jnp.where(lane < LANES - 1, one, 0.0) + jnp.where(lane < LANES - 2, two, 0.0)
        )

    for_tiles(channels, results)

    def gather(block, total):
        hot = one_hot_block(token_ref, block, vocab)
        value = late_ref[block]
        high = value.astype(BF16)
        low = (value - high.astype(F32)).astype(BF16)
        return total + lax.dot_general(
            jnp.concatenate([hot, hot], axis=1),
            jnp.concatenate([high, low], axis=1),
            (((1,), (1,)), ((), ())),
            preferred_element_type=F32,
        )

    total = lax.fori_loop(0, blocks, gather, jnp.zeros((vocab, channels), F32))
    grad_ref[0] = total[:, :half]
    grad_ref[1] = total[:, half:]


def anywhere(count):
    return [pl.BlockSpec(memory_space=pl.ANY)] * count


def in_vmem(count):
    return [pl.BlockSpec(memory_space=pltpu.VMEM)] * count


def gather_square(value, rank):
    def swap(part, bits):
        return lax.ppermute(part, "ctx", [(i, i ^ bits) for i in range(16)])

    column_of = jnp.stack([value] + [swap(value, bits) for bits in (4, 8, 12)])
    beside, below = swap(column_of, 1), swap(column_of, 2)
    across = jnp.concatenate([swap(beside[:2], 2), swap(below[2:], 1)])
    return column_of, beside, below, across


def body(token_ids, embedding, conv_taps, residues, decays, filter_seed, skip_gain, cotangent):
    blocks = lax.axis_size("ctx")
    rank = lax.axis_index("ctx")
    side = lax.axis_index("fsdp")
    width = conv_taps.shape[2]
    vocab = embedding.shape[0]
    half = width // 2 // blocks
    channels = 2 * half
    modes = residues.shape[1]
    slots = blocks + 1
    place = jnp.stack([rank, side]).astype(jnp.int32)
    other_core = [(0, 1), (1, 0)]

    def exchange(value):
        return lax.all_to_all(value, "ctx", split_axis=0, concat_axis=0, tiled=True)

    tokens = exchange(jnp.broadcast_to(token_ids[None], (blocks, SUBLANES, LANES)))
    cot_words = exchange(encode(cotangent[0], blocks))
    own_columns = lax.dynamic_slice_in_dim(embedding, rank * half, half, 1)
    other_columns = lax.ppermute(own_columns, "fsdp", other_core)

    ahead, back, twist = transform_tables(blocks)
    stack = jax.ShapeDtypeStruct((blocks, channels, LANES), F32)
    spectra = (slots, channels, 2 * LANES)
    work = pltpu.VMEM(spectra, F32)
    buffer = pltpu.VMEM((blocks, channels, LANES), F32)
    tables = [work, pltpu.VMEM(ahead.shape, BF16), pltpu.VMEM(back.shape, BF16), pltpu.VMEM(twist.shape, F32)]

    def halves(value):
        lead = value.shape[:-1]
        zeros = (0,) * len(lead)
        if half % LANES == 0:
            return [value, value], [
                pl.BlockSpec((*lead, half), lambda i, at: (*zeros, at[0])),
                pl.BlockSpec((*lead, half), lambda i, at: (*zeros, blocks + at[0])),
            ]
        parts = [
            lax.dynamic_slice_in_dim(value, start + rank * half, half, len(lead)) for start in (0, width // 2)
        ]
        return parts, [pl.BlockSpec((*lead, half), lambda i, at: (*zeros, 0))] * 2

    listed = [halves(v) for v in (conv_taps, skip_gain[None], residues.T, decays.T, filter_seed.T)]
    response, sides = pl.pallas_call(
        filter_kernel,
        grid_spec=pltpu.PrefetchScalarGridSpec(
            num_scalar_prefetch=1,
            grid=(1,),
            in_specs=[spec for _, specs in listed for spec in specs] + in_vmem(2),
            out_specs=(pl.BlockSpec(memory_space=pl.ANY), *in_vmem(1)),
            scratch_shapes=[work, work, pltpu.VMEM((channels, LANES), F32), pltpu.SemaphoreType.DMA((slots,))],
        ),
        out_shape=(jax.ShapeDtypeStruct(spectra, F32), jax.ShapeDtypeStruct((channels, LANES), F32)),
        compiler_params=pltpu.CompilerParams(vmem_limit_bytes=VMEM_BYTES),
        cost_estimate=takes(15),
        name="modal_filter",
    )(place, *[part for parts, _ in listed for part in parts], ahead, twist)

    mixer_words, long_out, x = pl.pallas_call(
        forward_kernel,
        in_specs=[pl.BlockSpec(memory_space=pltpu.SMEM)] + in_vmem(4) + anywhere(4),
        out_specs=(*in_vmem(1), *anywhere(2)),
        out_shape=(jax.ShapeDtypeStruct((blocks, half + SUBLANES, LANES), jnp.int32), stack, stack),
        scratch_shapes=tables + [buffer, buffer, work, buffer, buffer, pltpu.SemaphoreType.DMA((6,))],
        compiler_params=pltpu.CompilerParams(vmem_limit_bytes=VMEM_BYTES),
        cost_estimate=takes(18),
        name="forward",
    )(place, own_columns, other_columns, tokens, sides, response, ahead, back, twist)

    mixer_words = exchange(mixer_words)

    grads = pl.pallas_call(
        backward_kernel,
        in_specs=in_vmem(3) + anywhere(6),
        out_specs=in_vmem(1)[0],
        out_shape=jax.ShapeDtypeStruct((2, vocab, half), F32),
        scratch_shapes=[buffer, *tables, buffer, work, buffer, buffer, pltpu.SemaphoreType.DMA((6,))],
        compiler_params=pltpu.CompilerParams(vmem_limit_bytes=VMEM_BYTES),
        cost_estimate=takes(20),
        name="backward",
    )(cot_words, tokens, sides, x, response, ahead, back, twist, long_out)

    mine = lax.dynamic_index_in_dim(grads, side, 0, keepdims=False)
    theirs = lax.dynamic_index_in_dim(grads, 1 - side, 0, keepdims=False)
    theirs = lax.ppermute(theirs, "fsdp", other_core)
    tall = vocab // 2 + SUBLANES
    grad_words = pl.pallas_call(
        pack_table_kernel,
        out_shape=jax.ShapeDtypeStruct((tall, half), jnp.int32),
        cost_estimate=takes(1),
        name="pack_table",
    )(mine, theirs)
    table = jax.ShapeDtypeStruct((vocab, blocks * half), F32)
    if blocks == 16 and half == LANES:
        embed_grad = pl.pallas_call(
            unpack_square_kernel,
            grid_spec=pltpu.PrefetchScalarGridSpec(
                num_scalar_prefetch=1,
                grid=(4,),
                in_specs=[pl.BlockSpec((1, tall, half), lambda i, at: (i, 0, 0))] * 4,
                out_specs=pl.BlockSpec((vocab, 4 * half), lambda i, at: (0, (at[0] >> 2) ^ i)),
            ),
            out_shape=table,
            cost_estimate=takes(3),
            name="unpack_table",
        )(place, *gather_square(grad_words, rank))
    else:
        grad_words = lax.all_gather(grad_words, "ctx", axis=0, tiled=False)
        group = max(1, LANES // half)
        grad_words = grad_words.reshape(blocks // group, group, tall, half)
        grad_words = jnp.swapaxes(grad_words, 1, 2).reshape(blocks // group, tall, group * half)
        embed_grad = pl.pallas_call(
            unpack_table_kernel,
            grid=(blocks // group,),
            in_specs=[pl.BlockSpec((1, tall, group * half), lambda i: (i, 0, 0))],
            out_specs=pl.BlockSpec((vocab, group * half), lambda i: (0, i)),
            out_shape=table,
            cost_estimate=takes(3),
            name="unpack_table",
        )(grad_words)
    return decode(mixer_words, blocks)[None], embed_grad


def solution(mesh):
    placed = (P("fsdp", "ctx"), P(None, "fsdp"), P(), P(), P(), P(), P(), P("fsdp", None, "ctx"))
    return jax.shard_map(
        body,
        mesh=mesh,
        in_specs=placed,
        out_specs=(P("fsdp", None, "ctx"), P(None, "fsdp")),
        check_vma=False,
    )
```

```python
import functools
import math

import jax
import jax.numpy as jnp
import ml_dtypes
import numpy as np
from jax import lax
from jax.experimental import pallas as pl
from jax.experimental.pallas import tpu as pltpu
from jax.sharding import PartitionSpec as P

PERIOD = 4096
LANES = 128
SUBLANES = 8
FULL = 32000.0
TINY = 2.0**-110
CODE = 1024.0
VMEM_BYTES = 60 * 1024 * 1024
F32 = jnp.float32
BF16 = jnp.bfloat16


def pack_pair(upper, lower):
    top = jnp.max(jnp.maximum(jnp.abs(upper), jnp.abs(lower)), axis=0, keepdims=True)
    code = jnp.ceil(jnp.log2(jnp.maximum(top, TINY)) * CODE)
    gain = FULL * jnp.exp2(code * (-1.0 / CODE))
    high = jnp.round(upper * gain).astype(jnp.int32)
    low = jnp.round(lower * gain).astype(jnp.int32)
    words = (high << 16) | (low & 0xFFFF)
    return words, jnp.broadcast_to(code.astype(jnp.int32), (SUBLANES, upper.shape[1]))


def unpack_pair(words, code):
    step = jnp.exp2(code.astype(F32) * (1.0 / CODE)) * (1.0 / FULL)
    return (
        (words >> 16).astype(F32) * step,
        ((words << 16) >> 16).astype(F32) * step,
    )


def plus(a, b):
    return b if a is None else a if b is None else a + b


def minus(a, b):
    return a if b is None else -b if a is None else a - b


def turn(re, im, top, bottom):
    top %= bottom
    if 8 * top % bottom == 0:
        eighth = 8 * top // bottom
        if eighth == 0:
            return re, im
        if eighth == 4:
            return -re, -im
        if eighth == 2:
            return im, -re
        if eighth == 6:
            return -im, re
        half = math.sqrt(0.5)
        if eighth == 1:
            return (re + im) * half, (im - re) * half
        if eighth == 5:
            return (re + im) * -half, (re - im) * half
        if eighth == 3:
            return (im - re) * half, (re + im) * -half
        return (re - im) * half, (re + im) * half
    angle = 2.0 * math.pi * top / bottom
    c, s = math.cos(angle), math.sin(angle)
    return re * c + im * s, im * c - re * s


def complex_dft(points):
    n = len(points)
    if n == 1:
        return points
    even, odd = complex_dft(points[::2]), complex_dft(points[1::2])
    out = [None] * n
    for k in range(n // 2):
        re, im = turn(*odd[k], k, n)
        out[k] = (even[k][0] + re, even[k][1] + im)
        out[k + n // 2] = (even[k][0] - re, even[k][1] - im)
    return out


def odd_part(diff, n):
    quarter = n // 4
    return complex_dft([turn(diff[s], -diff[s + quarter], s, n) for s in range(quarter)])


def place_odd(out, odd, n):
    for index, (re, im) in enumerate(odd):
        k = 4 * index + 1
        if k <= n // 2:
            out[k] = (re, im)
        else:
            out[n - k] = (re, -im)


def real_dft(x):
    n = len(x)
    if n == 1:
        return [(x[0], None)]
    if n == 2:
        return [(x[0] + x[1], None), (x[0] - x[1], None)]
    half = n // 2
    out = [None] * (half + 1)
    out[::2] = real_dft([x[s] + x[s + half] for s in range(half)])
    place_odd(out, odd_part([x[s] - x[s + half] for s in range(half)], n), n)
    return out


def padded_real_dft(x):
    n = 2 * len(x)
    out = [None] * (len(x) + 1)
    out[::2] = real_dft(x)
    place_odd(out, odd_part(x, n), n)
    return out


def odd_back(spectrum, n):
    quarter = n // 4
    points = []
    for index in range(quarter):
        k = 4 * index + 1
        re, im = spectrum[k] if k <= n // 2 else spectrum[n - k]
        points.append((im if k <= n // 2 else -im, re))
    waves = [(re, im) for im, re in complex_dft(points)]
    first, second = [], []
    for s, (re, im) in enumerate(waves):
        im, re = turn(im, re, s, n)
        first.append(re)
        second.append(-im)
    return first + second


def real_back(spectrum):
    n = 2 * (len(spectrum) - 1)
    if n == 2:
        a, b = spectrum[0][0], spectrum[1][0]
        return [a + b, a - b]
    even = real_back(spectrum[::2])
    odd = odd_back(spectrum, n)
    return [a + b for a, b in zip(even, odd)] + [a - b for a, b in zip(even, odd)]


def padded_real_back(spectrum):
    n = 2 * (len(spectrum) - 1)
    even = real_back(spectrum[::2])
    return [a + b for a, b in zip(even, odd_back(spectrum, n))]


def stacked(matrix):
    high = matrix.astype(ml_dtypes.bfloat16)
    low = (matrix - high.astype(np.float64)).astype(ml_dtypes.bfloat16)
    return np.concatenate([high, high, low], axis=0)


def transform_tables(blocks):
    total = 2 * blocks * LANES
    inner = np.arange(LANES)[:, None] * np.arange(LANES)[None, :] % LANES
    angle = 2.0 * np.pi / LANES * inner
    c, s = np.cos(angle), np.sin(angle)
    ahead = np.block([[c, -s], [s, c]])
    back = np.block([[c, s], [-s, c]]) * (2.0 / total)
    turns = np.arange(blocks + 1)[:, None] * np.arange(LANES)[None, :] % total
    angle = 2.0 * np.pi / total * turns
    weight = np.ones((blocks + 1, 1))
    weight[0] = weight[-1] = 0.5
    twist = np.stack([np.cos(angle), np.sin(angle), np.cos(angle) * weight, np.sin(angle) * weight], axis=1)
    return (
        jnp.asarray(stacked(ahead)),
        jnp.asarray(stacked(back)),
        jnp.asarray(np.pad(twist, ((0, 0), (0, 4), (0, 0))), F32),
    )


def split_dot(value, table):
    high = value.astype(BF16)
    low = (value - high.astype(F32)).astype(BF16)
    return jnp.dot(jnp.concatenate([high, low, high], axis=1), table, preferred_element_type=F32)


def inner_ahead(value, twist, table):
    re, im = value[:, :LANES], value[:, LANES:]
    c, s = twist[0:1], twist[1:2]
    turned = jnp.concatenate([re * c + im * s, im * c - re * s], axis=1)
    return split_dot(turned, table)


def inner_back(value, twist, table):
    out = split_dot(value, table)
    re, im = out[:, :LANES], out[:, LANES:]
    c, s = twist[2:3], twist[3:4]
    return jnp.concatenate([re * c - im * s, im * c + re * s], axis=1)


def store_spectrum(ref, rows, spectrum):
    for k, (re, im) in enumerate(spectrum):
        ref[k, rows, :LANES] = re
        ref[k, rows, LANES:] = jnp.zeros_like(re) if im is None else im


def load_spectrum(ref, rows, count):
    return [(ref[k, rows, :LANES], ref[k, rows, LANES:]) for k in range(count)]


def later(previous, current, steps, lane):
    moved = pltpu.roll(current, steps, 1)
    if previous is None:
        return jnp.where(lane < steps, 0.0, moved), moved
    return jnp.where(lane < steps, previous, moved), moved


def earlier(following, current, steps, lane):
    moved = pltpu.roll(current, LANES - steps, 1)
    kept = lane < LANES - steps
    if following is None:
        return jnp.where(kept, moved, 0.0), moved
    return jnp.where(kept, moved, following), moved


def shifted_blocks(x_ref, rows, blocks, lane):
    one = two = None
    for block in range(blocks):
        x = x_ref[block, rows, :]
        back_one, one = later(one, x, 1, lane)
        back_two, two = later(two, x, 2, lane)
        yield block, (x, back_one, back_two)


def column(values, index):
    return values[:, index : index + 1]


def mix(taps, stream, terms):
    return sum(taps[3 * stream + j] * terms[j] for j in range(3))


def wide_taps(ref, rows):
    return [ref[i, rows, :] for i in range(9)]


def for_tiles(channels, unroll, step):
    def run(tile, carry):
        step(pl.ds(pl.multiple_of(tile * SUBLANES, SUBLANES), SUBLANES))
        return carry

    lax.fori_loop(0, channels // SUBLANES, run, 0, unroll=unroll)


def unit_turn(turns):
    angle = (turns - jnp.round(turns)) * math.pi
    square = angle * angle
    sin, cos = SINE[-1], COSINE[-1]
    for coefficient in SINE[-2::-1]:
        sin = sin * square + coefficient
    for coefficient in COSINE[-2::-1]:
        cos = cos * square + coefficient
    sin = sin * angle
    twice = sin + sin
    return 1.0 - twice * sin, twice * cos


def fitted(function, terms):
    top = (math.pi / 2) ** 2
    points = top / 2 * (1 + np.cos(np.pi * (np.arange(64) + 0.5) / 64))
    series = np.polynomial.chebyshev.Chebyshev.fit(points, function(np.sqrt(points)), terms - 1, domain=[0, top])
    return [float(c) for c in series.convert(kind=np.polynomial.Polynomial).coef]


SINE = fitted(lambda a: np.sin(a) / a, 5)
COSINE = fitted(np.cos, 6)
RESTART = 16
LOG2_E = math.log2(math.e)


def modal_rows(residues, decays, seeds, blocks):
    rates = decays * -LOG2_E
    turns = seeds.astype(F32) * (1.0 / PERIOD)
    weights = residues * jnp.sqrt(decays + 1.0 / (blocks * LANES))
    leap = jnp.exp2(rates * LANES)
    c, s = unit_turn(turns * LANES)
    rows = [rates, turns, leap * c, leap * s, 2.0 * (leap * c), leap * leap]
    for start in range(0, blocks, RESTART):
        fall = weights * jnp.exp2(rates * (LANES * start))
        c, s = unit_turn(turns * (LANES * start))
        rows += [fall * c, fall * s]
    return rows


def filter_tile(row, time, blocks, modes):
    total = [None] * blocks
    for mode in range(modes):
        rate, turns, jump_re, jump_im, ahead, behind = (row(i, mode) for i in range(6))
        c, s = unit_turn(turns * time)
        fall = jnp.exp2(rate * time)
        re, im = fall * c, fall * s
        for first in range(0, blocks, RESTART):
            place = 6 + 2 * (first // RESTART)
            if first == 0:
                weight = row(place, mode)
                a, b = weight * re, weight * im
            else:
                start_re, start_im = row(place, mode), row(place + 1, mode)
                a, b = start_re * re - start_im * im, start_re * im + start_im * re
            old, new = a, jump_re * a - jump_im * b
            for block in range(first, min(first + RESTART, blocks)):
                total[block] = plus(total[block], old)
                old, new = new, ahead * new - behind * old
    return total


GAIN_SIDE = 9
SIDES = 10
UNROLLED = 32


def over_slots(count, step):
    if count <= UNROLLED:
        for k in range(count):
            step(k)
    else:
        pl.loop(0, count)(step)


def encode_kernel(value_ref, out_ref):
    height = value_ref.shape[2]
    for i in range(value_ref.shape[1]):
        words, code = pack_pair(value_ref[0, i], value_ref[1, i])
        out_ref[i, :height, :] = words
        out_ref[i, height:, :] = code


def decode_kernel(words_ref, out_ref):
    height = out_ref.shape[2]
    for i in range(out_ref.shape[1]):
        upper, lower = unpack_pair(words_ref[i, :height, :], words_ref[i, height : height + 1, :])
        out_ref[0, i] = upper
        out_ref[1, i] = lower


def encode(value, blocks):
    half = value.shape[0] // 2 // blocks
    some = blocks // 2
    return pl.pallas_call(
        encode_kernel,
        grid=(blocks // some,),
        in_specs=[pl.BlockSpec((2, some, half, LANES), lambda i: (0, i, 0, 0))],
        out_specs=pl.BlockSpec((some, half + SUBLANES, LANES), lambda i: (i, 0, 0)),
        out_shape=jax.ShapeDtypeStruct((blocks, half + SUBLANES, LANES), jnp.int32),
        cost_estimate=takes(2),
        name="encode_cotangent",
    )(value.reshape(2, blocks, half, LANES))


def decode(words, blocks):
    half = words.shape[1] - SUBLANES
    some = blocks // 4
    out = pl.pallas_call(
        decode_kernel,
        grid=(blocks // some,),
        in_specs=[pl.BlockSpec((some, half + SUBLANES, LANES), lambda i: (i, 0, 0))],
        out_specs=pl.BlockSpec((2, some, half, LANES), lambda i: (0, i, 0, 0)),
        out_shape=jax.ShapeDtypeStruct((2, blocks, half, LANES), F32),
        cost_estimate=takes(2),
        name="decode_mixer",
    )(words)
    return out.reshape(2 * blocks * half, LANES)


def takes(microseconds):
    return pl.CostEstimate(flops=int(microseconds * 1e9), bytes_accessed=int(microseconds * 3e6), transcendentals=0)


def pack_table_kernel(mine_ref, other_ref, out_ref):
    total = mine_ref[...] + other_ref[...]
    half = total.shape[0] // 2
    words, code = pack_pair(total[:half], total[half:])
    out_ref[:half, :] = words
    out_ref[half:, :] = code


def unpack_table_kernel(words_ref, out_ref):
    half = out_ref.shape[0] // 2
    upper, lower = unpack_pair(words_ref[0, :half, :], words_ref[0, half : half + 1, :])
    out_ref[:half, :] = upper
    out_ref[half:, :] = lower


def unpack_square_kernel(place_ref, *refs):
    *pair_refs, out_ref, table_ref, sems = refs
    half = out_ref.shape[0] // 2
    copies = []
    for index, ref in enumerate(pair_refs):
        for i in range(2):
            away = 4 * (2 * (index // 4) + i) + index % 4
            upper, lower = unpack_pair(ref[i, :half, :], ref[i, half : half + 1, :])
            table_ref[away, :half, :] = upper
            table_ref[away, half:, :] = lower
            place = pl.ds(pl.multiple_of((place_ref[0] ^ away) * LANES, LANES), LANES)
            copies.append(pltpu.make_async_copy(table_ref.at[away], out_ref.at[:, place], sems.at[away]))
            copies[-1].start()
    for copy in copies:
        copy.wait()


def one_hot_block(token_ref, block, vocab):
    wanted = token_ref[block : block + 1, :]
    entry = lax.broadcasted_iota(jnp.int32, (vocab, LANES), 0)
    return (entry == wanted).astype(F32).astype(BF16)


def filter_kernel(
    _,
    tap_ref, tap_next_ref, gain_ref, gain_next_ref, residue_ref, residue_next_ref, decay_ref, decay_next_ref, seed_ref, seed_next_ref,
    ahead_ref, twist_ref,
    response_out, side_out,
    work_ref, response_ref, mode_ref, taken_ref, time_ref, side_ref, sems,
):
    slots, channels, _ = response_ref.shape
    blocks = slots - 1
    half = channels // 2
    modes = residue_ref.shape[0]
    sides = []
    for index, (taps, gain, residues, decays, seeds) in enumerate((
        (tap_ref, gain_ref, residue_ref, decay_ref, seed_ref),
        (tap_next_ref, gain_next_ref, residue_next_ref, decay_next_ref, seed_next_ref),
    )):
        for i, rows in enumerate(modal_rows(residues[...], decays[...], seeds[...], blocks)):
            mode_ref[index, i] = rows
        listed = jnp.concatenate([taps[0], taps[1], taps[2], gain[...]], axis=0)
        sides.append(jnp.pad(listed, ((0, LANES - listed.shape[0]), (0, 0))).T)
    sides = jnp.concatenate(sides, axis=0)
    for i in range(SIDES):
        side_ref[i] = jnp.broadcast_to(column(sides, i), (channels, LANES))
    side_copy = pltpu.make_async_copy(side_ref, side_out, sems.at[slots])
    side_copy.start()

    for index in range(2):

        def tile(number, carry):
            first = pl.multiple_of(number * SUBLANES, SUBLANES)
            time = (lax.broadcasted_iota(jnp.int32, (SUBLANES, half), 0) + first).astype(F32)
            taken = filter_tile(lambda i, mode: mode_ref[index, i, mode : mode + 1, :], time, blocks, modes)
            for block in range(blocks):
                taken_ref[index, block, pl.ds(first, SUBLANES), :] = taken[block]
            return carry

        lax.fori_loop(0, LANES // SUBLANES, tile, 0, unroll=2)

    for index in range(2):
        for block in range(blocks):
            time_ref[block, index * half : (index + 1) * half, :] = taken_ref[index, block].T

    def transforms(rows):
        store_spectrum(work_ref, rows, padded_real_dft([time_ref[block, rows, :] for block in range(blocks)]))

    for_tiles(channels, 4, transforms)

    def step(k):
        response_ref[k] = inner_ahead(work_ref[k], twist_ref[k], ahead_ref[...])
        pltpu.make_async_copy(response_ref.at[k], response_out.at[k], sems.at[k]).start()

    over_slots(slots, step)

    @pl.loop(0, slots)
    def _(k):
        pltpu.make_async_copy(response_ref.at[k], response_out.at[k], sems.at[k]).wait()

    side_copy.wait()


def filtered(work_ref, response_ref, ahead_ref, back_ref, twist_ref, sign):
    def step(k):
        twist = twist_ref[k]
        spectrum = inner_ahead(work_ref[k], twist, ahead_ref[...])
        a, b = response_ref[k, :, :LANES], response_ref[k, :, LANES:] * sign
        c, d = spectrum[:, :LANES], spectrum[:, LANES:]
        product = jnp.concatenate([a * c - b * d, a * d + b * c], axis=1)
        work_ref[k] = inner_back(product, twist, back_ref[...])

    over_slots(work_ref.shape[0], step)


def forward_kernel(
    place_ref, own_ref, other_ref, token_ref, side_ref, *refs
):
    held, (words_out_ref, long_out_ref, stream_out_ref), refs = refs[:4], refs[4:7], refs[7:]
    response_ref, ahead_ref, back_ref, twist_ref, words_ref, long_ref, stream_ref, x_ref, work_ref, sems, word_sems = refs
    tables = [pltpu.make_async_copy(held[i], refs[i], sems.at[i]) for i in range(4)]
    stream_copy = pltpu.make_async_copy(stream_ref, stream_out_ref, sems.at[4])
    long_copy = pltpu.make_async_copy(long_ref, long_out_ref, sems.at[5])
    for copy in tables:
        copy.start()
    blocks, channels, _ = x_ref.shape
    half = channels // 2
    vocab = own_ref.shape[0]
    own, other = own_ref[...].astype(F32).T, other_ref[...].astype(F32).T
    first = place_ref[1] == 0
    tall = jnp.concatenate([jnp.where(first, own, other), jnp.where(first, other, own)], axis=0).astype(BF16)

    for pair in range(blocks // 2):
        hot = jnp.concatenate([one_hot_block(token_ref, 2 * pair + i, vocab) for i in range(2)], axis=1)
        found = jnp.dot(tall, hot, preferred_element_type=F32)
        x_ref[2 * pair] = found[:, :LANES]
        x_ref[2 * pair + 1] = found[:, LANES:]

    def streams(rows):
        lane = lax.broadcasted_iota(jnp.int32, (SUBLANES, LANES), 1)
        taps = wide_taps(side_ref, rows)
        mixed = []
        for block, terms in shifted_blocks(x_ref, rows, blocks, lane):
            query, key, value = (mix(taps, stream, terms) for stream in range(3))
            stream_ref[0, block, rows, :] = query
            stream_ref[1, block, rows, :] = key
            stream_ref[2, block, rows, :] = value
            mixed.append(key * value)
        store_spectrum(work_ref, rows, padded_real_dft(mixed))

    for_tiles(channels, 4, streams)
    stream_copy.start()
    for copy in tables:
        copy.wait()
    filtered(work_ref, response_ref, ahead_ref, back_ref, twist_ref, 1.0)

    def results(rows):
        conv = padded_real_back(load_spectrum(work_ref, rows, blocks + 1))
        gain = side_ref[GAIN_SIDE, rows, :]
        for block in range(blocks):
            long_out = conv[block] + gain * (stream_ref[1, block, rows, :] * stream_ref[2, block, rows, :])
            long_ref[block, rows, :] = long_out
            x_ref[block, rows, :] = stream_ref[0, block, rows, :] * long_out

    for_tiles(channels, 2, results)
    long_copy.start()

    def words_copy(block):
        return pltpu.make_async_copy(words_ref.at[block], words_out_ref.at[block], word_sems.at[block])

    for block in range(blocks):
        words, code = pack_pair(x_ref[block, :half, :], x_ref[block, half:, :])
        words_ref[block, :half, :] = words
        words_ref[block, half:, :] = code
        words_copy(block).start()
    for block in range(blocks):
        words_copy(block).wait()
    stream_copy.wait()
    long_copy.wait()


def backward_kernel(
    place_ref, words_ref, token_ref, side_ref, *refs
):
    held, (mine_ref, theirs_ref), refs = refs[:6], refs[6:8], refs[8:]
    stream_ref, response_ref, ahead_ref, back_ref, twist_ref, long_ref, work_ref, cot_ref, late_ref, sems = refs
    copies = [pltpu.make_async_copy(held[i], refs[i], sems.at[i]) for i in range(6)]
    for copy in copies:
        copy.start()
    blocks, channels, _ = cot_ref.shape
    half = channels // 2
    vocab = mine_ref.shape[0]

    for block in range(blocks):
        upper, lower = unpack_pair(words_ref[block, :half, :], words_ref[block, half : half + 1, :])
        cot_ref[block, :half, :] = upper
        cot_ref[block, half:, :] = lower
    copies[0].wait()

    def streams(rows):
        late = [cot_ref[block, rows, :] * stream_ref[0, block, rows, :] for block in range(blocks)]
        store_spectrum(work_ref, rows, padded_real_dft(late))

    for_tiles(channels, 4, streams)
    for copy in copies[1:]:
        copy.wait()
    filtered(work_ref, response_ref, ahead_ref, back_ref, twist_ref, -1.0)

    def results(rows):
        lane = lax.broadcasted_iota(jnp.int32, (SUBLANES, LANES), 1)
        taps = wide_taps(side_ref, rows)
        gain = side_ref[GAIN_SIDE, rows, :]
        correlated = padded_real_back(load_spectrum(work_ref, rows, blocks + 1))
        before = None
        for block in range(blocks):
            query, key, value = (stream_ref[stream, block, rows, :] for stream in range(3))
            cot = cot_ref[block, rows, :]
            mixed_grad = correlated[block] + gain * (cot * query)
            grads = (cot * long_ref[block, rows, :], mixed_grad * value, mixed_grad * key)
            now, next_one, next_two = (sum(taps[3 * s + j] * grads[s] for s in range(3)) for j in range(3))
            next_one = pltpu.roll(next_one, LANES - 1, 1)
            next_two = pltpu.roll(next_two, LANES - 2, 1)
            if before is not None:
                base, one, two = before
                late_ref[block - 1, rows, :] = (
                    base + jnp.where(lane < LANES - 1, one, next_one) + jnp.where(lane < LANES - 2, two, next_two)
                )
            before = (now, next_one, next_two)
        base, one, two = before
        late_ref[blocks - 1, rows, :] = (
            base + jnp.where(lane < LANES - 1, one, 0.0) + jnp.where(lane < LANES - 2, two, 0.0)
        )

    for_tiles(channels, 2, results)

    total = None
    for start in range(0, blocks, 4):
        some = range(start, start + 4)
        hot = jnp.concatenate([one_hot_block(token_ref, block, vocab) for block in some], axis=1)
        value = jnp.concatenate([late_ref[block] for block in some], axis=1)
        high = value.astype(BF16)
        low = (value - high.astype(F32)).astype(BF16)
        part = lax.dot_general(
            jnp.concatenate([hot, hot], axis=1),
            jnp.concatenate([high, low], axis=1),
            (((1,), (1,)), ((), ())),
            preferred_element_type=F32,
        )
        total = plus(total, part)
    first = place_ref[1] == 0
    mine_ref[...] = jnp.where(first, total[:, :half], total[:, half:])
    theirs_ref[...] = jnp.where(first, total[:, half:], total[:, :half])


def anywhere(count):
    return [pl.BlockSpec(memory_space=pl.ANY)] * count


def in_vmem(count):
    return [pl.BlockSpec(memory_space=pltpu.VMEM)] * count


def gather_square(value):
    def swap(part, bits):
        return lax.ppermute(part, "ctx", [(i, i ^ bits) for i in range(16)])

    near = jnp.stack([value, swap(value, 4)])
    far = jnp.stack([swap(value, 8), swap(value, 12)])
    near_beside, far_below = swap(near, 1), swap(far, 2)
    near_below, far_beside = swap(near, 2), swap(far, 1)
    return near, near_beside, near_below, swap(near_beside, 2), far, far_beside, far_below, swap(far_below, 1)


def body(token_ids, embedding, conv_taps, residues, decays, filter_seed, skip_gain, cotangent):
    blocks = lax.axis_size("ctx")
    rank = lax.axis_index("ctx")
    side = lax.axis_index("fsdp")
    width = conv_taps.shape[2]
    vocab = embedding.shape[0]
    half = width // 2 // blocks
    channels = 2 * half
    modes = residues.shape[1]
    slots = blocks + 1
    place = jnp.stack([rank, side]).astype(jnp.int32)
    other_core = [(0, 1), (1, 0)]

    def exchange(value):
        return lax.all_to_all(value, "ctx", split_axis=0, concat_axis=0, tiled=True)

    tokens = exchange(jnp.broadcast_to(token_ids, (blocks, LANES)))
    cot_words = exchange(encode(cotangent[0], blocks))
    own_columns = lax.dynamic_slice_in_dim(embedding, rank * half, half, 1)
    other_columns = lax.ppermute(own_columns, "fsdp", other_core)

    ahead, back, twist = transform_tables(blocks)
    spectra = (slots, channels, 2 * LANES)
    work = pltpu.VMEM(spectra, F32)
    buffer = pltpu.VMEM((blocks, channels, LANES), F32)
    tables = [work, pltpu.VMEM(ahead.shape, BF16), pltpu.VMEM(back.shape, BF16), pltpu.VMEM(twist.shape, F32)]

    def halves(value):
        lead = value.shape[:-1]
        zeros = (0,) * len(lead)
        if half % LANES == 0:
            return [value, value], [
                pl.BlockSpec((*lead, half), lambda i, at: (*zeros, at[0])),
                pl.BlockSpec((*lead, half), lambda i, at: (*zeros, blocks + at[0])),
            ]
        parts = [
            lax.dynamic_slice_in_dim(value, start + rank * half, half, len(lead)) for start in (0, width // 2)
        ]
        return parts, [pl.BlockSpec((*lead, half), lambda i, at: (*zeros, 0))] * 2

    listed = [halves(v) for v in (conv_taps, skip_gain[None], residues.T, decays.T, filter_seed.T)]
    response, sides = pl.pallas_call(
        filter_kernel,
        grid_spec=pltpu.PrefetchScalarGridSpec(
            num_scalar_prefetch=1,
            grid=(1,),
            in_specs=[spec for _, specs in listed for spec in specs] + in_vmem(2),
            out_specs=tuple(anywhere(2)),
            scratch_shapes=[
                work,
                work,
                pltpu.VMEM((2, 6 + 2 * (-(-blocks // RESTART)), modes, half), F32),
                pltpu.VMEM((2, blocks, LANES, half), F32),
                buffer,
                pltpu.VMEM((SIDES, channels, LANES), F32),
                pltpu.SemaphoreType.DMA((slots + 1,)),
            ],
        ),
        out_shape=(jax.ShapeDtypeStruct(spectra, F32), jax.ShapeDtypeStruct((SIDES, channels, LANES), F32)),
        compiler_params=pltpu.CompilerParams(vmem_limit_bytes=VMEM_BYTES),
        cost_estimate=takes(15),
        name="modal_filter",
    )(place, *[part for parts, _ in listed for part in parts], ahead, twist)

    scalars = functools.partial(pltpu.PrefetchScalarGridSpec, num_scalar_prefetch=1, grid=(1,))
    mixer_words, long_out, streams = pl.pallas_call(
        forward_kernel,
        grid_spec=scalars(
            in_specs=in_vmem(4) + anywhere(4),
            out_specs=tuple(anywhere(3)),
            scratch_shapes=[
                *tables,
                pltpu.VMEM((blocks, half + SUBLANES, LANES), jnp.int32),
                buffer,
                pltpu.VMEM((3, blocks, channels, LANES), F32),
                buffer,
                work,
                pltpu.SemaphoreType.DMA((6,)),
                pltpu.SemaphoreType.DMA((blocks,)),
            ],
        ),
        out_shape=(
            jax.ShapeDtypeStruct((blocks, half + SUBLANES, LANES), jnp.int32),
            jax.ShapeDtypeStruct((blocks, channels, LANES), F32),
            jax.ShapeDtypeStruct((3, blocks, channels, LANES), F32),
        ),
        compiler_params=pltpu.CompilerParams(vmem_limit_bytes=VMEM_BYTES),
        cost_estimate=takes(14),
        name="forward",
    )(place, own_columns, other_columns, tokens, sides, response, ahead, back, twist)

    mixer_words = exchange(mixer_words)

    mine, theirs = pl.pallas_call(
        backward_kernel,
        grid_spec=scalars(
            in_specs=in_vmem(3) + anywhere(6),
            out_specs=tuple(in_vmem(2)),
            scratch_shapes=[
                pltpu.VMEM((3, blocks, channels, LANES), F32),
                *tables,
                buffer,
                work,
                buffer,
                buffer,
                pltpu.SemaphoreType.DMA((6,)),
            ],
        ),
        out_shape=(jax.ShapeDtypeStruct((vocab, half), F32),) * 2,
        compiler_params=pltpu.CompilerParams(vmem_limit_bytes=VMEM_BYTES),
        cost_estimate=takes(15),
        name="backward",
    )(place, cot_words, tokens, sides, streams, response, ahead, back, twist, long_out)
    theirs = lax.ppermute(theirs, "fsdp", other_core)
    tall = vocab // 2 + SUBLANES
    grad_words = pl.pallas_call(
        pack_table_kernel,
        in_specs=in_vmem(2),
        out_specs=in_vmem(1)[0],
        out_shape=jax.ShapeDtypeStruct((tall, half), jnp.int32),
        cost_estimate=takes(1),
        name="pack_table",
    )(mine, theirs)
    table = jax.ShapeDtypeStruct((vocab, blocks * half), F32)
    if blocks == 16 and half == LANES:
        embed_grad = pl.pallas_call(
            unpack_square_kernel,
            grid_spec=scalars(
                in_specs=in_vmem(8),
                out_specs=anywhere(1)[0],
                scratch_shapes=[pltpu.VMEM((blocks, vocab, half), F32), pltpu.SemaphoreType.DMA((blocks,))],
            ),
            out_shape=table,
            compiler_params=pltpu.CompilerParams(vmem_limit_bytes=16 * 1024 * 1024),
            cost_estimate=takes(3),
            name="unpack_table",
        )(place, *gather_square(grad_words))
    else:
        grad_words = lax.all_gather(grad_words, "ctx", axis=0, tiled=False)
        group = max(1, LANES // half)
        grad_words = grad_words.reshape(blocks // group, group, tall, half)
        grad_words = jnp.swapaxes(grad_words, 1, 2).reshape(blocks // group, tall, group * half)
        embed_grad = pl.pallas_call(
            unpack_table_kernel,
            grid=(blocks // group,),
            in_specs=[pl.BlockSpec((1, tall, group * half), lambda i: (i, 0, 0))],
            out_specs=pl.BlockSpec((vocab, group * half), lambda i: (0, i)),
            out_shape=table,
            cost_estimate=takes(3),
            name="unpack_table",
        )(grad_words)
    return decode(mixer_words, blocks)[None], embed_grad


def solution(mesh):
    placed = (P("fsdp", "ctx"), P(None, "fsdp"), P(), P(), P(), P(), P(), P("fsdp", None, "ctx"))
    return jax.shard_map(
        body,
        mesh=mesh,
        in_specs=placed,
        out_specs=(P("fsdp", None, "ctx"), P(None, "fsdp")),
        check_vma=False,
    )
```

```python
import functools
import math

import jax
import jax.numpy as jnp
import ml_dtypes
import numpy as np
from jax import lax
from jax.experimental import pallas as pl
from jax.experimental.pallas import tpu as pltpu
from jax.sharding import PartitionSpec as P

PERIOD = 4096
LANES = 128
SUBLANES = 8
FULL = 32000.0
TINY = 2.0**-110
CODE = 1024.0
VMEM_BYTES = 60 * 1024 * 1024
F32 = jnp.float32
BF16 = jnp.bfloat16


def pack_pair(upper, lower):
    top = jnp.max(jnp.maximum(jnp.abs(upper), jnp.abs(lower)), axis=0, keepdims=True)
    code = jnp.ceil(jnp.log2(jnp.maximum(top, TINY)) * CODE)
    gain = FULL * jnp.exp2(code * (-1.0 / CODE))
    high = jnp.round(upper * gain).astype(jnp.int32)
    low = jnp.round(lower * gain).astype(jnp.int32)
    words = (high << 16) | (low & 0xFFFF)
    return words, jnp.broadcast_to(code.astype(jnp.int32), (SUBLANES, upper.shape[1]))


def unpack_pair(words, code):
    step = jnp.exp2(code.astype(F32) * (1.0 / CODE)) * (1.0 / FULL)
    return (
        (words >> 16).astype(F32) * step,
        ((words << 16) >> 16).astype(F32) * step,
    )


def plus(a, b):
    return b if a is None else a if b is None else a + b


def minus(a, b):
    return a if b is None else -b if a is None else a - b


def turn(re, im, top, bottom):
    top %= bottom
    if 8 * top % bottom == 0:
        eighth = 8 * top // bottom
        if eighth == 0:
            return re, im
        if eighth == 4:
            return -re, -im
        if eighth == 2:
            return im, -re
        if eighth == 6:
            return -im, re
        half = math.sqrt(0.5)
        if eighth == 1:
            return (re + im) * half, (im - re) * half
        if eighth == 5:
            return (re + im) * -half, (re - im) * half
        if eighth == 3:
            return (im - re) * half, (re + im) * -half
        return (re - im) * half, (re + im) * half
    angle = 2.0 * math.pi * top / bottom
    c, s = math.cos(angle), math.sin(angle)
    return re * c + im * s, im * c - re * s


def complex_dft(points):
    n = len(points)
    if n == 1:
        return points
    even, odd = complex_dft(points[::2]), complex_dft(points[1::2])
    out = [None] * n
    for k in range(n // 2):
        re, im = turn(*odd[k], k, n)
        out[k] = (even[k][0] + re, even[k][1] + im)
        out[k + n // 2] = (even[k][0] - re, even[k][1] - im)
    return out


def odd_part(diff, n):
    quarter = n // 4
    return complex_dft([turn(diff[s], -diff[s + quarter], s, n) for s in range(quarter)])


def place_odd(out, odd, n):
    for index, (re, im) in enumerate(odd):
        k = 4 * index + 1
        if k <= n // 2:
            out[k] = (re, im)
        else:
            out[n - k] = (re, -im)


def real_dft(x):
    n = len(x)
    if n == 1:
        return [(x[0], None)]
    if n == 2:
        return [(x[0] + x[1], None), (x[0] - x[1], None)]
    half = n // 2
    out = [None] * (half + 1)
    out[::2] = real_dft([x[s] + x[s + half] for s in range(half)])
    place_odd(out, odd_part([x[s] - x[s + half] for s in range(half)], n), n)
    return out


def padded_real_dft(x):
    n = 2 * len(x)
    out = [None] * (len(x) + 1)
    out[::2] = real_dft(x)
    place_odd(out, odd_part(x, n), n)
    return out


def odd_back(spectrum, n):
    quarter = n // 4
    points = []
    for index in range(quarter):
        k = 4 * index + 1
        re, im = spectrum[k] if k <= n // 2 else spectrum[n - k]
        points.append((im if k <= n // 2 else -im, re))
    waves = [(re, im) for im, re in complex_dft(points)]
    first, second = [], []
    for s, (re, im) in enumerate(waves):
        im, re = turn(im, re, s, n)
        first.append(re)
        second.append(-im)
    return first + second


def real_back(spectrum):
    n = 2 * (len(spectrum) - 1)
    if n == 2:
        a, b = spectrum[0][0], spectrum[1][0]
        return [a + b, a - b]
    even = real_back(spectrum[::2])
    odd = odd_back(spectrum, n)
    return [a + b for a, b in zip(even, odd)] + [a - b for a, b in zip(even, odd)]


def padded_real_back(spectrum):
    n = 2 * (len(spectrum) - 1)
    even = real_back(spectrum[::2])
    return [a + b for a, b in zip(even, odd_back(spectrum, n))]


def stacked(matrix):
    high = matrix.astype(ml_dtypes.bfloat16)
    low = (matrix - high.astype(np.float64)).astype(ml_dtypes.bfloat16)
    return np.concatenate([high, high, low], axis=0)


def transform_tables(blocks):
    total = 2 * blocks * LANES
    inner = np.arange(LANES)[:, None] * np.arange(LANES)[None, :] % LANES
    angle = 2.0 * np.pi / LANES * inner
    c, s = np.cos(angle), np.sin(angle)
    ahead = np.block([[c, -s], [s, c]])
    back = np.block([[c, s], [-s, c]]) * (2.0 / total)
    turns = np.arange(blocks + 1)[:, None] * np.arange(LANES)[None, :] % total
    angle = 2.0 * np.pi / total * turns
    weight = np.ones((blocks + 1, 1))
    weight[0] = weight[-1] = 0.5
    twist = np.stack([np.cos(angle), np.sin(angle), np.cos(angle) * weight, np.sin(angle) * weight], axis=1)
    return (
        jnp.asarray(stacked(ahead)),
        jnp.asarray(stacked(back)),
        jnp.asarray(np.pad(twist, ((0, 0), (0, 4), (0, 0))), F32),
    )


def split_dot(value, table):
    high = value.astype(BF16)
    low = (value - high.astype(F32)).astype(BF16)
    return jnp.dot(jnp.concatenate([high, low, high], axis=1), table, preferred_element_type=F32)


def inner_ahead(value, twist, table):
    re, im = value[:, :LANES], value[:, LANES:]
    c, s = twist[0:1], twist[1:2]
    turned = jnp.concatenate([re * c + im * s, im * c - re * s], axis=1)
    return split_dot(turned, table)


def inner_back(value, twist, table):
    out = split_dot(value, table)
    re, im = out[:, :LANES], out[:, LANES:]
    c, s = twist[2:3], twist[3:4]
    return jnp.concatenate([re * c - im * s, im * c + re * s], axis=1)


def store_spectrum(ref, rows, spectrum):
    for k, (re, im) in enumerate(spectrum):
        ref[k, rows, :LANES] = re
        ref[k, rows, LANES:] = jnp.zeros_like(re) if im is None else im


def load_spectrum(ref, rows, count):
    return [(ref[k, rows, :LANES], ref[k, rows, LANES:]) for k in range(count)]


def later(previous, current, steps, lane):
    moved = pltpu.roll(current, steps, 1)
    if previous is None:
        return jnp.where(lane < steps, 0.0, moved), moved
    return jnp.where(lane < steps, previous, moved), moved


def earlier(following, current, steps, lane):
    moved = pltpu.roll(current, LANES - steps, 1)
    kept = lane < LANES - steps
    if following is None:
        return jnp.where(kept, moved, 0.0), moved
    return jnp.where(kept, moved, following), moved


def shifted_blocks(x_ref, rows, blocks, lane):
    one = two = None
    for block in range(blocks):
        x = x_ref[block, rows, :]
        back_one, one = later(one, x, 1, lane)
        back_two, two = later(two, x, 2, lane)
        yield block, (x, back_one, back_two)


def column(values, index):
    return values[:, index : index + 1]


def mix(taps, stream, terms):
    return sum(taps[3 * stream + j] * terms[j] for j in range(3))


def wide_taps(ref, rows):
    return [ref[i, rows, :] for i in range(9)]


def for_tiles(channels, unroll, step):
    def run(tile, carry):
        step(pl.ds(pl.multiple_of(tile * SUBLANES, SUBLANES), SUBLANES))
        return carry

    lax.fori_loop(0, channels // SUBLANES, run, 0, unroll=unroll)


def unit_turn(turns):
    angle = (turns - jnp.round(turns)) * math.pi
    square = angle * angle
    sin, cos = SINE[-1], COSINE[-1]
    for coefficient in SINE[-2::-1]:
        sin = sin * square + coefficient
    for coefficient in COSINE[-2::-1]:
        cos = cos * square + coefficient
    sin = sin * angle
    twice = sin + sin
    return 1.0 - twice * sin, twice * cos


def fitted(function, terms):
    top = (math.pi / 2) ** 2
    points = top / 2 * (1 + np.cos(np.pi * (np.arange(64) + 0.5) / 64))
    series = np.polynomial.chebyshev.Chebyshev.fit(points, function(np.sqrt(points)), terms - 1, domain=[0, top])
    return [float(c) for c in series.convert(kind=np.polynomial.Polynomial).coef]


SINE = fitted(lambda a: np.sin(a) / a, 5)
COSINE = fitted(np.cos, 6)
RESTART = 16
LOG2_E = math.log2(math.e)


def modal_rows(residues, decays, seeds, blocks):
    rates = decays * -LOG2_E
    turns = seeds.astype(F32) * (1.0 / PERIOD)
    weights = residues * jnp.sqrt(decays + 1.0 / (blocks * LANES))
    leap = jnp.exp2(rates * LANES)
    c, s = unit_turn(turns * LANES)
    rows = [rates, turns, leap * c, leap * s, 2.0 * (leap * c), leap * leap]
    for start in range(0, blocks, RESTART):
        fall = weights * jnp.exp2(rates * (LANES * start))
        c, s = unit_turn(turns * (LANES * start))
        rows += [fall * c, fall * s]
    return rows


def filter_tile(row, time, blocks, modes):
    total = [None] * blocks
    for mode in range(modes):
        rate, turns, jump_re, jump_im, ahead, behind = (row(i, mode) for i in range(6))
        c, s = unit_turn(turns * time)
        fall = jnp.exp2(rate * time)
        re, im = fall * c, fall * s
        for first in range(0, blocks, RESTART):
            place = 6 + 2 * (first // RESTART)
            if first == 0:
                weight = row(place, mode)
                a, b = weight * re, weight * im
            else:
                start_re, start_im = row(place, mode), row(place + 1, mode)
                a, b = start_re * re - start_im * im, start_re * im + start_im * re
            old, new = a, jump_re * a - jump_im * b
            for block in range(first, min(first + RESTART, blocks)):
                total[block] = plus(total[block], old)
                old, new = new, ahead * new - behind * old
    return total


GAIN_SIDE = 9
SIDES = 10
UNROLLED = 32


def over_slots(count, step):
    if count <= UNROLLED:
        for k in range(count):
            step(k)
    else:
        pl.loop(0, count)(step)


def encode_kernel(value_ref, out_ref):
    height = value_ref.shape[2]
    for i in range(value_ref.shape[1]):
        words, code = pack_pair(value_ref[0, i], value_ref[1, i])
        out_ref[i, :height, :] = words
        out_ref[i, height:, :] = code


def decode_kernel(words_ref, out_ref):
    height = out_ref.shape[2]
    for i in range(out_ref.shape[1]):
        upper, lower = unpack_pair(words_ref[i, :height, :], words_ref[i, height : height + 1, :])
        out_ref[0, i] = upper
        out_ref[1, i] = lower


def encode(value, blocks):
    half = value.shape[0] // 2 // blocks
    some = blocks // 2
    return pl.pallas_call(
        encode_kernel,
        grid=(blocks // some,),
        in_specs=[pl.BlockSpec((2, some, half, LANES), lambda i: (0, i, 0, 0))],
        out_specs=pl.BlockSpec((some, half + SUBLANES, LANES), lambda i: (i, 0, 0)),
        out_shape=jax.ShapeDtypeStruct((blocks, half + SUBLANES, LANES), jnp.int32),
        cost_estimate=takes(2),
        name="encode_cotangent",
    )(value.reshape(2, blocks, half, LANES))


def decode(words, blocks):
    half = words.shape[1] - SUBLANES
    some = blocks // 4
    out = pl.pallas_call(
        decode_kernel,
        grid=(blocks // some,),
        in_specs=[pl.BlockSpec((some, half + SUBLANES, LANES), lambda i: (i, 0, 0))],
        out_specs=pl.BlockSpec((2, some, half, LANES), lambda i: (0, i, 0, 0)),
        out_shape=jax.ShapeDtypeStruct((2, blocks, half, LANES), F32),
        cost_estimate=takes(2),
        name="decode_mixer",
    )(words)
    return out.reshape(2 * blocks * half, LANES)


def takes(microseconds):
    return pl.CostEstimate(flops=int(microseconds * 1e9), bytes_accessed=int(microseconds * 3e6), transcendentals=0)


def pack_table_kernel(mine_ref, other_ref, out_ref):
    total = mine_ref[...] + other_ref[...]
    half = total.shape[0] // 2
    words, code = pack_pair(total[:half], total[half:])
    out_ref[:half, :] = words
    out_ref[half:, :] = code


def unpack_table_kernel(words_ref, out_ref):
    half = out_ref.shape[0] // 2
    upper, lower = unpack_pair(words_ref[0, :half, :], words_ref[0, half : half + 1, :])
    out_ref[:half, :] = upper
    out_ref[half:, :] = lower


def unpack_square_kernel(aways, place_ref, *refs):
    part_refs, (out_ref, table_ref, sems) = refs[: len(aways)], refs[-3:]
    half = out_ref.shape[0] // 2
    copies = []
    for slot, (ref, away) in enumerate(zip(part_refs, aways)):
        upper, lower = unpack_pair(ref[:half, :], ref[half : half + 1, :])
        table_ref[slot, :half, :] = upper
        table_ref[slot, half:, :] = lower
        place = pl.ds(pl.multiple_of((place_ref[0] ^ away) * LANES, LANES), LANES)
        copies.append(pltpu.make_async_copy(table_ref.at[slot], out_ref.at[:, place], sems.at[slot]))
        copies[-1].start()
    for copy in copies:
        copy.wait()


def fill_table(held, parts, aways, place, vocab, width):
    count = len(aways)
    return pl.pallas_call(
        functools.partial(unpack_square_kernel, aways),
        grid_spec=pltpu.PrefetchScalarGridSpec(
            num_scalar_prefetch=1,
            grid=(1,),
            in_specs=in_vmem(len(parts)) + anywhere(len(held)),
            out_specs=anywhere(1)[0],
            scratch_shapes=[pltpu.VMEM((count, vocab, LANES), F32), pltpu.SemaphoreType.DMA((count,))],
        ),
        out_shape=jax.ShapeDtypeStruct((vocab, width), F32),
        input_output_aliases={len(parts) + 1: 0} if held else {},
        compiler_params=pltpu.CompilerParams(vmem_limit_bytes=16 * 1024 * 1024),
        cost_estimate=takes(2.5 if count > 4 else 1.5),
        name="unpack_table",
    )(place, *parts, *held)


def hold_tokens(refs, token_ref):
    count = refs[0].shape[0]
    for index, ref in enumerate(refs):
        token_ref[index * count : (index + 1) * count, :] = ref[...]


def token_row(block, place_ref, pieces):
    if pieces == 1:
        return block
    away = place_ref[0] ^ block
    return 4 * (away & 3) + (away >> 2)


def one_hot_block(token_ref, block, vocab):
    wanted = token_ref[pl.ds(block, 1), :]
    entry = lax.broadcasted_iota(jnp.int32, (vocab, LANES), 0)
    return (entry == wanted).astype(F32).astype(BF16)


def filter_kernel(
    _,
    tap_ref, tap_next_ref, gain_ref, gain_next_ref, residue_ref, residue_next_ref, decay_ref, decay_next_ref, seed_ref, seed_next_ref,
    ahead_ref, twist_ref,
    response_out, side_out,
    work_ref, response_ref, mode_ref, taken_ref, time_ref, side_ref, sems,
):
    slots, channels, _ = response_ref.shape
    blocks = slots - 1
    half = channels // 2
    modes = residue_ref.shape[0]
    sides = []
    for index, (taps, gain, residues, decays, seeds) in enumerate((
        (tap_ref, gain_ref, residue_ref, decay_ref, seed_ref),
        (tap_next_ref, gain_next_ref, residue_next_ref, decay_next_ref, seed_next_ref),
    )):
        for i, rows in enumerate(modal_rows(residues[...], decays[...], seeds[...], blocks)):
            mode_ref[index, i] = rows
        listed = jnp.concatenate([taps[0], taps[1], taps[2], gain[...]], axis=0)
        sides.append(jnp.pad(listed, ((0, LANES - listed.shape[0]), (0, 0))).T)
    sides = jnp.concatenate(sides, axis=0)
    for i in range(SIDES):
        side_ref[i] = jnp.broadcast_to(column(sides, i), (channels, LANES))
    side_copy = pltpu.make_async_copy(side_ref, side_out, sems.at[slots])
    side_copy.start()

    for index in range(2):

        def tile(number, carry):
            first = pl.multiple_of(number * SUBLANES, SUBLANES)
            time = (lax.broadcasted_iota(jnp.int32, (SUBLANES, half), 0) + first).astype(F32)
            taken = filter_tile(lambda i, mode: mode_ref[index, i, mode : mode + 1, :], time, blocks, modes)
            for block in range(blocks):
                taken_ref[index, block, pl.ds(first, SUBLANES), :] = taken[block]
            return carry

        lax.fori_loop(0, LANES // SUBLANES, tile, 0, unroll=2)

    for index in range(2):
        for block in range(blocks):
            time_ref[block, index * half : (index + 1) * half, :] = taken_ref[index, block].T

    def transforms(rows):
        store_spectrum(work_ref, rows, padded_real_dft([time_ref[block, rows, :] for block in range(blocks)]))

    for_tiles(channels, 4, transforms)

    def step(k):
        response_ref[k] = inner_ahead(work_ref[k], twist_ref[k], ahead_ref[...])
        pltpu.make_async_copy(response_ref.at[k], response_out.at[k], sems.at[k]).start()

    over_slots(slots, step)

    @pl.loop(0, slots)
    def _(k):
        pltpu.make_async_copy(response_ref.at[k], response_out.at[k], sems.at[k]).wait()

    side_copy.wait()


def filtered(work_ref, response_ref, ahead_ref, back_ref, twist_ref, sign):
    def step(k):
        twist = twist_ref[k]
        spectrum = inner_ahead(work_ref[k], twist, ahead_ref[...])
        a, b = response_ref[k, :, :LANES], response_ref[k, :, LANES:] * sign
        c, d = spectrum[:, :LANES], spectrum[:, LANES:]
        product = jnp.concatenate([a * c - b * d, a * d + b * c], axis=1)
        work_ref[k] = inner_back(product, twist, back_ref[...])

    over_slots(work_ref.shape[0], step)


def forward_kernel(pieces, place_ref, own_ref, other_ref, *refs):
    token_refs, token_ref, refs = refs[:pieces], refs[-1], refs[pieces:-1]
    hold_tokens(token_refs, token_ref)
    held, (words_out_ref, long_out_ref, stream_out_ref), refs = refs[:5], refs[5:8], refs[8:]
    side_ref, response_ref, ahead_ref, back_ref, twist_ref, words_ref, long_ref, stream_ref, x_ref, work_ref, sems, word_sems = refs
    side_copy, *tables = [pltpu.make_async_copy(held[i], refs[i], sems.at[i]) for i in range(5)]
    stream_copy = pltpu.make_async_copy(stream_ref, stream_out_ref, sems.at[5])
    long_copy = pltpu.make_async_copy(long_ref, long_out_ref, sems.at[6])
    side_copy.start()
    for copy in tables:
        copy.start()
    blocks, channels, _ = x_ref.shape
    half = channels // 2
    vocab = own_ref.shape[0]
    own, other = own_ref[...].astype(F32).T, other_ref[...].astype(F32).T
    first = place_ref[1] == 0
    tall = jnp.concatenate([jnp.where(first, own, other), jnp.where(first, other, own)], axis=0).astype(BF16)

    for pair in range(blocks // 2):
        hot = jnp.concatenate([one_hot_block(token_ref, token_row(2 * pair + i, place_ref, pieces), vocab) for i in range(2)], axis=1)
        found = jnp.dot(tall, hot, preferred_element_type=F32)
        x_ref[2 * pair] = found[:, :LANES]
        x_ref[2 * pair + 1] = found[:, LANES:]
    side_copy.wait()

    def streams(rows):
        lane = lax.broadcasted_iota(jnp.int32, (SUBLANES, LANES), 1)
        taps = wide_taps(side_ref, rows)
        mixed = []
        for block, terms in shifted_blocks(x_ref, rows, blocks, lane):
            query, key, value = (mix(taps, stream, terms) for stream in range(3))
            stream_ref[0, block, rows, :] = query
            stream_ref[1, block, rows, :] = key
            stream_ref[2, block, rows, :] = value
            mixed.append(key * value)
        store_spectrum(work_ref, rows, padded_real_dft(mixed))

    for_tiles(channels, 4, streams)
    stream_copy.start()
    for copy in tables:
        copy.wait()
    filtered(work_ref, response_ref, ahead_ref, back_ref, twist_ref, 1.0)

    def results(rows):
        conv = padded_real_back(load_spectrum(work_ref, rows, blocks + 1))
        gain = side_ref[GAIN_SIDE, rows, :]
        for block in range(blocks):
            long_out = conv[block] + gain * (stream_ref[1, block, rows, :] * stream_ref[2, block, rows, :])
            long_ref[block, rows, :] = long_out
            x_ref[block, rows, :] = stream_ref[0, block, rows, :] * long_out

    for_tiles(channels, 2, results)
    long_copy.start()

    def words_copy(block):
        return pltpu.make_async_copy(words_ref.at[block], words_out_ref.at[block], word_sems.at[block])

    for block in range(blocks):
        words, code = pack_pair(x_ref[block, :half, :], x_ref[block, half:, :])
        words_ref[block, :half, :] = words
        words_ref[block, half:, :] = code
        words_copy(block).start()
    for block in range(blocks):
        words_copy(block).wait()
    stream_copy.wait()
    long_copy.wait()


def backward_kernel(pieces, place_ref, words_ref, *refs):
    token_refs, token_ref, refs = refs[:pieces], refs[-1], refs[pieces:-1]
    hold_tokens(token_refs, token_ref)
    held, (mine_ref, theirs_ref), refs = refs[:7], refs[7:9], refs[9:]
    stream_ref, response_ref, ahead_ref, back_ref, twist_ref, side_ref, long_ref, work_ref, cot_ref, late_ref, sems = refs
    query_copy = pltpu.make_async_copy(held[0].at[0], stream_ref.at[0], sems.at[0])
    tables = [pltpu.make_async_copy(held[i], refs[i], sems.at[i]) for i in range(1, 5)]
    rest = [pltpu.make_async_copy(held[i], refs[i], sems.at[i]) for i in range(5, 7)]
    rest += [pltpu.make_async_copy(held[0].at[i], stream_ref.at[i], sems.at[6 + i]) for i in range(1, 3)]
    query_copy.start()
    blocks, channels, _ = cot_ref.shape
    half = channels // 2
    vocab = mine_ref.shape[0]

    for block in range(blocks):
        upper, lower = unpack_pair(words_ref[block, :half, :], words_ref[block, half : half + 1, :])
        cot_ref[block, :half, :] = upper
        cot_ref[block, half:, :] = lower
    query_copy.wait()
    for copy in tables:
        copy.start()

    def streams(rows):
        late = [cot_ref[block, rows, :] * stream_ref[0, block, rows, :] for block in range(blocks)]
        store_spectrum(work_ref, rows, padded_real_dft(late))

    for_tiles(channels, 4, streams)
    for copy in tables:
        copy.wait()
    for copy in rest:
        copy.start()
    filtered(work_ref, response_ref, ahead_ref, back_ref, twist_ref, -1.0)
    for copy in rest:
        copy.wait()

    def results(rows):
        lane = lax.broadcasted_iota(jnp.int32, (SUBLANES, LANES), 1)
        taps = wide_taps(side_ref, rows)
        gain = side_ref[GAIN_SIDE, rows, :]
        correlated = padded_real_back(load_spectrum(work_ref, rows, blocks + 1))
        before = None
        for block in range(blocks):
            query, key, value = (stream_ref[stream, block, rows, :] for stream in range(3))
            cot = cot_ref[block, rows, :]
            mixed_grad = correlated[block] + gain * (cot * query)
            grads = (cot * long_ref[block, rows, :], mixed_grad * value, mixed_grad * key)
            now, next_one, next_two = (sum(taps[3 * s + j] * grads[s] for s in range(3)) for j in range(3))
            next_one = pltpu.roll(next_one, LANES - 1, 1)
            next_two = pltpu.roll(next_two, LANES - 2, 1)
            if before is not None:
                base, one, two = before
                late_ref[block - 1, rows, :] = (
                    base + jnp.where(lane < LANES - 1, one, next_one) + jnp.where(lane < LANES - 2, two, next_two)
                )
            before = (now, next_one, next_two)
        base, one, two = before
        late_ref[blocks - 1, rows, :] = (
            base + jnp.where(lane < LANES - 1, one, 0.0) + jnp.where(lane < LANES - 2, two, 0.0)
        )

    for_tiles(channels, 2, results)

    total = None
    for start in range(0, blocks, 4):
        some = range(start, start + 4)
        hot = jnp.concatenate([one_hot_block(token_ref, token_row(block, place_ref, pieces), vocab) for block in some], axis=1)
        value = jnp.concatenate([late_ref[block] for block in some], axis=1)
        high = value.astype(BF16)
        low = (value - high.astype(F32)).astype(BF16)
        part = lax.dot_general(
            jnp.concatenate([hot, hot], axis=1),
            jnp.concatenate([high, low], axis=1),
            (((1,), (1,)), ((), ())),
            preferred_element_type=F32,
        )
        total = plus(total, part)
    first = place_ref[1] == 0
    mine_ref[...] = jnp.where(first, total[:, :half], total[:, half:])
    theirs_ref[...] = jnp.where(first, total[:, half:], total[:, :half])


def anywhere(count):
    return [pl.BlockSpec(memory_space=pl.ANY)] * count


def in_vmem(count):
    return [pl.BlockSpec(memory_space=pltpu.VMEM)] * count


def gather_tokens(tokens):
    def swap(part, bits):
        return lax.ppermute(part, "ctx", [(i, i ^ bits) for i in range(16)])

    stack = jnp.concatenate([tokens] + [swap(tokens, bits) for bits in (4, 8, 12)], axis=0)
    return [stack] + [swap(stack, bits) for bits in (1, 2, 3)]


def gather_square(value, mixer_out, place, width):
    def swap(part, bits):
        return lax.ppermute(part, "ctx", [(i, i ^ bits) for i in range(16)])

    def square(part, first, second):
        beside, below = swap(part, first), swap(part, second)
        return part, beside, below, swap(beside, second)

    eight, four = swap(value, 8), swap(value, 4)
    parts = (*square(value, 1, 2), *square(four, 2, 1), *square(eight, 1, 2))
    *last, mixer_out = lax.optimization_barrier((*square(swap(eight, 4), 2, 1), mixer_out))
    vocab = 2 * (value.shape[0] - SUBLANES)
    table = fill_table((), parts, (0, 1, 2, 3, 4, 6, 5, 7, 8, 9, 10, 11), place, vocab, width)
    return mixer_out, fill_table((table,), last, (12, 14, 13, 15), place, vocab, width)


def body(token_ids, embedding, conv_taps, residues, decays, filter_seed, skip_gain, cotangent):
    blocks = lax.axis_size("ctx")
    rank = lax.axis_index("ctx")
    side = lax.axis_index("fsdp")
    width = conv_taps.shape[2]
    vocab = embedding.shape[0]
    half = width // 2 // blocks
    channels = 2 * half
    modes = residues.shape[1]
    slots = blocks + 1
    place = jnp.stack([rank, side]).astype(jnp.int32)
    other_core = [(0, 1), (1, 0)]

    def exchange(value):
        return lax.all_to_all(value, "ctx", split_axis=0, concat_axis=0, tiled=True)

    if blocks == 16:
        tokens = gather_tokens(token_ids)
    else:
        tokens = [exchange(jnp.broadcast_to(token_ids, (blocks, LANES)))]
    cot_words = exchange(encode(cotangent[0], blocks))
    own_columns = lax.dynamic_slice_in_dim(embedding, rank * half, half, 1)
    other_columns = lax.ppermute(own_columns, "fsdp", other_core)
    place, other_columns = lax.optimization_barrier((place, other_columns))

    ahead, back, twist = transform_tables(blocks)
    spectra = (slots, channels, 2 * LANES)
    work = pltpu.VMEM(spectra, F32)
    buffer = pltpu.VMEM((blocks, channels, LANES), F32)
    tables = [work, pltpu.VMEM(ahead.shape, BF16), pltpu.VMEM(back.shape, BF16), pltpu.VMEM(twist.shape, F32)]

    def halves(value):
        lead = value.shape[:-1]
        zeros = (0,) * len(lead)
        if half % LANES == 0:
            return [value, value], [
                pl.BlockSpec((*lead, half), lambda i, at: (*zeros, at[0])),
                pl.BlockSpec((*lead, half), lambda i, at: (*zeros, blocks + at[0])),
            ]
        parts = [
            lax.dynamic_slice_in_dim(value, start + rank * half, half, len(lead)) for start in (0, width // 2)
        ]
        return parts, [pl.BlockSpec((*lead, half), lambda i, at: (*zeros, 0))] * 2

    listed = [halves(v) for v in (conv_taps, skip_gain[None], residues.T, decays.T, filter_seed.T)]
    response, sides = pl.pallas_call(
        filter_kernel,
        grid_spec=pltpu.PrefetchScalarGridSpec(
            num_scalar_prefetch=1,
            grid=(1,),
            in_specs=[spec for _, specs in listed for spec in specs] + in_vmem(2),
            out_specs=tuple(anywhere(2)),
            scratch_shapes=[
                work,
                work,
                pltpu.VMEM((2, 6 + 2 * (-(-blocks // RESTART)), modes, half), F32),
                pltpu.VMEM((2, blocks, LANES, half), F32),
                buffer,
                pltpu.VMEM((SIDES, channels, LANES), F32),
                pltpu.SemaphoreType.DMA((slots + 1,)),
            ],
        ),
        out_shape=(jax.ShapeDtypeStruct(spectra, F32), jax.ShapeDtypeStruct((SIDES, channels, LANES), F32)),
        compiler_params=pltpu.CompilerParams(vmem_limit_bytes=VMEM_BYTES),
        cost_estimate=takes(15),
        name="modal_filter",
    )(place, *[part for parts, _ in listed for part in parts], ahead, twist)

    scalars = functools.partial(pltpu.PrefetchScalarGridSpec, num_scalar_prefetch=1, grid=(1,))
    mixer_words, long_out, streams = pl.pallas_call(
        functools.partial(forward_kernel, len(tokens)),
        grid_spec=scalars(
            in_specs=in_vmem(2 + len(tokens)) + anywhere(5),
            out_specs=tuple(anywhere(3)),
            scratch_shapes=[
                pltpu.VMEM((SIDES, channels, LANES), F32),
                *tables,
                pltpu.VMEM((blocks, half + SUBLANES, LANES), jnp.int32),
                buffer,
                pltpu.VMEM((3, blocks, channels, LANES), F32),
                buffer,
                work,
                pltpu.SemaphoreType.DMA((7,)),
                pltpu.SemaphoreType.DMA((blocks,)),
                pltpu.VMEM((blocks, LANES), jnp.int32),
            ],
        ),
        out_shape=(
            jax.ShapeDtypeStruct((blocks, half + SUBLANES, LANES), jnp.int32),
            jax.ShapeDtypeStruct((blocks, channels, LANES), F32),
            jax.ShapeDtypeStruct((3, blocks, channels, LANES), F32),
        ),
        compiler_params=pltpu.CompilerParams(vmem_limit_bytes=VMEM_BYTES),
        cost_estimate=takes(14),
        name="forward",
    )(place, own_columns, other_columns, *tokens, sides, response, ahead, back, twist)

    mixer_words = exchange(mixer_words)

    mine, theirs = pl.pallas_call(
        functools.partial(backward_kernel, len(tokens)),
        grid_spec=scalars(
            in_specs=in_vmem(1 + len(tokens)) + anywhere(7),
            out_specs=tuple(in_vmem(2)),
            scratch_shapes=[
                pltpu.VMEM((3, blocks, channels, LANES), F32),
                *tables,
                pltpu.VMEM((SIDES, channels, LANES), F32),
                buffer,
                work,
                buffer,
                buffer,
                pltpu.SemaphoreType.DMA((9,)),
                pltpu.VMEM((blocks, LANES), jnp.int32),
            ],
        ),
        out_shape=(jax.ShapeDtypeStruct((vocab, half), F32),) * 2,
        compiler_params=pltpu.CompilerParams(vmem_limit_bytes=VMEM_BYTES),
        cost_estimate=takes(15),
        name="backward",
    )(place, cot_words, *tokens, streams, response, ahead, back, twist, sides, long_out)
    theirs = lax.ppermute(theirs, "fsdp", other_core)
    mixer_out = decode(mixer_words, blocks)
    tall = vocab // 2 + SUBLANES
    grad_words = pl.pallas_call(
        pack_table_kernel,
        in_specs=in_vmem(2),
        out_specs=in_vmem(1)[0],
        compiler_params=pltpu.CompilerParams(vmem_limit_bytes=8 * 1024 * 1024),
        out_shape=jax.ShapeDtypeStruct((tall, half), jnp.int32),
        cost_estimate=takes(1),
        name="pack_table",
    )(mine, theirs)
    table = jax.ShapeDtypeStruct((vocab, blocks * half), F32)
    if blocks == 16 and half == LANES:
        mixer_out, embed_grad = gather_square(grad_words, mixer_out, place, blocks * half)
    else:
        grad_words = lax.all_gather(grad_words, "ctx", axis=0, tiled=False)
        group = max(1, LANES // half)
        grad_words = grad_words.reshape(blocks // group, group, tall, half)
        grad_words = jnp.swapaxes(grad_words, 1, 2).reshape(blocks // group, tall, group * half)
        embed_grad = pl.pallas_call(
            unpack_table_kernel,
            grid=(blocks // group,),
            in_specs=[pl.BlockSpec((1, tall, group * half), lambda i: (i, 0, 0))],
            out_specs=pl.BlockSpec((vocab, group * half), lambda i: (0, i)),
            out_shape=table,
            cost_estimate=takes(3),
            name="unpack_table",
        )(grad_words)
    return mixer_out[None], embed_grad


def solution(mesh):
    placed = (P("fsdp", "ctx"), P(None, "fsdp"), P(), P(), P(), P(), P(), P("fsdp", None, "ctx"))
    return jax.shard_map(
        body,
        mesh=mesh,
        in_specs=placed,
        out_specs=(P("fsdp", None, "ctx"), P(None, "fsdp")),
        check_vma=False,
    )
```

```python
import functools
import math

import jax
import jax.numpy as jnp
import ml_dtypes
import numpy as np
from jax import lax
from jax.experimental import pallas as pl
from jax.experimental.pallas import tpu as pltpu
from jax.sharding import PartitionSpec as P

PERIOD = 4096
LANES = 128
SUBLANES = 8
FULL = 32000.0
TINY = 2.0**-110
CODE = 1024.0
VMEM_BYTES = 60 * 1024 * 1024
F32 = jnp.float32
BF16 = jnp.bfloat16


def pack_pair(upper, lower):
    top = jnp.max(jnp.maximum(jnp.abs(upper), jnp.abs(lower)), axis=0, keepdims=True)
    code = jnp.ceil(jnp.log2(jnp.maximum(top, TINY)) * CODE)
    gain = FULL * jnp.exp2(code * (-1.0 / CODE))
    high = jnp.round(upper * gain).astype(jnp.int32)
    low = jnp.round(lower * gain).astype(jnp.int32)
    words = (high << 16) | (low & 0xFFFF)
    return words, jnp.broadcast_to(code.astype(jnp.int32), (SUBLANES, upper.shape[1]))


def unpack_pair(words, code):
    step = jnp.exp2(code.astype(F32) * (1.0 / CODE)) * (1.0 / FULL)
    return (
        (words >> 16).astype(F32) * step,
        ((words << 16) >> 16).astype(F32) * step,
    )


def plus(a, b):
    return b if a is None else a if b is None else a + b


def minus(a, b):
    return a if b is None else -b if a is None else a - b


def turn(re, im, top, bottom):
    top %= bottom
    if 8 * top % bottom == 0:
        eighth = 8 * top // bottom
        if eighth == 0:
            return re, im
        if eighth == 4:
            return -re, -im
        if eighth == 2:
            return im, -re
        if eighth == 6:
            return -im, re
        half = math.sqrt(0.5)
        if eighth == 1:
            return (re + im) * half, (im - re) * half
        if eighth == 5:
            return (re + im) * -half, (re - im) * half
        if eighth == 3:
            return (im - re) * half, (re + im) * -half
        return (re - im) * half, (re + im) * half
    angle = 2.0 * math.pi * top / bottom
    c, s = math.cos(angle), math.sin(angle)
    return re * c + im * s, im * c - re * s


def complex_dft(points):
    n = len(points)
    if n == 1:
        return points
    even, odd = complex_dft(points[::2]), complex_dft(points[1::2])
    out = [None] * n
    for k in range(n // 2):
        re, im = turn(*odd[k], k, n)
        out[k] = (even[k][0] + re, even[k][1] + im)
        out[k + n // 2] = (even[k][0] - re, even[k][1] - im)
    return out


def odd_part(diff, n):
    quarter = n // 4
    return complex_dft([turn(diff[s], -diff[s + quarter], s, n) for s in range(quarter)])


def place_odd(out, odd, n):
    for index, (re, im) in enumerate(odd):
        k = 4 * index + 1
        if k <= n // 2:
            out[k] = (re, im)
        else:
            out[n - k] = (re, -im)


def real_dft(x):
    n = len(x)
    if n == 1:
        return [(x[0], None)]
    if n == 2:
        return [(x[0] + x[1], None), (x[0] - x[1], None)]
    half = n // 2
    out = [None] * (half + 1)
    out[::2] = real_dft([x[s] + x[s + half] for s in range(half)])
    place_odd(out, odd_part([x[s] - x[s + half] for s in range(half)], n), n)
    return out


def padded_real_dft(x):
    n = 2 * len(x)
    out = [None] * (len(x) + 1)
    out[::2] = real_dft(x)
    place_odd(out, odd_part(x, n), n)
    return out


def odd_back(spectrum, n):
    quarter = n // 4
    points = []
    for index in range(quarter):
        k = 4 * index + 1
        re, im = spectrum[k] if k <= n // 2 else spectrum[n - k]
        points.append((im if k <= n // 2 else -im, re))
    waves = [(re, im) for im, re in complex_dft(points)]
    first, second = [], []
    for s, (re, im) in enumerate(waves):
        im, re = turn(im, re, s, n)
        first.append(re)
        second.append(-im)
    return first + second


def real_back(spectrum):
    n = 2 * (len(spectrum) - 1)
    if n == 2:
        a, b = spectrum[0][0], spectrum[1][0]
        return [a + b, a - b]
    even = real_back(spectrum[::2])
    odd = odd_back(spectrum, n)
    return [a + b for a, b in zip(even, odd)] + [a - b for a, b in zip(even, odd)]


def padded_real_back(spectrum):
    n = 2 * (len(spectrum) - 1)
    even = real_back(spectrum[::2])
    return [a + b for a, b in zip(even, odd_back(spectrum, n))]


def stacked(matrix):
    high = matrix.astype(ml_dtypes.bfloat16)
    low = (matrix - high.astype(np.float64)).astype(ml_dtypes.bfloat16)
    return np.concatenate([high, high, low], axis=0)


def transform_tables(blocks):
    total = 2 * blocks * LANES
    inner = np.arange(LANES)[:, None] * np.arange(LANES)[None, :] % LANES
    angle = 2.0 * np.pi / LANES * inner
    c, s = np.cos(angle), np.sin(angle)
    ahead = np.block([[c, -s], [s, c]])
    back = np.block([[c, s], [-s, c]]) * (2.0 / total)
    turns = np.arange(blocks + 1)[:, None] * np.arange(LANES)[None, :] % total
    angle = 2.0 * np.pi / total * turns
    weight = np.ones((blocks + 1, 1))
    weight[0] = weight[-1] = 0.5
    twist = np.stack([np.cos(angle), np.sin(angle), np.cos(angle) * weight, np.sin(angle) * weight], axis=1)
    return (
        jnp.asarray(stacked(ahead)),
        jnp.asarray(stacked(back)),
        jnp.asarray(np.pad(twist, ((0, 0), (0, 4), (0, 0))), F32),
    )


def split_dot(value, table):
    high = value.astype(BF16)
    low = (value - high.astype(F32)).astype(BF16)
    return jnp.dot(jnp.concatenate([high, low, high], axis=1), table, preferred_element_type=F32)


def inner_ahead(value, twist, table):
    re, im = value[:, :LANES], value[:, LANES:]
    c, s = twist[0:1], twist[1:2]
    turned = jnp.concatenate([re * c + im * s, im * c - re * s], axis=1)
    return split_dot(turned, table)


def inner_back(value, twist, table):
    out = split_dot(value, table)
    re, im = out[:, :LANES], out[:, LANES:]
    c, s = twist[2:3], twist[3:4]
    return jnp.concatenate([re * c - im * s, im * c + re * s], axis=1)


def store_spectrum(ref, rows, spectrum):
    for k, (re, im) in enumerate(spectrum):
        ref[k, rows, :LANES] = re
        ref[k, rows, LANES:] = jnp.zeros_like(re) if im is None else im


def load_spectrum(ref, rows, count):
    return [(ref[k, rows, :LANES], ref[k, rows, LANES:]) for k in range(count)]


def later(previous, current, steps, lane):
    moved = pltpu.roll(current, steps, 1)
    if previous is None:
        return jnp.where(lane < steps, 0.0, moved), moved
    return jnp.where(lane < steps, previous, moved), moved


def earlier(following, current, steps, lane):
    moved = pltpu.roll(current, LANES - steps, 1)
    kept = lane < LANES - steps
    if following is None:
        return jnp.where(kept, moved, 0.0), moved
    return jnp.where(kept, moved, following), moved


def shifted_blocks(x_ref, rows, blocks, lane):
    one = two = None
    for block in range(blocks):
        x = x_ref[block, rows, :]
        back_one, one = later(one, x, 1, lane)
        back_two, two = later(two, x, 2, lane)
        yield block, (x, back_one, back_two)


def column(values, index):
    return values[:, index : index + 1]


def mix(taps, stream, terms):
    return sum(taps[3 * stream + j] * terms[j] for j in range(3))


def wide_taps(ref, rows):
    return [ref[i, rows, :] for i in range(9)]


def for_tiles(channels, unroll, step):
    def run(tile, carry):
        step(pl.ds(pl.multiple_of(tile * SUBLANES, SUBLANES), SUBLANES))
        return carry

    lax.fori_loop(0, channels // SUBLANES, run, 0, unroll=unroll)


def unit_turn(turns):
    angle = (turns - jnp.round(turns)) * math.pi
    square = angle * angle
    sin, cos = SINE[-1], COSINE[-1]
    for coefficient in SINE[-2::-1]:
        sin = sin * square + coefficient
    for coefficient in COSINE[-2::-1]:
        cos = cos * square + coefficient
    sin = sin * angle
    twice = sin + sin
    return 1.0 - twice * sin, twice * cos


def fitted(function, terms):
    top = (math.pi / 2) ** 2
    points = top / 2 * (1 + np.cos(np.pi * (np.arange(64) + 0.5) / 64))
    series = np.polynomial.chebyshev.Chebyshev.fit(points, function(np.sqrt(points)), terms - 1, domain=[0, top])
    return [float(c) for c in series.convert(kind=np.polynomial.Polynomial).coef]


SINE = fitted(lambda a: np.sin(a) / a, 5)
COSINE = fitted(np.cos, 6)
RESTART = 16
LOG2_E = math.log2(math.e)


def modal_rows(rates, turns, blocks):
    leap = jnp.exp2(rates * LANES)
    c, s = unit_turn(turns * LANES)
    rows = [leap * c, leap * s, 2.0 * (leap * c), leap * leap]
    for start in range(RESTART, blocks, RESTART):
        fall = jnp.exp2(rates * (LANES * start))
        c, s = unit_turn(turns * (LANES * start))
        rows += [fall * c, fall * s]
    return rows


def filter_tile(row, far, near, blocks, modes):
    total = [None] * blocks
    for mode in range(modes):
        jump_re, jump_im, ahead, behind = (row(i, mode) for i in range(4))
        far_re, far_im, near_re, near_im = far(0, mode), far(1, mode), near(0, mode), near(1, mode)
        re, im = far_re * near_re - far_im * near_im, far_re * near_im + far_im * near_re
        for first in range(0, blocks, RESTART):
            a, b = re, im
            if first:
                start_re, start_im = (row(2 + 2 * (first // RESTART) + i, mode) for i in range(2))
                a, b = start_re * re - start_im * im, start_re * im + start_im * re
            old, new = a, jump_re * a - jump_im * b
            for block in range(first, min(first + RESTART, blocks)):
                total[block] = plus(total[block], old)
                old, new = new, ahead * new - behind * old
    return total


GAIN_SIDE = 9
SIDES = 10
UNROLLED = 32


def over_slots(count, step):
    if count <= UNROLLED:
        for k in range(count):
            step(k)
    else:
        pl.loop(0, count)(step)


def encode_kernel(value_ref, out_ref):
    height = value_ref.shape[2]
    for i in range(value_ref.shape[1]):
        words, code = pack_pair(value_ref[0, i], value_ref[1, i])
        out_ref[i, :height, :] = words
        out_ref[i, height:, :] = code


def decode_kernel(held_ref, out_ref, words_ref, value_ref, in_sems, sems):
    blocks, height = value_ref.shape[1:3]
    copies = []
    fetches = [pltpu.make_async_copy(held_ref.at[i], words_ref.at[i], in_sems.at[i]) for i in range(blocks)]
    for fetch in fetches:
        fetch.start()
    for block in range(blocks):
        fetches[block].wait()
        upper, lower = unpack_pair(words_ref[block, :height, :], words_ref[block, height : height + 1, :])
        value_ref[0, block] = upper
        value_ref[1, block] = lower
        copies.append(pltpu.make_async_copy(value_ref.at[:, block], out_ref.at[:, block], sems.at[block]))
        copies[-1].start()
    for copy in copies:
        copy.wait()


def encode(value, blocks):
    half = value.shape[0] // 2 // blocks
    some = blocks // 2
    return pl.pallas_call(
        encode_kernel,
        grid=(blocks // some,),
        in_specs=[pl.BlockSpec((2, some, half, LANES), lambda i: (0, i, 0, 0))],
        out_specs=pl.BlockSpec((some, half + SUBLANES, LANES), lambda i: (i, 0, 0)),
        out_shape=jax.ShapeDtypeStruct((blocks, half + SUBLANES, LANES), jnp.int32),
        cost_estimate=takes(2),
        name="encode_cotangent",
    )(value.reshape(2, blocks, half, LANES))


def decode(words, blocks):
    half = words.shape[1] - SUBLANES
    out = pl.pallas_call(
        decode_kernel,
        in_specs=anywhere(1),
        out_specs=anywhere(1)[0],
        out_shape=jax.ShapeDtypeStruct((2, blocks, half, LANES), F32),
        scratch_shapes=[
            pltpu.VMEM(words.shape, jnp.int32),
            pltpu.VMEM((2, blocks, half, LANES), F32),
            pltpu.SemaphoreType.DMA((blocks,)),
            pltpu.SemaphoreType.DMA((blocks,)),
        ],
        compiler_params=pltpu.CompilerParams(vmem_limit_bytes=VMEM_BYTES),
        cost_estimate=takes(2),
        name="decode_mixer",
    )(words)
    return out.reshape(2 * blocks * half, LANES)


def takes(microseconds):
    return pl.CostEstimate(flops=int(microseconds * 1e9), bytes_accessed=int(microseconds * 3e6), transcendentals=0)


def pack_table_kernel(mine_ref, other_ref, out_ref):
    total = mine_ref[...] + other_ref[...]
    half = total.shape[0] // 2
    words, code = pack_pair(total[:half], total[half:])
    out_ref[:half, :] = words
    out_ref[half:, :] = code


def unpack_table_kernel(words_ref, out_ref):
    half = out_ref.shape[0] // 2
    upper, lower = unpack_pair(words_ref[0, :half, :], words_ref[0, half : half + 1, :])
    out_ref[:half, :] = upper
    out_ref[half:, :] = lower


def unpack_square_kernel(aways, place_ref, *refs):
    part_refs, (out_ref, table_ref, sems) = refs[: len(aways)], refs[-3:]
    half = out_ref.shape[0] // 2
    copies = []
    for slot, (ref, away) in enumerate(zip(part_refs, aways)):
        upper, lower = unpack_pair(ref[:half, :], ref[half : half + 1, :])
        table_ref[slot, :half, :] = upper
        table_ref[slot, half:, :] = lower
        place = pl.ds(pl.multiple_of((place_ref[0] ^ away) * LANES, LANES), LANES)
        copies.append(pltpu.make_async_copy(table_ref.at[slot], out_ref.at[:, place], sems.at[slot]))
        copies[-1].start()
    for copy in copies:
        copy.wait()


def fill_table(held, parts, aways, place, vocab, width):
    count = len(aways)
    return pl.pallas_call(
        functools.partial(unpack_square_kernel, aways),
        grid_spec=pltpu.PrefetchScalarGridSpec(
            num_scalar_prefetch=1,
            grid=(1,),
            in_specs=in_vmem(len(parts)) + anywhere(len(held)),
            out_specs=anywhere(1)[0],
            scratch_shapes=[pltpu.VMEM((count, vocab, LANES), F32), pltpu.SemaphoreType.DMA((count,))],
        ),
        out_shape=jax.ShapeDtypeStruct((vocab, width), F32),
        input_output_aliases={len(parts) + 1: 0} if held else {},
        compiler_params=pltpu.CompilerParams(vmem_limit_bytes=16 * 1024 * 1024),
        cost_estimate=takes(2.5 if count > 4 else 1.5),
        name="unpack_table",
    )(place, *parts, *held)


def token_row(token_ref, block, place_ref):
    if token_ref.shape[0] == 1:
        return token_ref[0, block : block + 1, :]
    away = place_ref[0] ^ block
    return token_ref[away & 3, pl.ds(away >> 2, 1), :]


def one_hot_block(wanted, vocab):
    entry = lax.broadcasted_iota(jnp.int32, (vocab, LANES), 0)
    return (entry == wanted).astype(F32).astype(BF16)


def filter_kernel(
    aligned, place_ref, tap_in, gain_in, residue_in, decay_in, seed_in, ahead_in, twist_in, response_out, side_out,
    tap_ref, gain_ref, residue_ref, decay_ref, seed_ref, ahead_ref, twist_ref,
    work_ref, response_ref, mode_ref, far_ref, near_ref, taken_ref, time_ref, side_ref, sems, in_sems,
):
    slots, channels, _ = response_ref.shape
    blocks = slots - 1
    half = channels // 2
    modes = residue_ref.shape[1]
    copies = []
    for index in range(2):
        first = pl.multiple_of((index * blocks + place_ref[0]) * half, half)
        for held, ref in (
            (residue_in, residue_ref),
            (decay_in, decay_ref),
            (seed_in, seed_ref),
            (tap_in, tap_ref),
            (gain_in, gain_ref),
        ):
            part = held.at[(*[slice(None)] * (len(held.shape) - 1), pl.ds(first, half))] if aligned else held.at[index]
            copies.append((part, ref.at[index]))
    copies += [(twist_in, twist_ref), (ahead_in, ahead_ref)]
    copies = [pltpu.make_async_copy(*pair, in_sems.at[i]) for i, pair in enumerate(copies)]
    for copy in copies:
        copy.start()
    for copy in copies[:10]:
        copy.wait()
    sides = []
    for index in range(2):
        decays = decay_ref[index]
        rates = decays * -LOG2_E
        turns = seed_ref[index].astype(F32) * (1.0 / PERIOD)
        weights = residue_ref[index] * jnp.sqrt(decays + 1.0 / (blocks * LANES))
        for i, rows in enumerate(modal_rows(rates, turns, blocks)):
            mode_ref[index, i] = rows
        for number in range(LANES // SUBLANES):
            fall = jnp.exp2(rates * (SUBLANES * number))
            c, s = unit_turn(turns * (SUBLANES * number))
            far_ref[index, number, 0] = fall * c
            far_ref[index, number, 1] = fall * s
        time = lax.broadcasted_iota(jnp.int32, (SUBLANES, half), 0).astype(F32)
        for mode in range(modes):
            row = slice(mode, mode + 1)
            fall = weights[row] * jnp.exp2(rates[row] * time)
            c, s = unit_turn(turns[row] * time)
            near_ref[index, 0, mode] = fall * c
            near_ref[index, 1, mode] = fall * s
        listed = jnp.concatenate([tap_ref[index, 0], tap_ref[index, 1], tap_ref[index, 2], gain_ref[index]], axis=0)
        sides.append(jnp.pad(listed, ((0, LANES - listed.shape[0]), (0, 0))).T)
    sides = jnp.concatenate(sides, axis=0)
    for i in range(SIDES):
        side_ref[i] = jnp.broadcast_to(column(sides, i), (channels, LANES))
    side_copy = pltpu.make_async_copy(side_ref, side_out, sems.at[slots])
    side_copy.start()

    for index in range(2):

        def tile(number, carry):
            first = pl.multiple_of(number * SUBLANES, SUBLANES)
            taken = filter_tile(
                lambda i, mode: mode_ref[index, i, mode : mode + 1, :],
                lambda i, mode: far_ref[index, number, i, mode : mode + 1, :],
                lambda i, mode: near_ref[index, i, mode],
                blocks,
                modes,
            )
            for block in range(blocks):
                taken_ref[index, block, pl.ds(first, SUBLANES), :] = taken[block]
            return carry

        lax.fori_loop(0, LANES // SUBLANES, tile, 0, unroll=2)

    for index in range(2):
        for block in range(blocks):
            time_ref[block, index * half : (index + 1) * half, :] = taken_ref[index, block].T

    def transforms(rows):
        store_spectrum(work_ref, rows, padded_real_dft([time_ref[block, rows, :] for block in range(blocks)]))

    for_tiles(channels, 4, transforms)
    for copy in copies[10:]:
        copy.wait()

    def step(k):
        response_ref[k] = inner_ahead(work_ref[k], twist_ref[k], ahead_ref[...])
        pltpu.make_async_copy(response_ref.at[k], response_out.at[k], sems.at[k]).start()

    over_slots(slots, step)

    @pl.loop(0, slots)
    def _(k):
        pltpu.make_async_copy(response_ref.at[k], response_out.at[k], sems.at[k]).wait()

    side_copy.wait()


def filtered(work_ref, response_ref, ahead_ref, back_ref, twist_ref, sign):
    def step(k):
        twist = twist_ref[k]
        spectrum = inner_ahead(work_ref[k], twist, ahead_ref[...])
        a, b = response_ref[k, :, :LANES], response_ref[k, :, LANES:] * sign
        c, d = spectrum[:, :LANES], spectrum[:, LANES:]
        product = jnp.concatenate([a * c - b * d, a * d + b * c], axis=1)
        work_ref[k] = inner_back(product, twist, back_ref[...])

    over_slots(work_ref.shape[0], step)


def forward_kernel(pieces, place_ref, *refs):
    count = pieces + 7
    held, (words_out_ref, long_out_ref, stream_out_ref), refs = refs[:count], refs[count : count + 3], refs[count + 3 :]
    token_ref, own_ref, other_ref, side_ref, response_ref, ahead_ref, back_ref, twist_ref = refs[:8]
    words_ref, long_ref, stream_ref, x_ref, work_ref, sems, word_sems = refs[8:]
    copies = [
        pltpu.make_async_copy(held[i], ref, sems.at[i])
        for i, ref in enumerate([token_ref.at[j] for j in range(pieces)] + list(refs[1:8]))
    ]
    for copy in copies:
        copy.start()
    stream_copy = pltpu.make_async_copy(stream_ref, stream_out_ref, sems.at[count])
    long_copy = pltpu.make_async_copy(long_ref, long_out_ref, sems.at[count + 1])
    blocks, channels, _ = x_ref.shape
    half = channels // 2
    vocab = own_ref.shape[0]
    for copy in copies[: pieces + 2]:
        copy.wait()
    own, other = own_ref[...].astype(F32).T, other_ref[...].astype(F32).T
    first = place_ref[1] == 0
    tall = jnp.concatenate([jnp.where(first, own, other), jnp.where(first, other, own)], axis=0).astype(BF16)

    for pair in range(blocks // 2):
        hot = jnp.concatenate([one_hot_block(token_row(token_ref, 2 * pair + i, place_ref), vocab) for i in range(2)], axis=1)
        found = jnp.dot(tall, hot, preferred_element_type=F32)
        x_ref[2 * pair] = found[:, :LANES]
        x_ref[2 * pair + 1] = found[:, LANES:]
    copies[pieces + 2].wait()

    def streams(rows):
        lane = lax.broadcasted_iota(jnp.int32, (SUBLANES, LANES), 1)
        taps = wide_taps(side_ref, rows)
        mixed = []
        for block, terms in shifted_blocks(x_ref, rows, blocks, lane):
            query, key, value = (mix(taps, stream, terms) for stream in range(3))
            stream_ref[0, block, rows, :] = query
            stream_ref[1, block, rows, :] = key
            stream_ref[2, block, rows, :] = value
            mixed.append(key * value)
        store_spectrum(work_ref, rows, padded_real_dft(mixed))

    for_tiles(channels, 4, streams)
    stream_copy.start()
    for copy in copies[pieces + 3 :]:
        copy.wait()
    filtered(work_ref, response_ref, ahead_ref, back_ref, twist_ref, 1.0)

    def results(rows):
        conv = padded_real_back(load_spectrum(work_ref, rows, blocks + 1))
        gain = side_ref[GAIN_SIDE, rows, :]
        for block in range(blocks):
            long_out = conv[block] + gain * (stream_ref[1, block, rows, :] * stream_ref[2, block, rows, :])
            long_ref[block, rows, :] = long_out
            x_ref[block, rows, :] = stream_ref[0, block, rows, :] * long_out

    for_tiles(channels, 2, results)
    long_copy.start()

    def words_copy(block):
        return pltpu.make_async_copy(words_ref.at[block], words_out_ref.at[block], word_sems.at[block])

    for block in range(blocks):
        words, code = pack_pair(x_ref[block, :half, :], x_ref[block, half:, :])
        words_ref[block, :half, :] = words
        words_ref[block, half:, :] = code
        words_copy(block).start()
    for block in range(blocks):
        words_copy(block).wait()
    stream_copy.wait()
    long_copy.wait()


def backward_kernel(pieces, place_ref, *refs):
    count = pieces + 8
    held, (mine_out_ref, theirs_out_ref), refs = refs[:count], refs[count : count + 2], refs[count + 2 :]
    token_ref, words_ref, stream_ref, response_ref, ahead_ref, back_ref, twist_ref, side_ref, long_ref = refs[:9]
    mine_ref, theirs_ref, work_ref, cot_ref, late_ref, sems = refs[9:]
    words_copy = pltpu.make_async_copy(held[pieces], words_ref, sems.at[pieces])
    query_copy = pltpu.make_async_copy(held[pieces + 1].at[0], stream_ref.at[0], sems.at[pieces + 1])
    tables = [pltpu.make_async_copy(held[pieces + i], refs[1 + i], sems.at[pieces + i]) for i in range(2, 6)]
    rest = [pltpu.make_async_copy(held[pieces + i], refs[1 + i], sems.at[pieces + i]) for i in range(6, 8)]
    rest += [
        pltpu.make_async_copy(held[pieces + 1].at[i], stream_ref.at[i], sems.at[count + i - 1]) for i in range(1, 3)
    ]
    rest += [pltpu.make_async_copy(held[i], token_ref.at[i], sems.at[i]) for i in range(pieces)]
    words_copy.start()
    query_copy.start()
    blocks, channels, _ = cot_ref.shape
    half = channels // 2
    vocab = mine_ref.shape[0]
    words_copy.wait()

    for block in range(blocks):
        upper, lower = unpack_pair(words_ref[block, :half, :], words_ref[block, half : half + 1, :])
        cot_ref[block, :half, :] = upper
        cot_ref[block, half:, :] = lower
    query_copy.wait()
    for copy in tables:
        copy.start()

    def streams(rows):
        late = [cot_ref[block, rows, :] * stream_ref[0, block, rows, :] for block in range(blocks)]
        store_spectrum(work_ref, rows, padded_real_dft(late))

    for_tiles(channels, 4, streams)
    for copy in tables:
        copy.wait()
    for copy in rest:
        copy.start()
    filtered(work_ref, response_ref, ahead_ref, back_ref, twist_ref, -1.0)
    for copy in rest:
        copy.wait()

    def results(rows):
        lane = lax.broadcasted_iota(jnp.int32, (SUBLANES, LANES), 1)
        taps = wide_taps(side_ref, rows)
        gain = side_ref[GAIN_SIDE, rows, :]
        correlated = padded_real_back(load_spectrum(work_ref, rows, blocks + 1))
        before = None
        for block in range(blocks):
            query, key, value = (stream_ref[stream, block, rows, :] for stream in range(3))
            cot = cot_ref[block, rows, :]
            mixed_grad = correlated[block] + gain * (cot * query)
            grads = (cot * long_ref[block, rows, :], mixed_grad * value, mixed_grad * key)
            now, next_one, next_two = (sum(taps[3 * s + j] * grads[s] for s in range(3)) for j in range(3))
            next_one = pltpu.roll(next_one, LANES - 1, 1)
            next_two = pltpu.roll(next_two, LANES - 2, 1)
            if before is not None:
                base, one, two = before
                late_ref[block - 1, rows, :] = (
                    base + jnp.where(lane < LANES - 1, one, next_one) + jnp.where(lane < LANES - 2, two, next_two)
                )
            before = (now, next_one, next_two)
        base, one, two = before
        late_ref[blocks - 1, rows, :] = (
            base + jnp.where(lane < LANES - 1, one, 0.0) + jnp.where(lane < LANES - 2, two, 0.0)
        )

    for_tiles(channels, 2, results)

    total = None
    for start in range(0, blocks, 4):
        some = range(start, start + 4)
        hot = jnp.concatenate([one_hot_block(token_row(token_ref, block, place_ref), vocab) for block in some], axis=1)
        value = jnp.concatenate([late_ref[block] for block in some], axis=1)
        high = value.astype(BF16)
        low = (value - high.astype(F32)).astype(BF16)
        part = lax.dot_general(
            jnp.concatenate([hot, hot], axis=1),
            jnp.concatenate([high, low], axis=1),
            (((1,), (1,)), ((), ())),
            preferred_element_type=F32,
        )
        total = plus(total, part)
    first = place_ref[1] == 0
    theirs_ref[...] = jnp.where(first, total[:, half:], total[:, :half])
    theirs_copy = pltpu.make_async_copy(theirs_ref, theirs_out_ref, sems.at[count + 2])
    theirs_copy.start()
    mine_ref[...] = jnp.where(first, total[:, :half], total[:, half:])
    mine_copy = pltpu.make_async_copy(mine_ref, mine_out_ref, sems.at[count + 3])
    mine_copy.start()
    theirs_copy.wait()
    mine_copy.wait()


def anywhere(count):
    return [pl.BlockSpec(memory_space=pl.ANY)] * count


def in_vmem(count):
    return [pl.BlockSpec(memory_space=pltpu.VMEM)] * count


def gather_tokens(tokens):
    def swap(part, bits):
        return lax.ppermute(part, "ctx", [(i, i ^ bits) for i in range(16)])

    stack = jnp.concatenate([tokens] + [swap(tokens, bits) for bits in (4, 8, 12)], axis=0)
    return [stack] + [swap(stack, bits) for bits in (1, 2, 3)]


def gather_square(value, mixer_out, place, width):
    def swap(part, bits):
        return lax.ppermute(part, "ctx", [(i, i ^ bits) for i in range(16)])

    def square(part, first, second):
        beside, below = swap(part, first), swap(part, second)
        return part, beside, below, swap(beside, second)

    eight, four = swap(value, 8), swap(value, 4)
    parts = (*square(value, 1, 2), *square(four, 2, 1), *square(eight, 1, 2))
    *last, mixer_out = lax.optimization_barrier((*square(swap(eight, 4), 2, 1), mixer_out))
    vocab = 2 * (value.shape[0] - SUBLANES)
    table = fill_table((), parts, (0, 1, 2, 3, 4, 6, 5, 7, 8, 9, 10, 11), place, vocab, width)
    return mixer_out, fill_table((table,), last, (12, 14, 13, 15), place, vocab, width)


def body(token_ids, embedding, conv_taps, residues, decays, filter_seed, skip_gain, cotangent):
    blocks = lax.axis_size("ctx")
    rank = lax.axis_index("ctx")
    side = lax.axis_index("fsdp")
    width = conv_taps.shape[2]
    vocab = embedding.shape[0]
    half = width // 2 // blocks
    channels = 2 * half
    modes = residues.shape[1]
    slots = blocks + 1
    place = jnp.stack([rank, side]).astype(jnp.int32)
    other_core = [(0, 1), (1, 0)]

    def exchange(value):
        return lax.all_to_all(value, "ctx", split_axis=0, concat_axis=0, tiled=True)

    if blocks == 16:
        tokens = gather_tokens(token_ids)
    else:
        tokens = [exchange(jnp.broadcast_to(token_ids, (blocks, LANES)))]
    cot_words = exchange(encode(cotangent[0], blocks))
    own_columns = lax.dynamic_slice_in_dim(embedding, rank * half, half, 1)
    other_columns = lax.ppermute(own_columns, "fsdp", other_core)
    place, other_columns = lax.optimization_barrier((place, other_columns))

    ahead, back, twist = transform_tables(blocks)
    spectra = (slots, channels, 2 * LANES)
    work = pltpu.VMEM(spectra, F32)
    buffer = pltpu.VMEM((blocks, channels, LANES), F32)
    tables = [work, pltpu.VMEM(ahead.shape, BF16), pltpu.VMEM(back.shape, BF16), pltpu.VMEM(twist.shape, F32)]

    def halves(value):
        if half % LANES == 0:
            return value
        parts = [lax.dynamic_slice_in_dim(value, start + rank * half, half, value.ndim - 1) for start in (0, width // 2)]
        return jnp.stack(parts)

    response, sides = pl.pallas_call(
        functools.partial(filter_kernel, half % LANES == 0),
        grid_spec=pltpu.PrefetchScalarGridSpec(
            num_scalar_prefetch=1,
            grid=(1,),
            in_specs=anywhere(7),
            out_specs=tuple(anywhere(2)),
            scratch_shapes=[
                pltpu.VMEM((2, 3, 3, half), F32),
                pltpu.VMEM((2, 1, half), F32),
                pltpu.VMEM((2, modes, half), F32),
                pltpu.VMEM((2, modes, half), F32),
                pltpu.VMEM((2, modes, half), jnp.int32),
                pltpu.VMEM(ahead.shape, BF16),
                pltpu.VMEM(twist.shape, F32),
                work,
                work,
                pltpu.VMEM((2, 2 + 2 * (-(-blocks // RESTART)), modes, half), F32),
                pltpu.VMEM((2, LANES // SUBLANES, 2, modes, half), F32),
                pltpu.VMEM((2, 2, modes, SUBLANES, half), F32),
                pltpu.VMEM((2, blocks, LANES, half), F32),
                buffer,
                pltpu.VMEM((SIDES, channels, LANES), F32),
                pltpu.SemaphoreType.DMA((slots + 1,)),
                pltpu.SemaphoreType.DMA((12,)),
            ],
        ),
        out_shape=(jax.ShapeDtypeStruct(spectra, F32), jax.ShapeDtypeStruct((SIDES, channels, LANES), F32)),
        compiler_params=pltpu.CompilerParams(vmem_limit_bytes=VMEM_BYTES),
        cost_estimate=takes(15),
        name="modal_filter",
    )(place, *[halves(v) for v in (conv_taps, skip_gain[None], residues.T, decays.T, filter_seed.T)], ahead, twist)

    token_scratch = pltpu.VMEM((len(tokens), *tokens[0].shape), jnp.int32)
    scalars = functools.partial(pltpu.PrefetchScalarGridSpec, num_scalar_prefetch=1, grid=(1,))
    mixer_words, long_out, streams = pl.pallas_call(
        functools.partial(forward_kernel, len(tokens)),
        grid_spec=scalars(
            in_specs=anywhere(len(tokens) + 7),
            out_specs=tuple(anywhere(3)),
            scratch_shapes=[
                token_scratch,
                pltpu.VMEM((vocab, half), BF16),
                pltpu.VMEM((vocab, half), BF16),
                pltpu.VMEM((SIDES, channels, LANES), F32),
                *tables,
                pltpu.VMEM((blocks, half + SUBLANES, LANES), jnp.int32),
                buffer,
                pltpu.VMEM((3, blocks, channels, LANES), F32),
                buffer,
                work,
                pltpu.SemaphoreType.DMA((len(tokens) + 9,)),
                pltpu.SemaphoreType.DMA((blocks,)),
            ],
        ),
        out_shape=(
            jax.ShapeDtypeStruct((blocks, half + SUBLANES, LANES), jnp.int32),
            jax.ShapeDtypeStruct((blocks, channels, LANES), F32),
            jax.ShapeDtypeStruct((3, blocks, channels, LANES), F32),
        ),
        compiler_params=pltpu.CompilerParams(vmem_limit_bytes=VMEM_BYTES),
        cost_estimate=takes(14),
        name="forward",
    )(place, *tokens, own_columns, other_columns, sides, response, ahead, back, twist)

    mixer_words = exchange(mixer_words)

    mine, theirs = pl.pallas_call(
        functools.partial(backward_kernel, len(tokens)),
        grid_spec=scalars(
            in_specs=anywhere(len(tokens) + 8),
            out_specs=tuple(anywhere(2)),
            scratch_shapes=[
                token_scratch,
                pltpu.VMEM((blocks, half + SUBLANES, LANES), jnp.int32),
                pltpu.VMEM((3, blocks, channels, LANES), F32),
                *tables,
                pltpu.VMEM((SIDES, channels, LANES), F32),
                buffer,
                pltpu.VMEM((vocab, half), F32),
                pltpu.VMEM((vocab, half), F32),
                work,
                buffer,
                buffer,
                pltpu.SemaphoreType.DMA((len(tokens) + 12,)),
            ],
        ),
        out_shape=(jax.ShapeDtypeStruct((vocab, half), F32),) * 2,
        compiler_params=pltpu.CompilerParams(vmem_limit_bytes=VMEM_BYTES),
        cost_estimate=takes(15),
        name="backward",
    )(place, *tokens, cot_words, streams, response, ahead, back, twist, sides, long_out)
    theirs = lax.ppermute(theirs, "fsdp", other_core)
    mixer_out = decode(mixer_words, blocks)
    tall = vocab // 2 + SUBLANES
    grad_words = pl.pallas_call(
        pack_table_kernel,
        in_specs=in_vmem(2),
        out_specs=in_vmem(1)[0],
        compiler_params=pltpu.CompilerParams(vmem_limit_bytes=8 * 1024 * 1024),
        out_shape=jax.ShapeDtypeStruct((tall, half), jnp.int32),
        cost_estimate=takes(1),
        name="pack_table",
    )(mine, theirs)
    table = jax.ShapeDtypeStruct((vocab, blocks * half), F32)
    if blocks == 16 and half == LANES:
        mixer_out, embed_grad = gather_square(grad_words, mixer_out, place, blocks * half)
    else:
        grad_words = lax.all_gather(grad_words, "ctx", axis=0, tiled=False)
        group = max(1, LANES // half)
        grad_words = grad_words.reshape(blocks // group, group, tall, half)
        grad_words = jnp.swapaxes(grad_words, 1, 2).reshape(blocks // group, tall, group * half)
        embed_grad = pl.pallas_call(
            unpack_table_kernel,
            grid=(blocks // group,),
            in_specs=[pl.BlockSpec((1, tall, group * half), lambda i: (i, 0, 0))],
            out_specs=pl.BlockSpec((vocab, group * half), lambda i: (0, i)),
            out_shape=table,
            cost_estimate=takes(3),
            name="unpack_table",
        )(grad_words)
    return mixer_out[None], embed_grad


def solution(mesh):
    placed = (P("fsdp", "ctx"), P(None, "fsdp"), P(), P(), P(), P(), P(), P("fsdp", None, "ctx"))
    return jax.shard_map(
        body,
        mesh=mesh,
        in_specs=placed,
        out_specs=(P("fsdp", None, "ctx"), P(None, "fsdp")),
        check_vma=False,
    )
```

```python
import functools
import math

import jax
import jax.numpy as jnp
import ml_dtypes
import numpy as np
from jax import lax
from jax.experimental import pallas as pl
from jax.experimental.pallas import tpu as pltpu
from jax.sharding import PartitionSpec as P

PERIOD = 4096
LANES = 128
SUBLANES = 8
FULL = 32000.0
TINY = 2.0**-110
CODE = 1024.0
VMEM_BYTES = 60 * 1024 * 1024
F32 = jnp.float32
BF16 = jnp.bfloat16


def pack_pair(upper, lower):
    top = jnp.max(jnp.maximum(jnp.abs(upper), jnp.abs(lower)), axis=0, keepdims=True)
    code = jnp.ceil(jnp.log2(jnp.maximum(top, TINY)) * CODE)
    gain = FULL * jnp.exp2(code * (-1.0 / CODE))
    high = jnp.round(upper * gain).astype(jnp.int32)
    low = jnp.round(lower * gain).astype(jnp.int32)
    words = (high << 16) | (low & 0xFFFF)
    return words, jnp.broadcast_to(code.astype(jnp.int32), (SUBLANES, upper.shape[1]))


def unpack_pair(words, code):
    step = jnp.exp2(code.astype(F32) * (1.0 / CODE)) * (1.0 / FULL)
    return (
        (words >> 16).astype(F32) * step,
        ((words << 16) >> 16).astype(F32) * step,
    )


def plus(a, b):
    return b if a is None else a if b is None else a + b


def minus(a, b):
    return a if b is None else -b if a is None else a - b


def turn(re, im, top, bottom):
    top %= bottom
    if 8 * top % bottom == 0:
        eighth = 8 * top // bottom
        if eighth == 0:
            return re, im
        if eighth == 4:
            return -re, -im
        if eighth == 2:
            return im, -re
        if eighth == 6:
            return -im, re
        half = math.sqrt(0.5)
        if eighth == 1:
            return (re + im) * half, (im - re) * half
        if eighth == 5:
            return (re + im) * -half, (re - im) * half
        if eighth == 3:
            return (im - re) * half, (re + im) * -half
        return (re - im) * half, (re + im) * half
    angle = 2.0 * math.pi * top / bottom
    c, s = math.cos(angle), math.sin(angle)
    return re * c + im * s, im * c - re * s


def complex_dft(points):
    n = len(points)
    if n == 1:
        return points
    even, odd = complex_dft(points[::2]), complex_dft(points[1::2])
    out = [None] * n
    for k in range(n // 2):
        re, im = turn(*odd[k], k, n)
        out[k] = (even[k][0] + re, even[k][1] + im)
        out[k + n // 2] = (even[k][0] - re, even[k][1] - im)
    return out


def odd_part(diff, n):
    quarter = n // 4
    return complex_dft([turn(diff[s], -diff[s + quarter], s, n) for s in range(quarter)])


def place_odd(out, odd, n):
    for index, (re, im) in enumerate(odd):
        k = 4 * index + 1
        if k <= n // 2:
            out[k] = (re, im)
        else:
            out[n - k] = (re, -im)


def real_dft(x):
    n = len(x)
    if n == 1:
        return [(x[0], None)]
    if n == 2:
        return [(x[0] + x[1], None), (x[0] - x[1], None)]
    half = n // 2
    out = [None] * (half + 1)
    out[::2] = real_dft([x[s] + x[s + half] for s in range(half)])
    place_odd(out, odd_part([x[s] - x[s + half] for s in range(half)], n), n)
    return out


def padded_real_dft(x):
    n = 2 * len(x)
    out = [None] * (len(x) + 1)
    out[::2] = real_dft(x)
    place_odd(out, odd_part(x, n), n)
    return out


def odd_back(spectrum, n):
    quarter = n // 4
    points = []
    for index in range(quarter):
        k = 4 * index + 1
        re, im = spectrum[k] if k <= n // 2 else spectrum[n - k]
        points.append((im if k <= n // 2 else -im, re))
    waves = [(re, im) for im, re in complex_dft(points)]
    first, second = [], []
    for s, (re, im) in enumerate(waves):
        im, re = turn(im, re, s, n)
        first.append(re)
        second.append(-im)
    return first + second


def real_back(spectrum):
    n = 2 * (len(spectrum) - 1)
    if n == 2:
        a, b = spectrum[0][0], spectrum[1][0]
        return [a + b, a - b]
    even = real_back(spectrum[::2])
    odd = odd_back(spectrum, n)
    return [a + b for a, b in zip(even, odd)] + [a - b for a, b in zip(even, odd)]


def padded_real_back(spectrum):
    n = 2 * (len(spectrum) - 1)
    even = real_back(spectrum[::2])
    return [a + b for a, b in zip(even, odd_back(spectrum, n))]


def stacked(matrix):
    high = matrix.astype(ml_dtypes.bfloat16)
    low = (matrix - high.astype(np.float64)).astype(ml_dtypes.bfloat16)
    return np.concatenate([high, high, low], axis=0)


def transform_tables(blocks):
    total = 2 * blocks * LANES
    inner = np.arange(LANES)[:, None] * np.arange(LANES)[None, :] % LANES
    angle = 2.0 * np.pi / LANES * inner
    c, s = np.cos(angle), np.sin(angle)
    ahead = np.block([[c, -s], [s, c]])
    back = np.block([[c, s], [-s, c]]) * (2.0 / total)
    turns = np.arange(blocks + 1)[:, None] * np.arange(LANES)[None, :] % total
    angle = 2.0 * np.pi / total * turns
    weight = np.ones((blocks + 1, 1))
    weight[0] = weight[-1] = 0.5
    twist = np.stack([np.cos(angle), np.sin(angle), np.cos(angle) * weight, np.sin(angle) * weight], axis=1)
    return (
        jnp.asarray(stacked(ahead)),
        jnp.asarray(stacked(back)),
        jnp.asarray(np.pad(twist, ((0, 0), (0, 4), (0, 0))), F32),
    )


def split_dot(value, table):
    high = value.astype(BF16)
    low = (value - high.astype(F32)).astype(BF16)
    return jnp.dot(jnp.concatenate([high, low, high], axis=1), table, preferred_element_type=F32)


def inner_ahead(value, twist, table):
    re, im = value[:, :LANES], value[:, LANES:]
    c, s = twist[0:1], twist[1:2]
    turned = jnp.concatenate([re * c + im * s, im * c - re * s], axis=1)
    return split_dot(turned, table)


def inner_back(value, twist, table):
    out = split_dot(value, table)
    re, im = out[:, :LANES], out[:, LANES:]
    c, s = twist[2:3], twist[3:4]
    return jnp.concatenate([re * c - im * s, im * c + re * s], axis=1)


def store_spectrum(ref, rows, spectrum):
    for k, (re, im) in enumerate(spectrum):
        ref[k, rows, :LANES] = re
        ref[k, rows, LANES:] = jnp.zeros_like(re) if im is None else im


def load_spectrum(ref, rows, count):
    return [(ref[k, rows, :LANES], ref[k, rows, LANES:]) for k in range(count)]


def later(previous, current, steps, lane):
    moved = pltpu.roll(current, steps, 1)
    if previous is None:
        return jnp.where(lane < steps, 0.0, moved), moved
    return jnp.where(lane < steps, previous, moved), moved


def earlier(following, current, steps, lane):
    moved = pltpu.roll(current, LANES - steps, 1)
    kept = lane < LANES - steps
    if following is None:
        return jnp.where(kept, moved, 0.0), moved
    return jnp.where(kept, moved, following), moved


def shifted_blocks(x_ref, rows, blocks, lane):
    one = two = None
    for block in range(blocks):
        x = x_ref[block, rows, :]
        back_one, one = later(one, x, 1, lane)
        back_two, two = later(two, x, 2, lane)
        yield block, (x, back_one, back_two)


def column(values, index):
    return values[:, index : index + 1]


def mix(taps, stream, terms):
    return sum(taps[3 * stream + j] * terms[j] for j in range(3))


def wide_taps(ref, rows):
    return [ref[i, rows, :] for i in range(9)]


def for_tiles(channels, unroll, step):
    def run(tile, carry):
        step(pl.ds(pl.multiple_of(tile * SUBLANES, SUBLANES), SUBLANES))
        return carry

    lax.fori_loop(0, channels // SUBLANES, run, 0, unroll=unroll)


def unit_turn(turns):
    angle = (turns - jnp.round(turns)) * math.pi
    square = angle * angle
    sin, cos = SINE[-1], COSINE[-1]
    for coefficient in SINE[-2::-1]:
        sin = sin * square + coefficient
    for coefficient in COSINE[-2::-1]:
        cos = cos * square + coefficient
    sin = sin * angle
    twice = sin + sin
    return 1.0 - twice * sin, twice * cos


def fitted(function, terms):
    top = (math.pi / 2) ** 2
    points = top / 2 * (1 + np.cos(np.pi * (np.arange(64) + 0.5) / 64))
    series = np.polynomial.chebyshev.Chebyshev.fit(points, function(np.sqrt(points)), terms - 1, domain=[0, top])
    return [float(c) for c in series.convert(kind=np.polynomial.Polynomial).coef]


SINE = fitted(lambda a: np.sin(a) / a, 5)
COSINE = fitted(np.cos, 6)
RESTART = 16
LOG2_E = math.log2(math.e)


def modal_rows(rates, turns, blocks):
    leap = jnp.exp2(rates * LANES)
    c, s = unit_turn(turns * LANES)
    rows = [leap * c, leap * s, 2.0 * (leap * c), leap * leap]
    for start in range(RESTART, blocks, RESTART):
        fall = jnp.exp2(rates * (LANES * start))
        c, s = unit_turn(turns * (LANES * start))
        rows += [fall * c, fall * s]
    return rows


def filter_tile(row, far, near, blocks, modes):
    total = [None] * blocks
    for mode in range(modes):
        jump_re, jump_im, ahead, behind = (row(i, mode) for i in range(4))
        far_re, far_im, near_re, near_im = far(0, mode), far(1, mode), near(0, mode), near(1, mode)
        re, im = far_re * near_re - far_im * near_im, far_re * near_im + far_im * near_re
        for first in range(0, blocks, RESTART):
            a, b = re, im
            if first:
                start_re, start_im = (row(2 + 2 * (first // RESTART) + i, mode) for i in range(2))
                a, b = start_re * re - start_im * im, start_re * im + start_im * re
            old, new = a, jump_re * a - jump_im * b
            for block in range(first, min(first + RESTART, blocks)):
                total[block] = plus(total[block], old)
                old, new = new, ahead * new - behind * old
    return total


GAIN_SIDE = 9
SIDES = 10
UNROLLED = 32


def over_slots(count, step):
    if count <= UNROLLED:
        for k in range(count):
            step(k)
    else:
        pl.loop(0, count)(step)


def encode_kernel(held_ref, words_out_ref, value_ref, words_ref, in_sems, sems):
    blocks, height = value_ref.shape[1:3]
    fetches = [pltpu.make_async_copy(held_ref.at[:, i], value_ref.at[:, i], in_sems.at[i]) for i in range(blocks)]
    for fetch in fetches:
        fetch.start()
    copies = []
    for block in range(blocks):
        fetches[block].wait()
        words, code = pack_pair(value_ref[0, block], value_ref[1, block])
        words_ref[block, :height, :] = words
        words_ref[block, height:, :] = code
        copies.append(pltpu.make_async_copy(words_ref.at[block], words_out_ref.at[block], sems.at[block]))
        copies[-1].start()
    for copy in copies:
        copy.wait()


def decode_kernel(held_ref, out_ref, words_ref, value_ref, in_sems, sems):
    blocks, height = value_ref.shape[1:3]
    copies = []
    fetches = [pltpu.make_async_copy(held_ref.at[i], words_ref.at[i], in_sems.at[i]) for i in range(blocks)]
    for fetch in fetches:
        fetch.start()
    for block in range(blocks):
        fetches[block].wait()
        upper, lower = unpack_pair(words_ref[block, :height, :], words_ref[block, height : height + 1, :])
        value_ref[0, block] = upper
        value_ref[1, block] = lower
        copies.append(pltpu.make_async_copy(value_ref.at[:, block], out_ref.at[:, block], sems.at[block]))
        copies[-1].start()
    for copy in copies:
        copy.wait()


def encode(value, blocks):
    half = value.shape[0] // 2 // blocks
    words = (blocks, half + SUBLANES, LANES)
    return pl.pallas_call(
        encode_kernel,
        in_specs=anywhere(1),
        out_specs=anywhere(1)[0],
        out_shape=jax.ShapeDtypeStruct(words, jnp.int32),
        scratch_shapes=[
            pltpu.VMEM((2, blocks, half, LANES), F32),
            pltpu.VMEM(words, jnp.int32),
            pltpu.SemaphoreType.DMA((blocks,)),
            pltpu.SemaphoreType.DMA((blocks,)),
        ],
        compiler_params=pltpu.CompilerParams(vmem_limit_bytes=VMEM_BYTES),
        cost_estimate=takes(2),
        name="encode_cotangent",
    )(value.reshape(2, blocks, half, LANES))


def decode(words, blocks):
    half = words.shape[1] - SUBLANES
    out = pl.pallas_call(
        decode_kernel,
        in_specs=anywhere(1),
        out_specs=anywhere(1)[0],
        out_shape=jax.ShapeDtypeStruct((2, blocks, half, LANES), F32),
        scratch_shapes=[
            pltpu.VMEM(words.shape, jnp.int32),
            pltpu.VMEM((2, blocks, half, LANES), F32),
            pltpu.SemaphoreType.DMA((blocks,)),
            pltpu.SemaphoreType.DMA((blocks,)),
        ],
        compiler_params=pltpu.CompilerParams(vmem_limit_bytes=VMEM_BYTES),
        cost_estimate=takes(2),
        name="decode_mixer",
    )(words)
    return out.reshape(2 * blocks * half, LANES)


def takes(microseconds):
    return pl.CostEstimate(flops=int(microseconds * 1e9), bytes_accessed=int(microseconds * 3e6), transcendentals=0)


def pack_table_kernel(mine_ref, other_ref, out_ref):
    total = mine_ref[...] + other_ref[...]
    half = total.shape[0] // 2
    words, code = pack_pair(total[:half], total[half:])
    out_ref[:half, :] = words
    out_ref[half:, :] = code


def unpack_table_kernel(words_ref, out_ref):
    half = out_ref.shape[0] // 2
    upper, lower = unpack_pair(words_ref[0, :half, :], words_ref[0, half : half + 1, :])
    out_ref[:half, :] = upper
    out_ref[half:, :] = lower


def unpack_square_kernel(aways, place_ref, *refs):
    part_refs, (out_ref, table_ref, sems) = refs[: len(aways)], refs[-3:]
    half = out_ref.shape[0] // 2
    copies = []
    for slot, (ref, away) in enumerate(zip(part_refs, aways)):
        upper, lower = unpack_pair(ref[:half, :], ref[half : half + 1, :])
        table_ref[slot, :half, :] = upper
        table_ref[slot, half:, :] = lower
        place = pl.ds(pl.multiple_of(((place_ref[0] >> 1) ^ away) * LANES, LANES), LANES)
        copies.append(pltpu.make_async_copy(table_ref.at[slot], out_ref.at[:, place], sems.at[slot]))
        copies[-1].start()
    for copy in copies:
        copy.wait()


def fill_table(held, parts, aways, place, vocab, width):
    count = len(aways)
    return pl.pallas_call(
        functools.partial(unpack_square_kernel, aways),
        grid_spec=pltpu.PrefetchScalarGridSpec(
            num_scalar_prefetch=1,
            grid=(1,),
            in_specs=in_vmem(len(parts)) + anywhere(len(held)),
            out_specs=anywhere(1)[0],
            scratch_shapes=[pltpu.VMEM((count, vocab, LANES), F32), pltpu.SemaphoreType.DMA((count,))],
        ),
        out_shape=jax.ShapeDtypeStruct((vocab, width), F32),
        input_output_aliases={len(parts) + 1: 0} if held else {},
        compiler_params=pltpu.CompilerParams(vmem_limit_bytes=16 * 1024 * 1024),
        cost_estimate=takes(2.5 if count > 4 else 1.5),
        name="unpack_table",
    )(place, *parts, *held)


def token_row(token_ref, block, place_ref):
    if token_ref.shape[0] == 1:
        return token_ref[0, block : block + 1, :]
    away = (place_ref[0] >> 1) ^ block
    return token_ref[away & 3, pl.ds(away >> 2, 1), :]


def one_hot_block(wanted, vocab):
    entry = lax.broadcasted_iota(jnp.int32, (vocab, LANES), 0)
    return (entry == wanted).astype(F32).astype(BF16)


def filter_kernel(
    aligned, place_ref, tap_in, gain_in, residue_in, decay_in, seed_in, ahead_in, twist_in, response_out, side_out,
    tap_ref, gain_ref, residue_ref, decay_ref, seed_ref, ahead_ref, twist_ref,
    work_ref, response_ref, mode_ref, far_ref, near_ref, taken_ref, time_ref, side_ref, sems, in_sems,
):
    slots, channels, _ = response_ref.shape
    blocks = slots - 1
    half = channels // 2
    modes = residue_ref.shape[1]
    copies = []
    for index in range(2):
        first = pl.multiple_of((index * blocks + (place_ref[0] >> 1)) * half, half)
        for held, ref in (
            (residue_in, residue_ref),
            (decay_in, decay_ref),
            (seed_in, seed_ref),
            (tap_in, tap_ref),
            (gain_in, gain_ref),
        ):
            part = held.at[(*[slice(None)] * (len(held.shape) - 1), pl.ds(first, half))] if aligned else held.at[index]
            copies.append((part, ref.at[index]))
    copies += [(twist_in, twist_ref), (ahead_in, ahead_ref)]
    copies = [pltpu.make_async_copy(*pair, in_sems.at[i]) for i, pair in enumerate(copies)]
    for copy in copies:
        copy.start()
    for copy in copies[:10]:
        copy.wait()
    sides = []
    for index in range(2):
        decays = decay_ref[index]
        rates = decays * -LOG2_E
        turns = seed_ref[index].astype(F32) * (1.0 / PERIOD)
        weights = residue_ref[index] * jnp.sqrt(decays + 1.0 / (blocks * LANES))
        for i, rows in enumerate(modal_rows(rates, turns, blocks)):
            mode_ref[index, i] = rows
        for number in range(LANES // SUBLANES):
            fall = jnp.exp2(rates * (SUBLANES * number))
            c, s = unit_turn(turns * (SUBLANES * number))
            far_ref[index, number, 0] = fall * c
            far_ref[index, number, 1] = fall * s
        time = lax.broadcasted_iota(jnp.int32, (SUBLANES, half), 0).astype(F32)
        for mode in range(modes):
            row = slice(mode, mode + 1)
            fall = weights[row] * jnp.exp2(rates[row] * time)
            c, s = unit_turn(turns[row] * time)
            near_ref[index, 0, mode] = fall * c
            near_ref[index, 1, mode] = fall * s
        listed = jnp.concatenate([tap_ref[index, 0], tap_ref[index, 1], tap_ref[index, 2], gain_ref[index]], axis=0)
        sides.append(jnp.pad(listed, ((0, LANES - listed.shape[0]), (0, 0))).T)
    sides = jnp.concatenate(sides, axis=0)
    for i in range(SIDES):
        side_ref[i] = jnp.broadcast_to(column(sides, i), (channels, LANES))
    side_copy = pltpu.make_async_copy(side_ref, side_out, sems.at[slots])
    side_copy.start()

    for index in range(2):

        def tile(number, carry):
            first = pl.multiple_of(number * SUBLANES, SUBLANES)
            taken = filter_tile(
                lambda i, mode: mode_ref[index, i, mode : mode + 1, :],
                lambda i, mode: far_ref[index, number, i, mode : mode + 1, :],
                lambda i, mode: near_ref[index, i, mode],
                blocks,
                modes,
            )
            for block in range(blocks):
                taken_ref[index, block, pl.ds(first, SUBLANES), :] = taken[block]
            return carry

        lax.fori_loop(0, LANES // SUBLANES, tile, 0, unroll=2)

    for index in range(2):
        for block in range(blocks):
            time_ref[block, index * half : (index + 1) * half, :] = taken_ref[index, block].T

    def transforms(rows):
        store_spectrum(work_ref, rows, padded_real_dft([time_ref[block, rows, :] for block in range(blocks)]))

    for_tiles(channels, 4, transforms)
    for copy in copies[10:]:
        copy.wait()

    def step(k):
        response_ref[k] = inner_ahead(work_ref[k], twist_ref[k], ahead_ref[...])
        pltpu.make_async_copy(response_ref.at[k], response_out.at[k], sems.at[k]).start()

    over_slots(slots, step)

    @pl.loop(0, slots)
    def _(k):
        pltpu.make_async_copy(response_ref.at[k], response_out.at[k], sems.at[k]).wait()

    side_copy.wait()


def filtered(work_ref, response_ref, ahead_ref, back_ref, twist_ref, sign):
    def step(k):
        twist = twist_ref[k]
        spectrum = inner_ahead(work_ref[k], twist, ahead_ref[...])
        a, b = response_ref[k, :, :LANES], response_ref[k, :, LANES:] * sign
        c, d = spectrum[:, :LANES], spectrum[:, LANES:]
        product = jnp.concatenate([a * c - b * d, a * d + b * c], axis=1)
        work_ref[k] = inner_back(product, twist, back_ref[...])

    over_slots(work_ref.shape[0], step)


def forward_kernel(pieces, place_ref, *refs):
    count = pieces + 7
    held, (words_out_ref, long_out_ref, stream_out_ref), refs = refs[:count], refs[count : count + 3], refs[count + 3 :]
    token_ref, own_ref, other_ref, side_ref, response_ref, ahead_ref, back_ref, twist_ref = refs[:8]
    words_ref, long_ref, stream_ref, x_ref, work_ref, sems, word_sems = refs[8:]
    copies = [
        pltpu.make_async_copy(held[i], ref, sems.at[i])
        for i, ref in enumerate([token_ref.at[j] for j in range(pieces)] + list(refs[1:8]))
    ]
    for copy in copies:
        copy.start()
    stream_copy = pltpu.make_async_copy(stream_ref, stream_out_ref, sems.at[count])
    blocks, channels, _ = x_ref.shape
    half = channels // 2
    long_copies = []
    for index in range(2):
        rows = pl.ds(index * half, half)
        long_copies.append(
            pltpu.make_async_copy(long_ref.at[:, rows], long_out_ref.at[:, rows], sems.at[count + 1 + index])
        )
    vocab = own_ref.shape[0]
    for copy in copies[: pieces + 2]:
        copy.wait()
    own, other = own_ref[...].astype(F32).T, other_ref[...].astype(F32).T
    first = (place_ref[0] & 1) == 0
    tall = jnp.concatenate([jnp.where(first, own, other), jnp.where(first, other, own)], axis=0).astype(BF16)

    for pair in range(blocks // 2):
        hot = jnp.concatenate([one_hot_block(token_row(token_ref, 2 * pair + i, place_ref), vocab) for i in range(2)], axis=1)
        found = jnp.dot(tall, hot, preferred_element_type=F32)
        x_ref[2 * pair] = found[:, :LANES]
        x_ref[2 * pair + 1] = found[:, LANES:]
    copies[pieces + 2].wait()

    def streams(rows):
        lane = lax.broadcasted_iota(jnp.int32, (SUBLANES, LANES), 1)
        taps = wide_taps(side_ref, rows)
        mixed = []
        for block, terms in shifted_blocks(x_ref, rows, blocks, lane):
            query, key, value = (mix(taps, stream, terms) for stream in range(3))
            stream_ref[0, block, rows, :] = query
            stream_ref[1, block, rows, :] = key
            stream_ref[2, block, rows, :] = value
            mixed.append(key * value)
        store_spectrum(work_ref, rows, padded_real_dft(mixed))

    for_tiles(channels, 8, streams)
    stream_copy.start()
    for copy in copies[pieces + 3 :]:
        copy.wait()
    filtered(work_ref, response_ref, ahead_ref, back_ref, twist_ref, 1.0)

    def results(rows):
        conv = padded_real_back(load_spectrum(work_ref, rows, blocks + 1))
        gain = side_ref[GAIN_SIDE, rows, :]
        for block in range(blocks):
            long_out = conv[block] + gain * (stream_ref[1, block, rows, :] * stream_ref[2, block, rows, :])
            long_ref[block, rows, :] = long_out
            x_ref[block, rows, :] = stream_ref[0, block, rows, :] * long_out

    for_tiles(half, 2, results)
    long_copies[0].start()
    for_tiles(half, 2, lambda rows: results(pl.ds(half + rows.start, SUBLANES)))
    long_copies[1].start()

    def words_copy(block):
        return pltpu.make_async_copy(words_ref.at[block], words_out_ref.at[block], word_sems.at[block])

    for block in range(blocks):
        words, code = pack_pair(x_ref[block, :half, :], x_ref[block, half:, :])
        words_ref[block, :half, :] = words
        words_ref[block, half:, :] = code
        words_copy(block).start()
    for block in range(blocks):
        words_copy(block).wait()
    stream_copy.wait()
    for copy in long_copies:
        copy.wait()


def backward_kernel(pieces, place_ref, *refs):
    count = pieces + 8
    held, (mine_out_ref, theirs_out_ref), refs = refs[:count], refs[count : count + 2], refs[count + 2 :]
    token_ref, words_ref, stream_ref, response_ref, ahead_ref, back_ref, twist_ref, side_ref, long_ref = refs[:9]
    mine_ref, theirs_ref, work_ref, cot_ref, late_ref, sems = refs[9:]
    words_copy = pltpu.make_async_copy(held[pieces], words_ref, sems.at[pieces])
    query_copy = pltpu.make_async_copy(held[pieces + 1].at[0], stream_ref.at[0], sems.at[pieces + 1])
    tables = [pltpu.make_async_copy(held[pieces + i], refs[1 + i], sems.at[pieces + i]) for i in range(2, 6)]
    rest = [pltpu.make_async_copy(held[pieces + i], refs[1 + i], sems.at[pieces + i]) for i in range(6, 8)]
    rest += [
        pltpu.make_async_copy(held[pieces + 1].at[i], stream_ref.at[i], sems.at[count + i - 1]) for i in range(1, 3)
    ]
    rest += [pltpu.make_async_copy(held[i], token_ref.at[i], sems.at[i]) for i in range(pieces)]
    words_copy.start()
    query_copy.start()
    blocks, channels, _ = cot_ref.shape
    half = channels // 2
    vocab = mine_ref.shape[0]
    words_copy.wait()

    for block in range(blocks):
        upper, lower = unpack_pair(words_ref[block, :half, :], words_ref[block, half : half + 1, :])
        cot_ref[block, :half, :] = upper
        cot_ref[block, half:, :] = lower
    query_copy.wait()
    for copy in tables:
        copy.start()

    def streams(rows):
        late = [cot_ref[block, rows, :] * stream_ref[0, block, rows, :] for block in range(blocks)]
        store_spectrum(work_ref, rows, padded_real_dft(late))

    for_tiles(channels, 4, streams)
    for copy in tables:
        copy.wait()
    for copy in rest:
        copy.start()
    filtered(work_ref, response_ref, ahead_ref, back_ref, twist_ref, -1.0)
    for copy in rest:
        copy.wait()

    def results(rows):
        lane = lax.broadcasted_iota(jnp.int32, (SUBLANES, LANES), 1)
        taps = wide_taps(side_ref, rows)
        gain = side_ref[GAIN_SIDE, rows, :]
        correlated = padded_real_back(load_spectrum(work_ref, rows, blocks + 1))
        before = None
        for block in range(blocks):
            query, key, value = (stream_ref[stream, block, rows, :] for stream in range(3))
            cot = cot_ref[block, rows, :]
            mixed_grad = correlated[block] + gain * (cot * query)
            grads = (cot * long_ref[block, rows, :], mixed_grad * value, mixed_grad * key)
            now, next_one, next_two = (sum(taps[3 * s + j] * grads[s] for s in range(3)) for j in range(3))
            next_one = pltpu.roll(next_one, LANES - 1, 1)
            next_two = pltpu.roll(next_two, LANES - 2, 1)
            if before is not None:
                base, one, two = before
                late_ref[block - 1, rows, :] = (
                    base + jnp.where(lane < LANES - 1, one, next_one) + jnp.where(lane < LANES - 2, two, next_two)
                )
            before = (now, next_one, next_two)
        base, one, two = before
        late_ref[blocks - 1, rows, :] = (
            base + jnp.where(lane < LANES - 1, one, 0.0) + jnp.where(lane < LANES - 2, two, 0.0)
        )

    for_tiles(channels, 2, results)

    total = None
    for start in range(0, blocks, 4):
        some = range(start, start + 4)
        hot = jnp.concatenate([one_hot_block(token_row(token_ref, block, place_ref), vocab) for block in some], axis=1)
        value = jnp.concatenate([late_ref[block] for block in some], axis=1)
        high = value.astype(BF16)
        low = (value - high.astype(F32)).astype(BF16)
        part = lax.dot_general(
            jnp.concatenate([hot, hot], axis=1),
            jnp.concatenate([high, low], axis=1),
            (((1,), (1,)), ((), ())),
            preferred_element_type=F32,
        )
        total = plus(total, part)
    first = (place_ref[0] & 1) == 0
    theirs_ref[...] = jnp.where(first, total[:, half:], total[:, :half])
    theirs_copy = pltpu.make_async_copy(theirs_ref, theirs_out_ref, sems.at[count + 2])
    theirs_copy.start()
    mine_ref[...] = jnp.where(first, total[:, :half], total[:, half:])
    mine_copy = pltpu.make_async_copy(mine_ref, mine_out_ref, sems.at[count + 3])
    mine_copy.start()
    theirs_copy.wait()
    mine_copy.wait()


def anywhere(count):
    return [pl.BlockSpec(memory_space=pl.ANY)] * count


def in_vmem(count):
    return [pl.BlockSpec(memory_space=pltpu.VMEM)] * count


def gather_tokens(tokens):
    def swap(part, bits):
        return lax.ppermute(part, "ctx", [(i, i ^ bits) for i in range(16)])

    stack = jnp.concatenate([tokens] + [swap(tokens, bits) for bits in (4, 8, 12)], axis=0)
    return [stack] + [swap(stack, bits) for bits in (1, 2, 3)]


def gather_square(value, mixer_out, place, width):
    def swap(part, bits):
        return lax.ppermute(part, "ctx", [(i, i ^ bits) for i in range(16)])

    def square(part, first, second):
        beside, below = swap(part, first), swap(part, second)
        return part, beside, below, swap(beside, second)

    eight, four = swap(value, 8), swap(value, 4)
    mine = square(value, 1, 2)
    eight, across = lax.optimization_barrier((eight, mine[3]))
    parts = (*mine[:3], across, *square(four, 2, 1), *square(eight, 1, 2))
    *last, mixer_out = lax.optimization_barrier((*square(swap(eight, 4), 2, 1), mixer_out))
    vocab = 2 * (value.shape[0] - SUBLANES)
    table = fill_table((), parts, (0, 1, 2, 3, 4, 6, 5, 7, 8, 9, 10, 11), place, vocab, width)
    return mixer_out, fill_table((table,), last, (12, 14, 13, 15), place, vocab, width)


def body(token_ids, embedding, conv_taps, residues, decays, filter_seed, skip_gain, cotangent):
    blocks = lax.axis_size("ctx")
    rank = lax.axis_index("ctx")
    side = lax.axis_index("fsdp")
    width = conv_taps.shape[2]
    vocab = embedding.shape[0]
    half = width // 2 // blocks
    channels = 2 * half
    modes = residues.shape[1]
    slots = blocks + 1
    place = jnp.reshape(2 * rank + side, (1,)).astype(jnp.int32)
    other_core = [(0, 1), (1, 0)]

    def exchange(value):
        return lax.all_to_all(value, "ctx", split_axis=0, concat_axis=0, tiled=True)

    if blocks == 16:
        tokens = gather_tokens(token_ids)
    else:
        tokens = [exchange(jnp.broadcast_to(token_ids, (blocks, LANES)))]
    cot_words = exchange(encode(cotangent[0], blocks))
    own_columns = lax.dynamic_slice_in_dim(embedding, rank * half, half, 1)
    other_columns = lax.ppermute(own_columns, "fsdp", other_core)

    ahead, back, twist = transform_tables(blocks)
    spectra = (slots, channels, 2 * LANES)
    work = pltpu.VMEM(spectra, F32)
    buffer = pltpu.VMEM((blocks, channels, LANES), F32)
    tables = [work, pltpu.VMEM(ahead.shape, BF16), pltpu.VMEM(back.shape, BF16), pltpu.VMEM(twist.shape, F32)]

    def halves(value):
        if half % LANES == 0:
            return value
        parts = [lax.dynamic_slice_in_dim(value, start + rank * half, half, value.ndim - 1) for start in (0, width // 2)]
        return jnp.stack(parts)

    response, sides = pl.pallas_call(
        functools.partial(filter_kernel, half % LANES == 0),
        grid_spec=pltpu.PrefetchScalarGridSpec(
            num_scalar_prefetch=1,
            grid=(1,),
            in_specs=anywhere(7),
            out_specs=tuple(anywhere(2)),
            scratch_shapes=[
                pltpu.VMEM((2, 3, 3, half), F32),
                pltpu.VMEM((2, 1, half), F32),
                pltpu.VMEM((2, modes, half), F32),
                pltpu.VMEM((2, modes, half), F32),
                pltpu.VMEM((2, modes, half), jnp.int32),
                pltpu.VMEM(ahead.shape, BF16),
                pltpu.VMEM(twist.shape, F32),
                work,
                work,
                pltpu.VMEM((2, 2 + 2 * (-(-blocks // RESTART)), modes, half), F32),
                pltpu.VMEM((2, LANES // SUBLANES, 2, modes, half), F32),
                pltpu.VMEM((2, 2, modes, SUBLANES, half), F32),
                pltpu.VMEM((2, blocks, LANES, half), F32),
                buffer,
                pltpu.VMEM((SIDES, channels, LANES), F32),
                pltpu.SemaphoreType.DMA((slots + 1,)),
                pltpu.SemaphoreType.DMA((12,)),
            ],
        ),
        out_shape=(jax.ShapeDtypeStruct(spectra, F32), jax.ShapeDtypeStruct((SIDES, channels, LANES), F32)),
        compiler_params=pltpu.CompilerParams(vmem_limit_bytes=VMEM_BYTES),
        cost_estimate=takes(15),
        name="modal_filter",
    )(place, *[halves(v) for v in (conv_taps, skip_gain[None], residues.T, decays.T, filter_seed.T)], ahead, twist)

    token_scratch = pltpu.VMEM((len(tokens), *tokens[0].shape), jnp.int32)
    scalars = functools.partial(pltpu.PrefetchScalarGridSpec, num_scalar_prefetch=1, grid=(1,))
    mixer_words, long_out, streams = pl.pallas_call(
        functools.partial(forward_kernel, len(tokens)),
        grid_spec=scalars(
            in_specs=anywhere(len(tokens) + 7),
            out_specs=tuple(anywhere(3)),
            scratch_shapes=[
                token_scratch,
                pltpu.VMEM((vocab, half), BF16),
                pltpu.VMEM((vocab, half), BF16),
                pltpu.VMEM((SIDES, channels, LANES), F32),
                *tables,
                pltpu.VMEM((blocks, half + SUBLANES, LANES), jnp.int32),
                buffer,
                pltpu.VMEM((3, blocks, channels, LANES), F32),
                buffer,
                work,
                pltpu.SemaphoreType.DMA((len(tokens) + 10,)),
                pltpu.SemaphoreType.DMA((blocks,)),
            ],
        ),
        out_shape=(
            jax.ShapeDtypeStruct((blocks, half + SUBLANES, LANES), jnp.int32),
            jax.ShapeDtypeStruct((blocks, channels, LANES), F32),
            jax.ShapeDtypeStruct((3, blocks, channels, LANES), F32),
        ),
        compiler_params=pltpu.CompilerParams(vmem_limit_bytes=VMEM_BYTES),
        cost_estimate=takes(14),
        name="forward",
    )(place, *tokens, own_columns, other_columns, sides, response, ahead, back, twist)

    mixer_words = exchange(mixer_words)

    mine, theirs = pl.pallas_call(
        functools.partial(backward_kernel, len(tokens)),
        grid_spec=scalars(
            in_specs=anywhere(len(tokens) + 8),
            out_specs=tuple(anywhere(2)),
            scratch_shapes=[
                token_scratch,
                pltpu.VMEM((blocks, half + SUBLANES, LANES), jnp.int32),
                pltpu.VMEM((3, blocks, channels, LANES), F32),
                *tables,
                pltpu.VMEM((SIDES, channels, LANES), F32),
                buffer,
                pltpu.VMEM((vocab, half), F32),
                pltpu.VMEM((vocab, half), F32),
                work,
                buffer,
                buffer,
                pltpu.SemaphoreType.DMA((len(tokens) + 12,)),
            ],
        ),
        out_shape=(jax.ShapeDtypeStruct((vocab, half), F32),) * 2,
        compiler_params=pltpu.CompilerParams(vmem_limit_bytes=VMEM_BYTES),
        cost_estimate=takes(15),
        name="backward",
    )(place, *tokens, cot_words, streams, response, ahead, back, twist, sides, long_out)
    theirs = lax.ppermute(theirs, "fsdp", other_core)
    mixer_out = decode(mixer_words, blocks)
    tall = vocab // 2 + SUBLANES
    grad_words = pl.pallas_call(
        pack_table_kernel,
        in_specs=in_vmem(2),
        out_specs=in_vmem(1)[0],
        compiler_params=pltpu.CompilerParams(vmem_limit_bytes=8 * 1024 * 1024),
        out_shape=jax.ShapeDtypeStruct((tall, half), jnp.int32),
        cost_estimate=takes(1),
        name="pack_table",
    )(mine, theirs)
    table = jax.ShapeDtypeStruct((vocab, blocks * half), F32)
    if blocks == 16 and half == LANES:
        mixer_out, embed_grad = gather_square(grad_words, mixer_out, place, blocks * half)
    else:
        grad_words = lax.all_gather(grad_words, "ctx", axis=0, tiled=False)
        group = max(1, LANES // half)
        grad_words = grad_words.reshape(blocks // group, group, tall, half)
        grad_words = jnp.swapaxes(grad_words, 1, 2).reshape(blocks // group, tall, group * half)
        embed_grad = pl.pallas_call(
            unpack_table_kernel,
            grid=(blocks // group,),
            in_specs=[pl.BlockSpec((1, tall, group * half), lambda i: (i, 0, 0))],
            out_specs=pl.BlockSpec((vocab, group * half), lambda i: (0, i)),
            out_shape=table,
            cost_estimate=takes(3),
            name="unpack_table",
        )(grad_words)
    return mixer_out[None], embed_grad


def solution(mesh):
    placed = (P("fsdp", "ctx"), P(None, "fsdp"), P(), P(), P(), P(), P(), P("fsdp", None, "ctx"))
    return jax.shard_map(
        body,
        mesh=mesh,
        in_specs=placed,
        out_specs=(P("fsdp", None, "ctx"), P(None, "fsdp")),
        check_vma=False,
    )
```

```python
import functools
import math

import jax
import jax.numpy as jnp
import ml_dtypes
import numpy as np
from jax import lax
from jax.experimental import pallas as pl
from jax.experimental.pallas import tpu as pltpu
from jax.sharding import PartitionSpec as P

PERIOD = 4096
LANES = 128
SUBLANES = 8
FULL = 32000.0
TINY = 2.0**-110
CODE = 1024.0
VMEM_BYTES = 60 * 1024 * 1024
F32 = jnp.float32
BF16 = jnp.bfloat16


def pack_pair(upper, lower):
    top = jnp.max(jnp.maximum(jnp.abs(upper), jnp.abs(lower)), axis=0, keepdims=True)
    code = jnp.ceil(jnp.log2(jnp.maximum(top, TINY)) * CODE)
    gain = FULL * jnp.exp2(code * (-1.0 / CODE))
    high = jnp.round(upper * gain).astype(jnp.int32)
    low = jnp.round(lower * gain).astype(jnp.int32)
    words = (high << 16) | (low & 0xFFFF)
    return words, jnp.broadcast_to(code.astype(jnp.int32), (SUBLANES, upper.shape[1]))


def unpack_pair(words, code):
    step = jnp.exp2(code.astype(F32) * (1.0 / CODE)) * (1.0 / FULL)
    return (
        (words >> 16).astype(F32) * step,
        ((words << 16) >> 16).astype(F32) * step,
    )


def plus(a, b):
    return b if a is None else a if b is None else a + b


def minus(a, b):
    return a if b is None else -b if a is None else a - b


def turn(re, im, top, bottom):
    top %= bottom
    if 8 * top % bottom == 0:
        eighth = 8 * top // bottom
        if eighth == 0:
            return re, im
        if eighth == 4:
            return -re, -im
        if eighth == 2:
            return im, -re
        if eighth == 6:
            return -im, re
        half = math.sqrt(0.5)
        if eighth == 1:
            return (re + im) * half, (im - re) * half
        if eighth == 5:
            return (re + im) * -half, (re - im) * half
        if eighth == 3:
            return (im - re) * half, (re + im) * -half
        return (re - im) * half, (re + im) * half
    angle = 2.0 * math.pi * top / bottom
    c, s = math.cos(angle), math.sin(angle)
    return re * c + im * s, im * c - re * s


def complex_dft(points):
    n = len(points)
    if n == 1:
        return points
    even, odd = complex_dft(points[::2]), complex_dft(points[1::2])
    out = [None] * n
    for k in range(n // 2):
        re, im = turn(*odd[k], k, n)
        out[k] = (even[k][0] + re, even[k][1] + im)
        out[k + n // 2] = (even[k][0] - re, even[k][1] - im)
    return out


def odd_part(diff, n):
    quarter = n // 4
    return complex_dft([turn(diff[s], -diff[s + quarter], s, n) for s in range(quarter)])


def place_odd(out, odd, n):
    for index, (re, im) in enumerate(odd):
        k = 4 * index + 1
        if k <= n // 2:
            out[k] = (re, im)
        else:
            out[n - k] = (re, -im)


def real_dft(x):
    n = len(x)
    if n == 1:
        return [(x[0], None)]
    if n == 2:
        return [(x[0] + x[1], None), (x[0] - x[1], None)]
    half = n // 2
    out = [None] * (half + 1)
    out[::2] = real_dft([x[s] + x[s + half] for s in range(half)])
    place_odd(out, odd_part([x[s] - x[s + half] for s in range(half)], n), n)
    return out


def padded_real_dft(x):
    n = 2 * len(x)
    out = [None] * (len(x) + 1)
    out[::2] = real_dft(x)
    place_odd(out, odd_part(x, n), n)
    return out


def odd_back(spectrum, n):
    quarter = n // 4
    points = []
    for index in range(quarter):
        k = 4 * index + 1
        re, im = spectrum[k] if k <= n // 2 else spectrum[n - k]
        points.append((im if k <= n // 2 else -im, re))
    waves = [(re, im) for im, re in complex_dft(points)]
    first, second = [], []
    for s, (re, im) in enumerate(waves):
        im, re = turn(im, re, s, n)
        first.append(re)
        second.append(-im)
    return first + second


def real_back(spectrum):
    n = 2 * (len(spectrum) - 1)
    if n == 2:
        a, b = spectrum[0][0], spectrum[1][0]
        return [a + b, a - b]
    even = real_back(spectrum[::2])
    odd = odd_back(spectrum, n)
    return [a + b for a, b in zip(even, odd)] + [a - b for a, b in zip(even, odd)]


def padded_real_back(spectrum):
    n = 2 * (len(spectrum) - 1)
    even = real_back(spectrum[::2])
    return [a + b for a, b in zip(even, odd_back(spectrum, n))]


def stacked(matrix):
    high = matrix.astype(ml_dtypes.bfloat16)
    low = (matrix - high.astype(np.float64)).astype(ml_dtypes.bfloat16)
    return np.concatenate([high, high, low], axis=0)


def transform_tables(blocks):
    total = 2 * blocks * LANES
    inner = np.arange(LANES)[:, None] * np.arange(LANES)[None, :] % LANES
    angle = 2.0 * np.pi / LANES * inner
    c, s = np.cos(angle), np.sin(angle)
    ahead = np.block([[c, -s], [s, c]])
    back = np.block([[c, s], [-s, c]]) * (2.0 / total)
    turns = np.arange(blocks + 1)[:, None] * np.arange(LANES)[None, :] % total
    angle = 2.0 * np.pi / total * turns
    weight = np.ones((blocks + 1, 1))
    weight[0] = weight[-1] = 0.5
    twist = np.stack([np.cos(angle), np.sin(angle), np.cos(angle) * weight, np.sin(angle) * weight], axis=1)
    return (
        jnp.asarray(stacked(ahead)),
        jnp.asarray(stacked(back)),
        jnp.asarray(np.pad(twist, ((0, 0), (0, 4), (0, 0))), F32),
    )


def split_dot(value, table):
    high = value.astype(BF16)
    low = (value - high.astype(F32)).astype(BF16)
    return jnp.dot(jnp.concatenate([high, low, high], axis=1), table, preferred_element_type=F32)


def inner_ahead(value, twist, table):
    re, im = value[:, :LANES], value[:, LANES:]
    c, s = twist[0:1], twist[1:2]
    turned = jnp.concatenate([re * c + im * s, im * c - re * s], axis=1)
    return split_dot(turned, table)


def inner_back(value, twist, table):
    out = split_dot(value, table)
    re, im = out[:, :LANES], out[:, LANES:]
    c, s = twist[2:3], twist[3:4]
    return jnp.concatenate([re * c - im * s, im * c + re * s], axis=1)


def store_spectrum(ref, rows, spectrum):
    for k, (re, im) in enumerate(spectrum):
        ref[k, rows, :LANES] = re
        ref[k, rows, LANES:] = jnp.zeros_like(re) if im is None else im


def load_spectrum(ref, rows, count):
    return [(ref[k, rows, :LANES], ref[k, rows, LANES:]) for k in range(count)]


def later(previous, current, steps, lane):
    moved = pltpu.roll(current, steps, 1)
    if previous is None:
        return jnp.where(lane < steps, 0.0, moved), moved
    return jnp.where(lane < steps, previous, moved), moved


def earlier(following, current, steps, lane):
    moved = pltpu.roll(current, LANES - steps, 1)
    kept = lane < LANES - steps
    if following is None:
        return jnp.where(kept, moved, 0.0), moved
    return jnp.where(kept, moved, following), moved


def shifted_blocks(x_ref, rows, blocks, lane):
    one = two = None
    for block in range(blocks):
        x = x_ref[block, rows, :]
        back_one, one = later(one, x, 1, lane)
        back_two, two = later(two, x, 2, lane)
        yield block, (x, back_one, back_two)


def column(values, index):
    return values[:, index : index + 1]


def mix(taps, stream, terms):
    return sum(taps[3 * stream + j] * terms[j] for j in range(3))


def wide_taps(ref, rows):
    return [ref[i, rows, :] for i in range(9)]


def for_tiles(channels, unroll, step):
    def run(tile, carry):
        step(pl.ds(pl.multiple_of(tile * SUBLANES, SUBLANES), SUBLANES))
        return carry

    lax.fori_loop(0, channels // SUBLANES, run, 0, unroll=unroll)


def unit_turn(turns):
    angle = (turns - jnp.round(turns)) * math.pi
    square = angle * angle
    sin, cos = SINE[-1], COSINE[-1]
    for coefficient in SINE[-2::-1]:
        sin = sin * square + coefficient
    for coefficient in COSINE[-2::-1]:
        cos = cos * square + coefficient
    sin = sin * angle
    twice = sin + sin
    return 1.0 - twice * sin, twice * cos


def fitted(function, terms):
    top = (math.pi / 2) ** 2
    points = top / 2 * (1 + np.cos(np.pi * (np.arange(64) + 0.5) / 64))
    series = np.polynomial.chebyshev.Chebyshev.fit(points, function(np.sqrt(points)), terms - 1, domain=[0, top])
    return [float(c) for c in series.convert(kind=np.polynomial.Polynomial).coef]


SINE = fitted(lambda a: np.sin(a) / a, 5)
COSINE = fitted(np.cos, 6)
RESTART = 16
LOG2_E = math.log2(math.e)


def modal_rows(rates, turns, blocks):
    leap = jnp.exp2(rates * LANES)
    c, s = unit_turn(turns * LANES)
    rows = [leap * c, leap * s, 2.0 * (leap * c), leap * leap]
    for start in range(RESTART, blocks, RESTART):
        fall = jnp.exp2(rates * (LANES * start))
        c, s = unit_turn(turns * (LANES * start))
        rows += [fall * c, fall * s]
    return rows


def filter_tile(row, far, near, blocks, modes):
    total = [None] * blocks
    for mode in range(modes):
        jump_re, jump_im, ahead, behind = (row(i, mode) for i in range(4))
        far_re, far_im, near_re, near_im = far(0, mode), far(1, mode), near(0, mode), near(1, mode)
        re, im = far_re * near_re - far_im * near_im, far_re * near_im + far_im * near_re
        for first in range(0, blocks, RESTART):
            a, b = re, im
            if first:
                start_re, start_im = (row(2 + 2 * (first // RESTART) + i, mode) for i in range(2))
                a, b = start_re * re - start_im * im, start_re * im + start_im * re
            old, new = a, jump_re * a - jump_im * b
            for block in range(first, min(first + RESTART, blocks)):
                total[block] = plus(total[block], old)
                old, new = new, ahead * new - behind * old
    return total


GAIN_SIDE = 9
SIDES = 10
UNROLLED = 32


def over_slots(count, step):
    if count <= UNROLLED:
        for k in range(count):
            step(k)
    else:
        pl.loop(0, count)(step)


def encode_kernel(held_ref, words_out_ref, value_ref, words_ref, in_sems, sems):
    blocks, height = value_ref.shape[1:3]
    fetches = [pltpu.make_async_copy(held_ref.at[:, i], value_ref.at[:, i], in_sems.at[i]) for i in range(blocks)]
    for fetch in fetches:
        fetch.start()
    copies = []
    for block in range(blocks):
        fetches[block].wait()
        words, code = pack_pair(value_ref[0, block], value_ref[1, block])
        words_ref[block, :height, :] = words
        words_ref[block, height:, :] = code
        copies.append(pltpu.make_async_copy(words_ref.at[block], words_out_ref.at[block], sems.at[block]))
        copies[-1].start()
    for copy in copies:
        copy.wait()


def decode_kernel(held_ref, out_ref, words_ref, value_ref, in_sems, sems):
    blocks, height = value_ref.shape[1:3]
    copies = []
    fetches = [pltpu.make_async_copy(held_ref.at[i], words_ref.at[i], in_sems.at[i]) for i in range(blocks)]
    for fetch in fetches:
        fetch.start()
    for block in range(blocks):
        fetches[block].wait()
        upper, lower = unpack_pair(words_ref[block, :height, :], words_ref[block, height : height + 1, :])
        value_ref[0, block] = upper
        value_ref[1, block] = lower
        copies.append(pltpu.make_async_copy(value_ref.at[:, block], out_ref.at[:, block], sems.at[block]))
        copies[-1].start()
    for copy in copies:
        copy.wait()


def encode(value, blocks):
    half = value.shape[0] // 2 // blocks
    words = (blocks, half + SUBLANES, LANES)
    return pl.pallas_call(
        encode_kernel,
        in_specs=anywhere(1),
        out_specs=anywhere(1)[0],
        out_shape=jax.ShapeDtypeStruct(words, jnp.int32),
        scratch_shapes=[
            pltpu.VMEM((2, blocks, half, LANES), F32),
            pltpu.VMEM(words, jnp.int32),
            pltpu.SemaphoreType.DMA((blocks,)),
            pltpu.SemaphoreType.DMA((blocks,)),
        ],
        compiler_params=pltpu.CompilerParams(vmem_limit_bytes=VMEM_BYTES),
        cost_estimate=takes(2),
        name="encode_cotangent",
    )(value.reshape(2, blocks, half, LANES))


def decode(words, blocks):
    half = words.shape[1] - SUBLANES
    out = pl.pallas_call(
        decode_kernel,
        in_specs=anywhere(1),
        out_specs=anywhere(1)[0],
        out_shape=jax.ShapeDtypeStruct((2, blocks, half, LANES), F32),
        scratch_shapes=[
            pltpu.VMEM(words.shape, jnp.int32),
            pltpu.VMEM((2, blocks, half, LANES), F32),
            pltpu.SemaphoreType.DMA((blocks,)),
            pltpu.SemaphoreType.DMA((blocks,)),
        ],
        compiler_params=pltpu.CompilerParams(vmem_limit_bytes=VMEM_BYTES),
        cost_estimate=takes(2),
        name="decode_mixer",
    )(words)
    return out.reshape(2 * blocks * half, LANES)


def takes(microseconds):
    return pl.CostEstimate(flops=int(microseconds * 1e9), bytes_accessed=int(microseconds * 3e6), transcendentals=0)


def pack_table_kernel(mine_ref, other_ref, out_ref):
    total = mine_ref[...] + other_ref[...]
    half = total.shape[0] // 2
    words, code = pack_pair(total[:half], total[half:])
    out_ref[:half, :] = words
    out_ref[half:, :] = code


def unpack_table_kernel(words_ref, out_ref):
    half = out_ref.shape[0] // 2
    upper, lower = unpack_pair(words_ref[0, :half, :], words_ref[0, half : half + 1, :])
    out_ref[:half, :] = upper
    out_ref[half:, :] = lower


def unpack_square_kernel(aways, place_ref, *refs):
    part_refs, (out_ref, table_ref, sems) = refs[: len(aways)], refs[-3:]
    half = out_ref.shape[0] // 2
    copies = []
    for slot, (ref, away) in enumerate(zip(part_refs, aways)):
        upper, lower = unpack_pair(ref[:half, :], ref[half : half + 1, :])
        table_ref[slot, :half, :] = upper
        table_ref[slot, half:, :] = lower
        place = pl.ds(pl.multiple_of(((place_ref[0] >> 1) ^ away) * LANES, LANES), LANES)
        copies.append(pltpu.make_async_copy(table_ref.at[slot], out_ref.at[:, place], sems.at[slot]))
        copies[-1].start()
    for copy in copies:
        copy.wait()


def fill_table(held, parts, aways, place, vocab, width):
    count = len(aways)
    return pl.pallas_call(
        functools.partial(unpack_square_kernel, aways),
        grid_spec=pltpu.PrefetchScalarGridSpec(
            num_scalar_prefetch=1,
            grid=(1,),
            in_specs=in_vmem(len(parts)) + anywhere(len(held)),
            out_specs=anywhere(1)[0],
            scratch_shapes=[pltpu.VMEM((count, vocab, LANES), F32), pltpu.SemaphoreType.DMA((count,))],
        ),
        out_shape=jax.ShapeDtypeStruct((vocab, width), F32),
        input_output_aliases={len(parts) + 1: 0} if held else {},
        compiler_params=pltpu.CompilerParams(vmem_limit_bytes=16 * 1024 * 1024),
        cost_estimate=takes(2.5 if count > 4 else 1.5),
        name="unpack_table",
    )(place, *parts, *held)


def token_row(token_ref, block, place_ref):
    if token_ref.shape[0] == 1:
        return token_ref[0, block : block + 1, :]
    away = (place_ref[0] >> 1) ^ block
    return token_ref[away & 3, pl.ds(away >> 2, 1), :]


def one_hot_block(wanted, vocab):
    entry = lax.broadcasted_iota(jnp.int32, (vocab, LANES), 0)
    return (entry == wanted).astype(F32).astype(BF16)


def filter_kernel(
    aligned, place_ref, tap_in, gain_in, residue_in, decay_in, seed_in, ahead_in, twist_in, response_out, side_out,
    tap_ref, gain_ref, residue_ref, decay_ref, seed_ref, ahead_ref, twist_ref,
    work_ref, response_ref, mode_ref, far_ref, near_ref, taken_ref, time_ref, side_ref, sems, in_sems,
):
    slots, channels, _ = response_ref.shape
    blocks = slots - 1
    half = channels // 2
    modes = residue_ref.shape[1]
    copies = []
    for index in range(2):
        first = pl.multiple_of((index * blocks + (place_ref[0] >> 1)) * half, half)
        for held, ref in (
            (residue_in, residue_ref),
            (decay_in, decay_ref),
            (seed_in, seed_ref),
            (tap_in, tap_ref),
            (gain_in, gain_ref),
        ):
            part = held.at[(*[slice(None)] * (len(held.shape) - 1), pl.ds(first, half))] if aligned else held.at[index]
            copies.append((part, ref.at[index]))
    copies += [(twist_in, twist_ref), (ahead_in, ahead_ref)]
    copies = [pltpu.make_async_copy(*pair, in_sems.at[i]) for i, pair in enumerate(copies)]
    for copy in copies:
        copy.start()
    for copy in copies[:10]:
        copy.wait()
    sides = []
    for index in range(2):
        decays = decay_ref[index]
        rates = decays * -LOG2_E
        turns = seed_ref[index].astype(F32) * (1.0 / PERIOD)
        weights = residue_ref[index] * jnp.sqrt(decays + 1.0 / (blocks * LANES))
        for i, rows in enumerate(modal_rows(rates, turns, blocks)):
            mode_ref[index, i] = rows
        for number in range(LANES // SUBLANES):
            fall = jnp.exp2(rates * (SUBLANES * number))
            c, s = unit_turn(turns * (SUBLANES * number))
            far_ref[index, number, 0] = fall * c
            far_ref[index, number, 1] = fall * s
        time = lax.broadcasted_iota(jnp.int32, (SUBLANES, half), 0).astype(F32)
        for mode in range(modes):
            row = slice(mode, mode + 1)
            fall = weights[row] * jnp.exp2(rates[row] * time)
            c, s = unit_turn(turns[row] * time)
            near_ref[index, 0, mode] = fall * c
            near_ref[index, 1, mode] = fall * s
        listed = jnp.concatenate([tap_ref[index, 0], tap_ref[index, 1], tap_ref[index, 2], gain_ref[index]], axis=0)
        sides.append(jnp.pad(listed, ((0, LANES - listed.shape[0]), (0, 0))).T)
    sides = jnp.concatenate(sides, axis=0)
    for i in range(SIDES):
        side_ref[i] = jnp.broadcast_to(column(sides, i), (channels, LANES))
    side_copy = pltpu.make_async_copy(side_ref, side_out, sems.at[slots])
    side_copy.start()

    for index in range(2):

        def tile(number, carry):
            first = pl.multiple_of(number * SUBLANES, SUBLANES)
            taken = filter_tile(
                lambda i, mode: mode_ref[index, i, mode : mode + 1, :],
                lambda i, mode: far_ref[index, number, i, mode : mode + 1, :],
                lambda i, mode: near_ref[index, i, mode],
                blocks,
                modes,
            )
            for block in range(blocks):
                taken_ref[index, block, pl.ds(first, SUBLANES), :] = taken[block]
            return carry

        lax.fori_loop(0, LANES // SUBLANES, tile, 0, unroll=2)

    for index in range(2):
        for block in range(blocks):
            time_ref[block, index * half : (index + 1) * half, :] = taken_ref[index, block].T

    def transforms(rows):
        store_spectrum(work_ref, rows, padded_real_dft([time_ref[block, rows, :] for block in range(blocks)]))

    for_tiles(channels, 4, transforms)
    for copy in copies[10:]:
        copy.wait()

    def step(k):
        response_ref[k] = inner_ahead(work_ref[k], twist_ref[k], ahead_ref[...])
        pltpu.make_async_copy(response_ref.at[k], response_out.at[k], sems.at[k]).start()

    over_slots(slots, step)

    @pl.loop(0, slots)
    def _(k):
        pltpu.make_async_copy(response_ref.at[k], response_out.at[k], sems.at[k]).wait()

    side_copy.wait()


def filtered(work_ref, response_ref, ahead_ref, back_ref, twist_ref, sign):
    def step(k):
        twist = twist_ref[k]
        spectrum = inner_ahead(work_ref[k], twist, ahead_ref[...])
        a, b = response_ref[k, :, :LANES], response_ref[k, :, LANES:] * sign
        c, d = spectrum[:, :LANES], spectrum[:, LANES:]
        product = jnp.concatenate([a * c - b * d, a * d + b * c], axis=1)
        work_ref[k] = inner_back(product, twist, back_ref[...])

    over_slots(work_ref.shape[0], step)


def forward_kernel(pieces, place_ref, *refs):
    count = pieces + 7
    held, (words_out_ref, long_out_ref, stream_out_ref), refs = refs[:count], refs[count : count + 3], refs[count + 3 :]
    token_ref, own_ref, other_ref, side_ref, response_ref, ahead_ref, back_ref, twist_ref = refs[:8]
    words_ref, long_ref, stream_ref, x_ref, work_ref, sems, word_sems = refs[8:]
    copies = [
        pltpu.make_async_copy(held[i], ref, sems.at[i])
        for i, ref in enumerate([token_ref.at[j] for j in range(pieces)] + list(refs[1:8]))
    ]
    for copy in copies:
        copy.start()
    stream_copy = pltpu.make_async_copy(stream_ref, stream_out_ref, sems.at[count])
    blocks, channels, _ = x_ref.shape
    half = channels // 2
    long_copies = []
    for index in range(2):
        rows = pl.ds(index * half, half)
        long_copies.append(
            pltpu.make_async_copy(long_ref.at[:, rows], long_out_ref.at[:, rows], sems.at[count + 1 + index])
        )
    vocab = own_ref.shape[0]
    for copy in copies[: pieces + 2]:
        copy.wait()
    own, other = own_ref[...].astype(F32).T, other_ref[...].astype(F32).T
    first = (place_ref[0] & 1) == 0
    tall = jnp.concatenate([jnp.where(first, own, other), jnp.where(first, other, own)], axis=0).astype(BF16)

    for pair in range(blocks // 2):
        hot = jnp.concatenate([one_hot_block(token_row(token_ref, 2 * pair + i, place_ref), vocab) for i in range(2)], axis=1)
        found = jnp.dot(tall, hot, preferred_element_type=F32)
        x_ref[2 * pair] = found[:, :LANES]
        x_ref[2 * pair + 1] = found[:, LANES:]
    copies[pieces + 2].wait()

    def streams(rows):
        lane = lax.broadcasted_iota(jnp.int32, (SUBLANES, LANES), 1)
        taps = wide_taps(side_ref, rows)
        mixed = []
        for block, terms in shifted_blocks(x_ref, rows, blocks, lane):
            query, key, value = (mix(taps, stream, terms) for stream in range(3))
            stream_ref[0, block, rows, :] = query
            stream_ref[1, block, rows, :] = key
            stream_ref[2, block, rows, :] = value
            mixed.append(key * value)
        store_spectrum(work_ref, rows, padded_real_dft(mixed))

    for_tiles(channels, 8, streams)
    stream_copy.start()
    for copy in copies[pieces + 3 :]:
        copy.wait()
    filtered(work_ref, response_ref, ahead_ref, back_ref, twist_ref, 1.0)

    def results(rows):
        conv = padded_real_back(load_spectrum(work_ref, rows, blocks + 1))
        gain = side_ref[GAIN_SIDE, rows, :]
        for block in range(blocks):
            long_out = conv[block] + gain * (stream_ref[1, block, rows, :] * stream_ref[2, block, rows, :])
            long_ref[block, rows, :] = long_out
            x_ref[block, rows, :] = stream_ref[0, block, rows, :] * long_out

    for_tiles(half, 2, results)
    long_copies[0].start()
    for_tiles(half, 2, lambda rows: results(pl.ds(half + rows.start, SUBLANES)))
    long_copies[1].start()

    def words_copy(block):
        return pltpu.make_async_copy(words_ref.at[block], words_out_ref.at[block], word_sems.at[block])

    for block in range(blocks):
        words, code = pack_pair(x_ref[block, :half, :], x_ref[block, half:, :])
        words_ref[block, :half, :] = words
        words_ref[block, half:, :] = code
        words_copy(block).start()
    for block in range(blocks):
        words_copy(block).wait()
    stream_copy.wait()
    for copy in long_copies:
        copy.wait()


def backward_kernel(pieces, place_ref, *refs):
    count = pieces + 8
    held, (mine_out_ref, theirs_out_ref), refs = refs[:count], refs[count : count + 2], refs[count + 2 :]
    token_ref, words_ref, stream_ref, response_ref, ahead_ref, back_ref, twist_ref, side_ref, long_ref = refs[:9]
    mine_ref, theirs_ref, work_ref, cot_ref, late_ref, sems = refs[9:]
    words_copy = pltpu.make_async_copy(held[pieces], words_ref, sems.at[pieces])
    query_copy = pltpu.make_async_copy(held[pieces + 1].at[0], stream_ref.at[0], sems.at[pieces + 1])
    tables = [pltpu.make_async_copy(held[pieces + i], refs[1 + i], sems.at[pieces + i]) for i in range(2, 6)]
    rest = [pltpu.make_async_copy(held[pieces + i], refs[1 + i], sems.at[pieces + i]) for i in range(6, 8)]
    rest += [
        pltpu.make_async_copy(held[pieces + 1].at[i], stream_ref.at[i], sems.at[count + i - 1]) for i in range(1, 3)
    ]
    rest += [pltpu.make_async_copy(held[i], token_ref.at[i], sems.at[i]) for i in range(pieces)]
    words_copy.start()
    query_copy.start()
    blocks, channels, _ = cot_ref.shape
    half = channels // 2
    vocab = mine_ref.shape[0]
    words_copy.wait()
    for copy in tables:
        copy.start()

    for block in range(blocks):
        upper, lower = unpack_pair(words_ref[block, :half, :], words_ref[block, half : half + 1, :])
        cot_ref[block, :half, :] = upper
        cot_ref[block, half:, :] = lower
    query_copy.wait()

    def streams(rows):
        late = [cot_ref[block, rows, :] * stream_ref[0, block, rows, :] for block in range(blocks)]
        store_spectrum(work_ref, rows, padded_real_dft(late))

    for_tiles(channels, 8, streams)
    for copy in tables:
        copy.wait()
    for copy in rest:
        copy.start()
    filtered(work_ref, response_ref, ahead_ref, back_ref, twist_ref, -1.0)
    for copy in rest:
        copy.wait()

    def results(rows):
        lane = lax.broadcasted_iota(jnp.int32, (SUBLANES, LANES), 1)
        taps = wide_taps(side_ref, rows)
        gain = side_ref[GAIN_SIDE, rows, :]
        correlated = padded_real_back(load_spectrum(work_ref, rows, blocks + 1))
        before = None
        for block in range(blocks):
            query, key, value = (stream_ref[stream, block, rows, :] for stream in range(3))
            cot = cot_ref[block, rows, :]
            mixed_grad = correlated[block] + gain * (cot * query)
            grads = (cot * long_ref[block, rows, :], mixed_grad * value, mixed_grad * key)
            now, next_one, next_two = (sum(taps[3 * s + j] * grads[s] for s in range(3)) for j in range(3))
            next_one = pltpu.roll(next_one, LANES - 1, 1)
            next_two = pltpu.roll(next_two, LANES - 2, 1)
            if before is not None:
                base, one, two = before
                late_ref[block - 1, rows, :] = (
                    base + jnp.where(lane < LANES - 1, one, next_one) + jnp.where(lane < LANES - 2, two, next_two)
                )
            before = (now, next_one, next_two)
        base, one, two = before
        late_ref[blocks - 1, rows, :] = (
            base + jnp.where(lane < LANES - 1, one, 0.0) + jnp.where(lane < LANES - 2, two, 0.0)
        )

    for_tiles(channels, 4, results)

    total = None
    for start in range(0, blocks, 4):
        some = range(start, start + 4)
        hot = jnp.concatenate([one_hot_block(token_row(token_ref, block, place_ref), vocab) for block in some], axis=1)
        value = jnp.concatenate([late_ref[block] for block in some], axis=1)
        high = value.astype(BF16)
        low = (value - high.astype(F32)).astype(BF16)
        part = lax.dot_general(
            jnp.concatenate([hot, hot], axis=1),
            jnp.concatenate([high, low], axis=1),
            (((1,), (1,)), ((), ())),
            preferred_element_type=F32,
        )
        total = plus(total, part)
    first = (place_ref[0] & 1) == 0
    theirs_ref[...] = jnp.where(first, total[:, half:], total[:, :half])
    theirs_copy = pltpu.make_async_copy(theirs_ref, theirs_out_ref, sems.at[count + 2])
    theirs_copy.start()
    mine_ref[...] = jnp.where(first, total[:, :half], total[:, half:])
    mine_copy = pltpu.make_async_copy(mine_ref, mine_out_ref, sems.at[count + 3])
    mine_copy.start()
    theirs_copy.wait()
    mine_copy.wait()


def anywhere(count):
    return [pl.BlockSpec(memory_space=pl.ANY)] * count


def in_vmem(count):
    return [pl.BlockSpec(memory_space=pltpu.VMEM)] * count


def gather_tokens(tokens):
    def swap(part, bits):
        return lax.ppermute(part, "ctx", [(i, i ^ bits) for i in range(16)])

    stack = jnp.concatenate([tokens] + [swap(tokens, bits) for bits in (4, 8, 12)], axis=0)
    return [stack] + [swap(stack, bits) for bits in (1, 2, 3)]


def gather_square(value, mixer_out, place, width):
    def swap(part, bits):
        return lax.ppermute(part, "ctx", [(i, i ^ bits) for i in range(16)])

    def square(part, first, second):
        beside, below = swap(part, first), swap(part, second)
        return part, beside, below, swap(beside, second)

    eight, four = swap(value, 8), swap(value, 4)
    mine = square(value, 1, 2)
    eight, across = lax.optimization_barrier((eight, mine[3]))
    parts = (*mine[:3], across, *square(four, 2, 1), *square(eight, 1, 2))
    *last, mixer_out = lax.optimization_barrier((*square(swap(eight, 4), 2, 1), mixer_out))
    vocab = 2 * (value.shape[0] - SUBLANES)
    table = fill_table((), parts, (0, 1, 2, 3, 4, 6, 5, 7, 8, 9, 10, 11), place, vocab, width)
    return mixer_out, fill_table((table,), last, (12, 14, 13, 15), place, vocab, width)


def body(token_ids, embedding, conv_taps, residues, decays, filter_seed, skip_gain, cotangent):
    blocks = lax.axis_size("ctx")
    rank = lax.axis_index("ctx")
    side = lax.axis_index("fsdp")
    width = conv_taps.shape[2]
    vocab = embedding.shape[0]
    half = width // 2 // blocks
    channels = 2 * half
    modes = residues.shape[1]
    slots = blocks + 1
    place = jnp.reshape(2 * rank + side, (1,)).astype(jnp.int32)
    other_core = [(0, 1), (1, 0)]

    def exchange(value):
        return lax.all_to_all(value, "ctx", split_axis=0, concat_axis=0, tiled=True)

    if blocks == 16:
        tokens = gather_tokens(token_ids)
    else:
        tokens = [exchange(jnp.broadcast_to(token_ids, (blocks, LANES)))]
    cot_words = exchange(encode(cotangent[0], blocks))
    own_columns = lax.dynamic_slice_in_dim(embedding, rank * half, half, 1)
    other_columns = lax.ppermute(own_columns, "fsdp", other_core)

    ahead, back, twist = transform_tables(blocks)
    spectra = (slots, channels, 2 * LANES)
    work = pltpu.VMEM(spectra, F32)
    buffer = pltpu.VMEM((blocks, channels, LANES), F32)
    tables = [work, pltpu.VMEM(ahead.shape, BF16), pltpu.VMEM(back.shape, BF16), pltpu.VMEM(twist.shape, F32)]

    def halves(value):
        if half % LANES == 0:
            return value
        parts = [lax.dynamic_slice_in_dim(value, start + rank * half, half, value.ndim - 1) for start in (0, width // 2)]
        return jnp.stack(parts)

    response, sides = pl.pallas_call(
        functools.partial(filter_kernel, half % LANES == 0),
        grid_spec=pltpu.PrefetchScalarGridSpec(
            num_scalar_prefetch=1,
            grid=(1,),
            in_specs=anywhere(7),
            out_specs=tuple(anywhere(2)),
            scratch_shapes=[
                pltpu.VMEM((2, 3, 3, half), F32),
                pltpu.VMEM((2, 1, half), F32),
                pltpu.VMEM((2, modes, half), F32),
                pltpu.VMEM((2, modes, half), F32),
                pltpu.VMEM((2, modes, half), jnp.int32),
                pltpu.VMEM(ahead.shape, BF16),
                pltpu.VMEM(twist.shape, F32),
                work,
                work,
                pltpu.VMEM((2, 2 + 2 * (-(-blocks // RESTART)), modes, half), F32),
                pltpu.VMEM((2, LANES // SUBLANES, 2, modes, half), F32),
                pltpu.VMEM((2, 2, modes, SUBLANES, half), F32),
                pltpu.VMEM((2, blocks, LANES, half), F32),
                buffer,
                pltpu.VMEM((SIDES, channels, LANES), F32),
                pltpu.SemaphoreType.DMA((slots + 1,)),
                pltpu.SemaphoreType.DMA((12,)),
            ],
        ),
        out_shape=(jax.ShapeDtypeStruct(spectra, F32), jax.ShapeDtypeStruct((SIDES, channels, LANES), F32)),
        compiler_params=pltpu.CompilerParams(vmem_limit_bytes=VMEM_BYTES),
        cost_estimate=takes(15),
        name="modal_filter",
    )(place, *[halves(v) for v in (conv_taps, skip_gain[None], residues.T, decays.T, filter_seed.T)], ahead, twist)

    token_scratch = pltpu.VMEM((len(tokens), *tokens[0].shape), jnp.int32)
    scalars = functools.partial(pltpu.PrefetchScalarGridSpec, num_scalar_prefetch=1, grid=(1,))
    mixer_words, long_out, streams = pl.pallas_call(
        functools.partial(forward_kernel, len(tokens)),
        grid_spec=scalars(
            in_specs=anywhere(len(tokens) + 7),
            out_specs=tuple(anywhere(3)),
            scratch_shapes=[
                token_scratch,
                pltpu.VMEM((vocab, half), BF16),
                pltpu.VMEM((vocab, half), BF16),
                pltpu.VMEM((SIDES, channels, LANES), F32),
                *tables,
                pltpu.VMEM((blocks, half + SUBLANES, LANES), jnp.int32),
                buffer,
                pltpu.VMEM((3, blocks, channels, LANES), F32),
                buffer,
                work,
                pltpu.SemaphoreType.DMA((len(tokens) + 10,)),
                pltpu.SemaphoreType.DMA((blocks,)),
            ],
        ),
        out_shape=(
            jax.ShapeDtypeStruct((blocks, half + SUBLANES, LANES), jnp.int32),
            jax.ShapeDtypeStruct((blocks, channels, LANES), F32),
            jax.ShapeDtypeStruct((3, blocks, channels, LANES), F32),
        ),
        compiler_params=pltpu.CompilerParams(vmem_limit_bytes=VMEM_BYTES),
        cost_estimate=takes(14),
        name="forward",
    )(place, *tokens, own_columns, other_columns, sides, response, ahead, back, twist)

    mixer_words = exchange(mixer_words)

    mine, theirs = pl.pallas_call(
        functools.partial(backward_kernel, len(tokens)),
        grid_spec=scalars(
            in_specs=anywhere(len(tokens) + 8),
            out_specs=tuple(anywhere(2)),
            scratch_shapes=[
                token_scratch,
                pltpu.VMEM((blocks, half + SUBLANES, LANES), jnp.int32),
                pltpu.VMEM((3, blocks, channels, LANES), F32),
                *tables,
                pltpu.VMEM((SIDES, channels, LANES), F32),
                buffer,
                pltpu.VMEM((vocab, half), F32),
                pltpu.VMEM((vocab, half), F32),
                work,
                buffer,
                buffer,
                pltpu.SemaphoreType.DMA((len(tokens) + 12,)),
            ],
        ),
        out_shape=(jax.ShapeDtypeStruct((vocab, half), F32),) * 2,
        compiler_params=pltpu.CompilerParams(vmem_limit_bytes=VMEM_BYTES),
        cost_estimate=takes(15),
        name="backward",
    )(place, *tokens, cot_words, streams, response, ahead, back, twist, sides, long_out)
    theirs = lax.ppermute(theirs, "fsdp", other_core)
    mixer_out = decode(mixer_words, blocks)
    tall = vocab // 2 + SUBLANES
    grad_words = pl.pallas_call(
        pack_table_kernel,
        in_specs=in_vmem(2),
        out_specs=in_vmem(1)[0],
        compiler_params=pltpu.CompilerParams(vmem_limit_bytes=8 * 1024 * 1024),
        out_shape=jax.ShapeDtypeStruct((tall, half), jnp.int32),
        cost_estimate=takes(1),
        name="pack_table",
    )(mine, theirs)
    table = jax.ShapeDtypeStruct((vocab, blocks * half), F32)
    if blocks == 16 and half == LANES:
        mixer_out, embed_grad = gather_square(grad_words, mixer_out, place, blocks * half)
    else:
        grad_words = lax.all_gather(grad_words, "ctx", axis=0, tiled=False)
        group = max(1, LANES // half)
        grad_words = grad_words.reshape(blocks // group, group, tall, half)
        grad_words = jnp.swapaxes(grad_words, 1, 2).reshape(blocks // group, tall, group * half)
        embed_grad = pl.pallas_call(
            unpack_table_kernel,
            grid=(blocks // group,),
            in_specs=[pl.BlockSpec((1, tall, group * half), lambda i: (i, 0, 0))],
            out_specs=pl.BlockSpec((vocab, group * half), lambda i: (0, i)),
            out_shape=table,
            cost_estimate=takes(3),
            name="unpack_table",
        )(grad_words)
    return mixer_out[None], embed_grad


def solution(mesh):
    placed = (P("fsdp", "ctx"), P(None, "fsdp"), P(), P(), P(), P(), P(), P("fsdp", None, "ctx"))
    return jax.shard_map(
        body,
        mesh=mesh,
        in_specs=placed,
        out_specs=(P("fsdp", None, "ctx"), P(None, "fsdp")),
        check_vma=False,
    )
```
